256 devices in a mesh: tr: 16 (over x_hi, z), tc: 16 (over y, x_lo, core).
Axes of the slice: x: 4 (x_hi: 2, x_lo: 2; x = x_hi * 2 + x_lo), y: 4, z: 8, core: 2. Of those that a mesh axis runs over, the one named last changes fastest.
Arguments:
- diag_block: bfloat16 [16, 16, 1024, 1024], P('tr', 'tc'), as said below
- coupling: bfloat16 [16, 16, 1024, 1024], P('tr', 'tc'), may hold values from -0.09375 to 0.09375
- precond: float32 [16, 16, 1024, 1024], P('tr', 'tc'), as said below
- rhs: float32 [16, 16, 1024, 128], P('tr', 'tc')
- slot_time: int32 [16, 16], P('tr', 'tc'), may hold values from 0 to 255, as said below
Outputs:
- solution: float32 [16, 16, 1024, 128], P('tr', 'tc')
- residual_norm: float32 [128], replicated
The draws below stay inside these ranges and needn't reach their ends.
Inputs may be any that keep to these rules, and one draw needn't show every extreme that they name: `slot_time`: a permutation of the time blocks in which time blocks t and t + 1 always sit in slots adjacent along tr or along tc. `diag_block`: every block is symmetric and indefinite. `precond`: every block is symmetric positive definite.
All inputs are finite; a program needn't handle non-finite values.
Results may differ from the reference program's by a relative error of at most 0.0035.
Values may be sent and summed in bfloat16 or wider, within the bound.
No kernel may reach another device: no remote copies, remote signals or barrier semaphores. Data moves between devices by JAX's collectives and lax.ppermute only.
A program may use at most 128 MiB of HBM per device.

```python
import math
import jax
import jax.numpy as jnp
from jax import lax

B = 1024
R = 128
ITERS = 3
N_TR = 16
N_TC = 16


def symmetric_part(raw):
    return (raw + jnp.swapaxes(raw, 2, 3)) / math.sqrt(2.0 * B)


def magnitudes(key):
    spread = jax.random.uniform(jax.random.fold_in(key, 7), (N_TR, N_TC, B), jnp.float32, 0.0, math.log(4.0))
    return jnp.exp(spread)


def gram_block(factor):
    product = jnp.dot(factor, factor.T, precision=lax.Precision.HIGHEST) / B
    product = 0.5 * (product + product.T)
    return product + 0.5 * jnp.eye(B, dtype=jnp.float32)


def draw_diag_block(key, part):
    base = jax.random.fold_in(key, 3)
    shape = (N_TR, N_TC, B, B)
    raw = jax.random.normal(base, shape, jnp.float32)
    noise = symmetric_part(raw)
    flips = jax.random.uniform(jax.random.fold_in(key, 9), (N_TR, N_TC, B), jnp.float32)
    signs = jnp.where(flips < 0.3, -1.0, 1.0)
    identity = jnp.eye(B, dtype=jnp.float32)
    return (0.4 * noise + (signs * magnitudes(key))[..., None] * identity).astype(jnp.bfloat16)


def draw_precond(key, part):
    base = jax.random.fold_in(key, 5)
    shape = (N_TR * N_TC, B, B)
    raw = jax.random.normal(base, shape, jnp.float32)
    wishart = lax.map(gram_block, raw).reshape(N_TR, N_TC, B, B)
    scale_rows = jnp.sqrt(magnitudes(key))
    return scale_rows[..., :, None] * wishart * scale_rows[..., None, :]


def draw_rhs(key, part):
    shape = (N_TR, N_TC, B, R)
    base = jax.random.fold_in(key, 13)
    values = jax.random.normal(base, shape, jnp.float32)
    slots = jnp.arange(N_TR * N_TC, dtype=jnp.float32).reshape(N_TR, N_TC)
    rising = 1.0 + 2.0 * slots / max(N_TR * N_TC - 1, 1)
    return values * rising[:, :, None, None]


def draw_slot_time(key, part):
    key = jax.random.fold_in(key, 17)
    flips = jax.random.randint(jax.random.fold_in(key, 1), (3,), 0, 2)
    start = jax.random.randint(jax.random.fold_in(key, 2), (), 0, N_TR * N_TC)
    count = N_TR * N_TC
    width = N_TC - 1
    rows = jnp.arange(N_TR, dtype=jnp.int32)[:, None] * jnp.ones((1, N_TC), jnp.int32)
    cols = jnp.arange(N_TC, dtype=jnp.int32)[None, :] * jnp.ones((N_TR, 1), jnp.int32)
    rows = jnp.where(flips[0] == 1, N_TR - 1 - rows, rows)
    cols = jnp.where(flips[1] == 1, N_TC - 1 - cols, cols)
    inner = N_TC + (rows - 1) * width + jnp.where(rows % 2 == 1, N_TC - 1 - cols, cols - 1)
    left = N_TC + (N_TR - 1) * width + (N_TR - 1 - rows)
    place = jnp.where(rows == 0, cols, jnp.where(cols == 0, left, inner))
    place = jnp.where(flips[2] == 1, count - 1 - place, place)
    return ((place + start) % count).astype(jnp.int32)


def block_levels(stream_key, dims, shards, least, top_value):
    def one(axis_at, shards_of):
        draws = jax.random.uniform(jax.random.fold_in(jax.random.fold_in(stream_key, 6), axis_at), (shards_of,), jnp.float32, least / len(shards), top_value / len(shards))
        return jnp.repeat(jnp.exp(draws), dims[axis_at] // shards_of).reshape((-1,) + (1,) * (len(dims) - axis_at - 1))

    loudness = one(*shards[0])
    for cut in shards[1:]:
        loudness = loudness * one(*cut)
    return loudness


def scatter_about(rng, shape, scale, limit, pieces=(), kind=jnp.bfloat16):
    entries = scale * jax.random.normal(rng, shape, jnp.float32)
    if pieces:
        entries = entries * block_levels(rng, shape, pieces, -0.22, 0.18)
    return jnp.clip(entries, -limit, limit).astype(kind)


def setup_inputs(seed: int = 0) -> dict:
    keys = jax.random.split(jax.random.key(seed), 6)
    diag_block = draw_diag_block(jax.random.fold_in(keys[5], 71), 0)
    coupling = scatter_about(keys[1], (N_TR, N_TC, B, B), (4 * B) ** -0.5, 0.09375, ((0, 16), (1, 16)))
    precond = draw_precond(jax.random.fold_in(keys[5], 71), 0)
    rhs = draw_rhs(jax.random.fold_in(keys[5], 71), 0)
    slot_time = draw_slot_time(jax.random.fold_in(keys[5], 71), 0)
    return dict(diag_block=diag_block, coupling=coupling, precond=precond, rhs=rhs, slot_time=slot_time)


def invert_block(block):
    lower = jnp.linalg.cholesky(block)
    lower_inv = jax.scipy.linalg.solve_triangular(lower, jnp.eye(block.shape[0], dtype=block.dtype), lower=True)
    return jnp.dot(lower_inv.T, lower_inv, precision=lax.Precision.HIGHEST)

def inner_prod(left, right):
    return lax.optimization_barrier(jnp.sum(left * right, axis=(0, 1)))

def reference(diag_block, coupling, precond, rhs, slot_time):
    count = N_TR * N_TC
    order = slot_time.reshape(-1).astype(jnp.int32)

    def to_time(array):
        flat = array.reshape((count,) + array.shape[2:])
        return jnp.zeros_like(flat).at[order].set(flat)
    diag_time = to_time(diag_block)
    coupling_time = to_time(coupling)
    precond_time = to_time(precond)
    rhs_time = to_time(rhs)
    inverses = lax.map(invert_block, precond_time)

    def precon(resid):
        return lax.map(lambda pair: jnp.dot(pair[0], pair[1], precision=lax.Precision.HIGHEST), (inverses, resid))

    def operator(vector):
        rounded = vector.astype(jnp.bfloat16)
        before = jnp.concatenate([jnp.zeros_like(rounded[:1]), rounded[:-1]], axis=0)

        def local_terms(items):
            diag_here, coupling_here, vec_here, vec_before = items
            own_part = jnp.dot(diag_here.astype(jnp.float32), vec_here.astype(jnp.float32), preferred_element_type=jnp.float32)
            own_part = own_part + jnp.dot(coupling_here.astype(jnp.float32), vec_before.astype(jnp.float32), preferred_element_type=jnp.float32)
            back_part = lax.dot_general(coupling_here.astype(jnp.float32), vec_here.astype(jnp.float32), (((0,), (0,)), ((), ())), preferred_element_type=jnp.float32)
            return (own_part, back_part)
        own_part, back_part = lax.map(local_terms, (diag_time, coupling_time, rounded, before))
        after = jnp.concatenate([back_part[1:], jnp.zeros_like(back_part[:1])], axis=0)
        return own_part + after
    resid_new = rhs_time
    resid_old = jnp.zeros_like(rhs_time)
    pre_vec = precon(rhs_time)
    beta_now = jnp.sqrt(inner_prod(rhs_time, pre_vec))
    old_beta = jnp.zeros_like(beta_now)
    phi_bar = beta_now
    cosine = -jnp.ones_like(beta_now)
    sine_now = jnp.zeros_like(beta_now)
    eps_now = jnp.zeros_like(beta_now)
    d_bar = jnp.zeros_like(beta_now)
    dir_now = jnp.zeros_like(rhs_time)
    dir_old = jnp.zeros_like(rhs_time)
    solution = jnp.zeros_like(rhs_time)
    for step in range(ITERS):
        lanczos = pre_vec / beta_now
        image = operator(lanczos)
        if step > 0:
            image = image - beta_now / old_beta * resid_old
        alpha_now = inner_prod(lanczos, image)
        resid_old = resid_new
        resid_new = image - alpha_now / beta_now * resid_new
        pre_vec = precon(resid_new)
        old_beta = beta_now
        beta_now = jnp.sqrt(inner_prod(resid_new, pre_vec))
        old_eps = eps_now
        delta_now = cosine * d_bar + sine_now * alpha_now
        g_bar = sine_now * d_bar - cosine * alpha_now
        eps_now = sine_now * beta_now
        d_bar = -cosine * beta_now
        gamma_now = jnp.sqrt(g_bar * g_bar + beta_now * beta_now)
        cosine = g_bar / gamma_now
        sine_now = beta_now / gamma_now
        phi_now = cosine * phi_bar
        phi_bar = sine_now * phi_bar
        dir_next = (lanczos - old_eps * dir_old - delta_now * dir_now) / gamma_now
        dir_old = dir_now
        dir_now = dir_next
        solution = solution + phi_now * dir_now
    solution_slots = solution[order].reshape(N_TR, N_TC, B, R)
    return (solution_slots, phi_bar)
```

```python
import functools

import jax
import jax.numpy as jnp
from jax import lax
from jax.experimental import pallas as pl
from jax.experimental.pallas import tpu as pltpu
from jax.sharding import PartitionSpec as P

ITERS = 3
BASIS = ITERS + 1
PAIRS = tuple((i, j) for i in range(BASIS) for j in range(i, BASIS))
LEAF = 256
F32 = jnp.float32
BF16 = jnp.bfloat16
MIB = 2**20


def vmem():
    return pl.BlockSpec(memory_space=pltpu.VMEM)


def smem():
    return pl.BlockSpec(memory_space=pltpu.SMEM)


def pinned(x):
    return pltpu.with_memory_space_constraint(x, pltpu.VMEM)


def params(mib):
    return pltpu.CompilerParams(vmem_limit_bytes=mib * MIB)


def mm(a, b):
    return lax.dot_general(a, b, (((1,), (0,)), ((), ())), preferred_element_type=F32)


def tn(a, b):
    return lax.dot_general(a, b, (((0,), (0,)), ((), ())), preferred_element_type=F32)


def split(x):
    high = x.astype(BF16)
    return high, (x - high.astype(F32)).astype(BF16)


def mm3(a, b):
    return mm(a[0], b[0]) + (mm(a[0], b[1]) + mm(a[1], b[0]))


def tn3(a, b):
    return tn(a[0], b[0]) + (tn(a[0], b[1]) + tn(a[1], b[0]))


def column_norm(x):
    return jnp.max(jnp.sum(jnp.abs(x), axis=0, keepdims=True), axis=1, keepdims=True)


def pivot_inverse(block):
    n = block.shape[0]
    rows = lax.broadcasted_iota(jnp.int32, (n, n), 0)
    cols = lax.broadcasted_iota(jnp.int32, (n, n), 1)
    eye = jnp.where(rows == cols, 1.0, 0.0).astype(F32)
    alpha = 1.8 / column_norm(block)
    parts = split(block)
    power = eye - alpha * block
    inv = alpha * (eye + power)
    power = power.astype(BF16)
    for _ in range(4):
        power = mm(power, power).astype(BF16)
        inv = inv + mm(inv.astype(BF16), power)
    high = inv.astype(BF16)
    resid = eye - (mm(parts[0], high) + mm(parts[1], high))
    inv = high.astype(F32) + mm(high, resid.astype(BF16))
    inv_parts = split(inv)
    resid = eye - mm3(parts, inv_parts)
    inv = inv + mm(inv_parts[0], resid.astype(BF16))

    def unfinished(carry):
        return jnp.logical_and(carry[2] > 5e-3, carry[0] < 80)

    def refine(carry):
        count, x, _ = carry
        error = eye - jnp.dot(block, x, precision=lax.Precision.HIGHEST)
        x = x + jnp.dot(x, error, precision=lax.Precision.HIGHEST)
        return count + 1, x, jnp.max(column_norm(error))

    return lax.while_loop(
        unfinished, refine, (jnp.int32(0), inv, jnp.max(column_norm(resid)))
    )[1]


def store_applied(out_ref, high_ref, low_ref, vec_ref):
    high, low = split(vec_ref[...])
    both = jnp.concatenate([high, low], axis=1)
    width = high.shape[1]
    for k in range(0, out_ref.shape[0], LEAF):
        rows = pl.ds(k, LEAF)
        part = mm(high_ref[rows, :], both)
        out_ref[rows, :] = part[:, :width] + (part[:, width:] + mm(low_ref[rows, :], high))


def inverse_kernel(p_ref, rhs_ref, c_ref, high_ref, low_ref, ct_ref, vec_ref, size_ref, work, scale):
    n = p_ref.shape[0]
    rows = lax.broadcasted_iota(jnp.int32, (128, 128), 0)
    cols = lax.broadcasted_iota(jnp.int32, (128, 128), 1)
    lanes = []
    for k in range(0, n, 128):
        at = pl.ds(k, 128)
        diag = jnp.where(rows == cols, p_ref[at, at], 0.0)
        scale[at, :] = jnp.broadcast_to(lax.rsqrt(jnp.sum(diag, axis=1, keepdims=True)), (128, 128))
        lanes.append(lax.rsqrt(jnp.sum(diag, axis=0, keepdims=True)))
    lanes = jnp.concatenate(lanes, axis=1)
    starts = range(0, n, LEAF)
    for k in starts:
        at = pl.ds(k, LEAF)
        work[at, :] = p_ref[at, :] * scale[at, :][:, :1] * lanes
    for k in starts:
        at = pl.ds(k, LEAF)
        pivot = pivot_inverse(work[at, at])
        pivot_parts = split(pivot)
        old, new = {}, {}
        for j in starts:
            if j != k:
                old[j] = split(work[at, pl.ds(j, LEAF)])
                row = mm3(pivot_parts, old[j])
                new[j] = split(row)
                work[at, pl.ds(j, LEAF)] = row
        for i in old:
            for j in old:
                spot = (pl.ds(i, LEAF), pl.ds(j, LEAF))
                work[spot] = work[spot] - tn3(old[i], new[j])
            work[pl.ds(i, LEAF), at] = work[at, pl.ds(i, LEAF)].T
        work[at, at] = -pivot
    largest = jnp.zeros((1, 1), F32)
    for k in starts:
        at = pl.ds(k, LEAF)
        inv = -(work[at, :] * scale[at, :][:, :1] * lanes)
        high_ref[at, :], low_ref[at, :] = split(inv)
        largest = jnp.maximum(largest, jnp.max(jnp.max(jnp.abs(inv), axis=0, keepdims=True), axis=1, keepdims=True))
        ct_ref[:, at] = c_ref[at, :].T
    size_ref[...] = jnp.broadcast_to(largest, size_ref.shape)
    store_applied(vec_ref, high_ref, low_ref, rhs_ref)


def invert(precond, rhs, coupling):
    n, width = rhs.shape
    return pl.pallas_call(
        inverse_kernel,
        out_shape=[
            pltpu.VMEM((n, n), BF16),
            pltpu.VMEM((n, n), BF16),
            pltpu.VMEM((n, n), BF16),
            pltpu.VMEM((n, width), F32),
            pltpu.VMEM((8, width), F32),
        ],
        in_specs=[vmem()] * 3,
        out_specs=[vmem()] * 5,
        scratch_shapes=[pltpu.VMEM((n, n), F32), pltpu.VMEM((n, 128), F32)],
        compiler_params=params(32),
    )(pinned(precond), pinned(rhs), pinned(coupling))


def write_messages(flags, ct_ref, vec_ref, out_refs):
    high = vec_ref[...].astype(BF16)
    for k in range(0, vec_ref.shape[0], LEAF):
        rows = pl.ds(k, LEAF)
        back = mm(ct_ref[rows, :], high).astype(BF16)
        ahead = high[k:k + LEAF, :]
        for d, out in enumerate(out_refs):
            out[rows, :] = jnp.where(flags[d] == 1, ahead, jnp.where(flags[4 + d] == 1, back, jnp.zeros_like(back)))


def message_kernel(flags, ct_ref, vec_ref, *out_refs):
    write_messages(flags, ct_ref, vec_ref, out_refs)


def own_kernel(diag_ref, vec_ref, out_ref):
    both = jnp.concatenate(split(vec_ref[...]), axis=1)
    width = vec_ref.shape[1]
    for k in range(0, out_ref.shape[0], LEAF):
        rows = pl.ds(k, LEAF)
        part = mm(diag_ref[rows, :], both)
        out_ref[rows, :] = part[:, :width] + part[:, width:]


def residual_rows(flags, own_ref, c_ref, got, out_ref):
    zero = jnp.zeros(got[0].shape, BF16)
    before = zero
    for d, ref in enumerate(got):
        before = jnp.where(flags[4 + d] == 1, ref[...], before)
    for k in range(0, out_ref.shape[0], LEAF):
        rows = pl.ds(k, LEAF)
        after = zero[:LEAF]
        for d, ref in enumerate(got):
            after = jnp.where(flags[d] == 1, ref[rows, :], after)
        out_ref[rows, :] = own_ref[rows, :] + mm(c_ref[rows, :], before) + after.astype(F32)


def step_kernel(flags, own_ref, c_ref, ct_ref, high_ref, low_ref, g0, g1, g2, g3, res_ref, vec_ref, *out_refs):
    residual_rows(flags, own_ref, c_ref, (g0, g1, g2, g3), res_ref)
    store_applied(vec_ref, high_ref, low_ref, res_ref)
    write_messages(flags, ct_ref, vec_ref, out_refs)


def last_kernel(flags, own_ref, c_ref, high_ref, low_ref, size_ref, r0, p0, r1, p1, r2, p2, g0, g1, g2, g3, out_ref, r3, p3):
    residual_rows(flags, own_ref, c_ref, (g0, g1, g2, g3), r3)
    store_applied(p3, high_ref, low_ref, r3)
    res = (r0, r1, r2, r3)
    vec = (p0, p1, p2, p3)
    unit = size_ref[0:1, :]
    sizes = [jnp.maximum(jnp.max(jnp.abs(r[...]), axis=0, keepdims=True), 1e-30) for r in res]
    rows = [jnp.zeros_like(unit)] * len(PAIRS)
    for k in range(0, r3.shape[0], LEAF):
        at = pl.ds(k, LEAF)
        left = [res[i][at, :] / sizes[i] for i in range(BASIS)]
        right = [vec[i][at, :] / (sizes[i] * unit) for i in range(BASIS)]
        for m, (i, j) in enumerate(PAIRS):
            rows[m] = rows[m] + jnp.sum(left[i] * right[j], axis=0, keepdims=True)
    rows = rows + sizes + [unit]
    rows = rows + [jnp.zeros_like(unit)] * (16 - len(rows))
    packed = jnp.concatenate(rows, axis=0)
    for d in range(out_ref.shape[0]):
        out_ref[d] = packed


def merge(got):
    count = len(PAIRS)
    sizes = [jnp.max(got[:, count + i, :], axis=0, keepdims=True) for i in range(BASIS)]
    unit = jnp.max(got[:, count + BASIS, :], axis=0, keepdims=True)
    share = [got[:, count + i, :] / sizes[i] for i in range(BASIS)]
    unit_share = got[:, count + BASIS, :] / unit
    rows = []
    for m, (i, j) in enumerate(PAIRS):
        rows.append(jnp.sum(got[:, m, :] * (share[i] * share[j] * unit_share), axis=0, keepdims=True))
    return rows, sizes, unit


def merge_kernel(in_ref, out_ref):
    rows, sizes, unit = merge(in_ref[...])
    rows = rows + sizes + [unit]
    rows = rows + [jnp.zeros_like(unit)] * (16 - len(rows))
    packed = jnp.concatenate(rows, axis=0)
    for d in range(out_ref.shape[0]):
        out_ref[d] = packed


def recurrence(rows, sizes, unit):
    gram = {}
    for m, (i, j) in enumerate(PAIRS):
        gram[i, j] = gram[j, i] = rows[m]
    lead = sizes[1] / sizes[0]
    grow = [sizes[j + 1] / sizes[j] / lead for j in range(ITERS)]
    zero = jnp.zeros_like(unit)

    def dot(a, b):
        return sum(a[i] * b[j] * gram[i, j] for i in a for j in b)

    def axpy(a, x, y):
        out = {i: a * v for i, v in x.items()}
        for i, v in y.items():
            out[i] = out[i] + v if i in out else v
        return out

    resid_new = {0: jnp.ones_like(unit)}
    resid_old = {}
    beta_now = jnp.sqrt(dot(resid_new, resid_new))
    old_beta = zero
    phi_bar = beta_now
    cosine = -jnp.ones_like(unit)
    sine_now = eps_now = d_bar = zero
    dir_now, dir_old, total = {}, {}, {}
    for step in range(ITERS):
        lanczos = {i: v / beta_now for i, v in resid_new.items()}
        image = {i + 1: v * grow[i] for i, v in lanczos.items()}
        if step > 0:
            image = axpy(-beta_now / old_beta, resid_old, image)
        alpha_now = dot(lanczos, image)
        resid_old = resid_new
        resid_new = axpy(-alpha_now / beta_now, resid_new, image)
        old_beta = beta_now
        beta_now = jnp.sqrt(dot(resid_new, resid_new))
        old_eps = eps_now
        delta_now = cosine * d_bar + sine_now * alpha_now
        g_bar = sine_now * d_bar - cosine * alpha_now
        eps_now = sine_now * beta_now
        d_bar = -cosine * beta_now
        gamma_now = jnp.sqrt(g_bar * g_bar + beta_now * beta_now)
        cosine = g_bar / gamma_now
        sine_now = beta_now / gamma_now
        phi_now = cosine * phi_bar
        phi_bar = sine_now * phi_bar
        dir_next = axpy(-old_eps, dir_old, axpy(-delta_now, dir_now, lanczos))
        dir_next = {i: v / gamma_now for i, v in dir_next.items()}
        dir_old, dir_now = dir_now, dir_next
        total = axpy(phi_now, dir_now, total)
    coefs = [total[i] * (sizes[0] / sizes[i]) / lead for i in range(ITERS)]
    return coefs, phi_bar * sizes[0] * jnp.sqrt(unit)


def finish_kernel(in_ref, p0, p1, p2, out_ref, norm_ref):
    coefs, norm = recurrence(*merge(in_ref[...]))
    norm_ref[...] = norm
    for k in range(0, out_ref.shape[0], LEAF):
        at = pl.ds(k, LEAF)
        out_ref[at, :] = coefs[0] * p0[at, :] + coefs[1] * p1[at, :] + coefs[2] * p2[at, :]


def neighbour_perms(count):
    even = [(i, i ^ 1) for i in range(count)]
    odd = [(i, i + 1) for i in range(1, count - 1, 2)]
    return even, odd + [(j, i) for i, j in odd]


def exchange(values):
    even_r, odd_r = neighbour_perms(lax.axis_size("tr"))
    even_c, odd_c = neighbour_perms(lax.axis_size("tc"))
    return [
        lax.ppermute(values[0], "tr", odd_r),
        lax.ppermute(values[1], "tc", odd_c),
        lax.ppermute(values[2], "tr", even_r),
        lax.ppermute(values[3], "tc", even_c),
    ]


def body(diag_block, coupling, precond, rhs, slot_time):
    diag_here = diag_block[0, 0]
    coupling_here = coupling[0, 0]
    rhs_here = rhs[0, 0]
    n, width = rhs_here.shape
    tags = exchange([slot_time + 1] * 4)
    own_time = slot_time[0, 0]
    tags = jnp.concatenate([t.reshape(1) for t in tags])
    flags = jnp.concatenate([tags == own_time + 2, tags == own_time]).astype(jnp.int32)
    whole = jax.ShapeDtypeStruct((n, width), F32)
    sent = [jax.ShapeDtypeStruct((n, width), BF16)] * 4

    high, low, flipped, vec, size = invert(precond[0, 0], rhs_here, coupling_here)
    messages = pl.pallas_call(
        message_kernel,
        out_shape=sent,
        in_specs=[smem(), vmem(), vmem()],
        out_specs=[vmem()] * 4,
        compiler_params=params(8),
    )(flags, pinned(flipped), pinned(vec))
    basis = [rhs_here, vec]
    for step in range(ITERS):
        got = exchange(messages)
        own = pl.pallas_call(
            own_kernel,
            out_shape=pltpu.VMEM((n, width), F32),
            in_specs=[vmem()] * 2,
            out_specs=vmem(),
            compiler_params=params(8),
        )(pinned(diag_here), pinned(vec))
        if step < ITERS - 1:
            out = pl.pallas_call(
                step_kernel,
                out_shape=[pltpu.VMEM((n, width), F32)] * 2 + sent,
                in_specs=[smem()] + [vmem()] * 9,
                out_specs=[vmem()] * 6,
                compiler_params=params(12),
            )(flags, pinned(own), pinned(coupling_here), pinned(flipped), pinned(high), pinned(low), *got)
            vec = out[1]
            basis += [out[0], vec]
            messages = out[2:]
    count = lax.axis_size("tc")
    part = pl.pallas_call(
        last_kernel,
        out_shape=jax.ShapeDtypeStruct((count, 16, width), F32),
        in_specs=[smem()] + [vmem()] * 15,
        out_specs=vmem(),
        scratch_shapes=[pltpu.VMEM((n, width), F32)] * 2,
        compiler_params=params(12),
    )(flags, pinned(own), pinned(coupling_here), pinned(high), pinned(low), pinned(size), *[pinned(b) for b in basis], *got)
    part = lax.all_to_all(part, "tc", 0, 0, tiled=True)
    part = pl.pallas_call(
        merge_kernel,
        out_shape=jax.ShapeDtypeStruct((lax.axis_size("tr"), 16, width), F32),
        in_specs=[vmem()],
        out_specs=vmem(),
    )(part)
    part = lax.all_to_all(part, "tr", 0, 0, tiled=True)
    solution, norm = pl.pallas_call(
        finish_kernel,
        out_shape=[whole, jax.ShapeDtypeStruct((1, width), F32)],
        in_specs=[vmem()] * 4,
        out_specs=[vmem()] * 2,
        compiler_params=params(8),
    )(part, pinned(basis[1]), pinned(basis[3]), pinned(basis[5]))
    return (solution[None, None], norm[0])


def solution(mesh):
    placed = (
        P("tr", "tc", None, None),
        P("tr", "tc", None, None),
        P("tr", "tc", None, None),
        P("tr", "tc", None, None),
        P("tr", "tc"),
    )
    return jax.shard_map(
        body,
        mesh=mesh,
        in_specs=placed,
        out_specs=(P("tr", "tc", None, None), P()),
        check_vma=False,
    )
```

```python
import functools

import jax
import jax.numpy as jnp
from jax import lax
from jax.experimental import pallas as pl
from jax.experimental.pallas import tpu as pltpu
from jax.sharding import PartitionSpec as P

ITERS = 3
BASIS = ITERS + 1
PAIRS = tuple((i, j) for i in range(BASIS) for j in range(i, BASIS))
LEAF = 256
SLOTS = 16
F32 = jnp.float32
BF16 = jnp.bfloat16
MIB = 2**20


def vmem():
    return pl.BlockSpec(memory_space=pltpu.VMEM)


def smem():
    return pl.BlockSpec(memory_space=pltpu.SMEM)


def pinned(x):
    return pltpu.with_memory_space_constraint(x, pltpu.VMEM)


def params(mib):
    return pltpu.CompilerParams(vmem_limit_bytes=mib * MIB)


def mm(a, b):
    return lax.dot_general(a, b, (((1,), (0,)), ((), ())), preferred_element_type=F32)


def tn(a, b):
    return lax.dot_general(a, b, (((0,), (0,)), ((), ())), preferred_element_type=F32)


def split(x):
    high = x.astype(BF16)
    return high, (x - high.astype(F32)).astype(BF16)


def mm3(a, b):
    return mm(a[0], b[0]) + (mm(a[0], b[1]) + mm(a[1], b[0]))


def tn3(a, b):
    return tn(a[0], b[0]) + (tn(a[0], b[1]) + tn(a[1], b[0]))


def whole(x):
    return x


def mm_full(a, b):
    return lax.dot_general(a, b, (((1,), (0,)), ((), ())), precision=lax.Precision.HIGHEST)


def tn_full(a, b):
    return lax.dot_general(a, b, (((0,), (0,)), ((), ())), precision=lax.Precision.HIGHEST)


def column_norm(x):
    return jnp.max(jnp.sum(jnp.abs(x), axis=0, keepdims=True), axis=1, keepdims=True)


def pivot_steps(block, robust):
    n = block.shape[0]
    rows = lax.broadcasted_iota(jnp.int32, (n, n), 0)
    cols = lax.broadcasted_iota(jnp.int32, (n, n), 1)
    eye = jnp.where(rows == cols, 1.0, 0.0).astype(F32)
    diag = jnp.where(rows == cols, block, 0.0)
    across = lax.rsqrt(jnp.sum(diag, axis=0, keepdims=True))
    down = lax.rsqrt(jnp.sum(diag, axis=1, keepdims=True))
    scaled = block * down * across
    parts = split(scaled)
    square = mm(parts[0], parts[0])
    yield
    alpha = 1.8 * lax.rsqrt(column_norm(square))
    power = (eye - (2.0 * alpha) * scaled + (alpha * alpha) * square).astype(BF16)
    inv = alpha * (2.0 * eye - alpha * scaled)
    for _ in range(2):
        inv = inv + mm(inv.astype(BF16), power)
        power = mm(power, power).astype(BF16)
        yield
    inv = inv + mm(inv.astype(BF16), power)
    yield
    high = inv.astype(BF16)
    resid = eye - (mm(parts[0], high) + mm(parts[1], high))
    yield
    inv = high.astype(F32) + mm(high, resid.astype(BF16))
    yield
    inv_parts = split(inv)
    resid = eye - mm3(parts, inv_parts)
    yield
    inv = inv + mm(inv_parts[0], resid.astype(BF16))
    error = column_norm(resid)
    if robust:

        def unfinished(carry):
            return jnp.logical_and(carry[2] > 1e-3, carry[0] < 80)

        def refine(carry):
            count, x, _ = carry
            left = eye - mm_full(scaled, x)
            x = x + mm_full(x, left)
            return count + 1, x, jnp.max(column_norm(left))

        inv = lax.while_loop(unfinished, refine, (jnp.int32(0), inv, jnp.max(error)))[1]
    return inv * down * across, error


def interleave(steps, pending):
    while True:
        try:
            next(steps)
        except StopIteration as stop:
            return stop.value
        if pending:
            pending.pop(0)()


def eliminate(n, work, vec, extra, before, after, robust):
    blocks = n // LEAF
    at = [pl.ds(k * LEAF, LEAF) for k in range(blocks)]
    cut, nn, tn_ = (whole, mm_full, tn_full) if robust else (split, mm3, tn3)
    worst = jnp.zeros((1, 1), F32)
    pending = []
    for k in range(blocks):
        before(k)
        pivot, error = interleave(pivot_steps(work[at[k], at[k]], robust), pending)
        for task in pending:
            task()
        after(k)
        worst = jnp.maximum(worst, error)
        parts = cut(pivot)
        work[at[k], at[k]] = pivot
        old, row = {}, {}

        def scale_row(j, k=k, old=old, row=row, parts=parts):
            old[j] = cut(work[at[k], at[j]])
            value = nn(parts, old[j])
            row[j] = cut(value)
            work[at[k], at[j]] = value

        def update(i, j, old=old, row=row):
            work[at[i], at[j]] = work[at[i], at[j]] - tn_(old[i], row[j])

        def push(i, k=k, row=row):
            vec[at[i], :] = vec[at[i], :] - tn_(row[i], cut(vec[at[k], :]))

        def solve(k=k, parts=parts):
            vec[at[k], :] = nn(parts, cut(vec[at[k], :]))

        pending = []
        later = range(k + 1, blocks)
        for j in later:
            if j == k + 1:
                scale_row(j)
                update(j, j)
            else:
                pending.append(functools.partial(scale_row, j))
        for i in later:
            for j in range(i, blocks):
                if (i, j) != (k + 1, k + 1):
                    pending.append(functools.partial(update, i, j))
        for i in later:
            pending.append(functools.partial(push, i))
        pending.append(solve)
        pending += extra(k)
    for task in pending:
        task()
    for k in reversed(range(blocks - 1)):
        total = vec[at[k], :]
        for j in range(k + 1, blocks):
            total = total - nn(cut(work[at[k], at[j]]), cut(vec[at[j], :]))
        vec[at[k], :] = total
    return worst


def factor_kernel(own, t0, t1, t2, t3, p_hbm, rhs_hbm, c_hbm, d_hbm, work, c_ref, ct_ref, d_ref, rhs_ref, vec, m0, m1, m2, m3, sems):
    n = work.shape[0]
    blocks = n // LEAF
    panels = [
        pltpu.make_async_copy(p_hbm.at[pl.ds(k * LEAF, LEAF), :], work.at[pl.ds(k * LEAF, LEAF), :], sems.at[k])
        for k in range(blocks)
    ]
    others = [
        pltpu.make_async_copy(src, dst, sems.at[blocks + i])
        for i, (src, dst) in enumerate(((rhs_hbm, rhs_ref), (c_hbm, c_ref), (d_hbm, d_ref)))
    ]
    for copy in panels + others:
        copy.start()

    def before(k):
        if k == 0:
            panels[0].wait()
        elif k == 1:
            others[1].wait()

    def after(k):
        if k == 0:
            for copy in panels[1:]:
                copy.wait()
            others[0].wait()
            vec[...] = rhs_ref[...]

    def flip(k):
        ct_ref[:, pl.ds(k * LEAF, LEAF)] = c_ref[pl.ds(k * LEAF, LEAF), :].T

    def extra(k):
        if k == 0:
            return []
        if k == blocks - 1:
            return []
        span = blocks // 2
        return [functools.partial(flip, j) for j in range((k - 1) * span, k * span)]

    worst = eliminate(n, work, vec, extra, before, after, False)

    @pl.when(jnp.logical_not(jnp.max(worst) < 5e-3))
    def _():
        for copy in panels:
            copy.start()
        for copy in panels:
            copy.wait()
        vec[...] = rhs_ref[...]
        eliminate(n, work, vec, lambda k: [], lambda k: None, lambda k: None, True)

    others[2].wait()
    write_messages((own, t0, t1, t2, t3), ct_ref, vec, (m0, m1, m2, m3))


def factor(tags, precond, rhs, coupling, diag):
    n, width = rhs.shape
    square = pltpu.VMEM((n, n), BF16)
    column = pltpu.VMEM((n, width), F32)
    anywhere = pl.BlockSpec(memory_space=pl.ANY)
    return pl.pallas_call(
        factor_kernel,
        out_shape=[pltpu.VMEM((n, n), F32), square, square, square, column, column]
        + [jax.ShapeDtypeStruct((n, width), BF16)] * 4,
        in_specs=[smem()] * 5 + [anywhere] * 4,
        out_specs=[vmem()] * 10,
        scratch_shapes=[pltpu.SemaphoreType.DMA((n // LEAF + 3,))],
        compiler_params=params(20),
    )(*tags, precond, rhs, coupling, diag)


def build_kernel(work, high_ref, low_ref, size_ref):
    n = work.shape[0]
    blocks = n // LEAF
    at = [pl.ds(k * LEAF, LEAF) for k in range(blocks)]
    inv = {}
    largest = jnp.zeros((1, 1), F32)
    for k in reversed(range(blocks)):
        row = {j: split(work[at[k], at[j]]) for j in range(k + 1, blocks)}
        made = {}
        for j in range(k + 1, blocks):
            made[j] = -sum(mm3(row[m], inv[m, j]) for m in range(k + 1, blocks))
            inv[k, j] = split(made[j])
            flipped = made[j].T
            inv[j, k] = split(flipped)
        made[k] = work[at[k], at[k]] - sum([mm3(row[m], inv[m, k]) for m in range(k + 1, blocks)])
        inv[k, k] = split(made[k])
        for j in range(k, blocks):
            high_ref[at[k], at[j]], low_ref[at[k], at[j]] = inv[k, j]
            if j != k:
                high_ref[at[j], at[k]], low_ref[at[j], at[k]] = inv[j, k]
            largest = jnp.maximum(largest, jnp.max(jnp.max(jnp.abs(made[j]), axis=0, keepdims=True), axis=1, keepdims=True))
    size_ref[...] = jnp.broadcast_to(largest, size_ref.shape)


def build(work, width):
    n = work.shape[0]
    return pl.pallas_call(
        build_kernel,
        out_shape=[pltpu.VMEM((n, n), BF16), pltpu.VMEM((n, n), BF16), pltpu.VMEM((8, width), F32)],
        in_specs=[vmem()],
        out_specs=[vmem()] * 3,
        compiler_params=params(16),
    )(pinned(work))


def store_applied(out_ref, high_ref, low_ref, vec_ref):
    high, low = split(vec_ref[...])
    both = jnp.concatenate([high, low], axis=1)
    width = high.shape[1]
    for k in range(0, out_ref.shape[0], LEAF):
        rows = pl.ds(k, LEAF)
        part = mm(high_ref[rows, :], both)
        out_ref[rows, :] = part[:, :width] + (part[:, width:] + mm(low_ref[rows, :], high))


def relation(tags):
    own = tags[0][0, 0]
    return [t[0, 0] == own + 2 for t in tags[1:]], [t[0, 0] == own for t in tags[1:]]


def write_messages(tags, ct_ref, vec_ref, out_refs):
    is_next, is_prev = relation(tags)
    high = vec_ref[...].astype(BF16)
    for k in range(0, vec_ref.shape[0], LEAF):
        rows = pl.ds(k, LEAF)
        back = mm(ct_ref[rows, :], high).astype(BF16)
        ahead = high[k:k + LEAF, :]
        for d, out in enumerate(out_refs):
            out[rows, :] = jnp.where(is_next[d], ahead, jnp.where(is_prev[d], back, jnp.zeros_like(back)))


def own_kernel(diag_ref, vec_ref, out_ref):
    both = jnp.concatenate(split(vec_ref[...]), axis=1)
    width = vec_ref.shape[1]
    for k in range(0, out_ref.shape[0], LEAF):
        rows = pl.ds(k, LEAF)
        part = mm(diag_ref[rows, :], both)
        out_ref[rows, :] = part[:, :width] + part[:, width:]


def residual_rows(tags, own_ref, c_ref, got, out_ref):
    is_next, is_prev = relation(tags)
    zero = jnp.zeros(got[0].shape, BF16)
    before = zero
    for d, ref in enumerate(got):
        before = jnp.where(is_prev[d], ref[...], before)
    for k in range(0, out_ref.shape[0], LEAF):
        rows = pl.ds(k, LEAF)
        after = zero[:LEAF]
        for d, ref in enumerate(got):
            after = jnp.where(is_next[d], ref[rows, :], after)
        out_ref[rows, :] = own_ref[rows, :] + mm(c_ref[rows, :], before) + after.astype(F32)


def step_kernel(t, t0, t1, t2, t3, own_ref, c_ref, ct_ref, high_ref, low_ref, g0, g1, g2, g3, res_ref, vec_ref, *out_refs):
    tags = (t, t0, t1, t2, t3)
    residual_rows(tags, own_ref, c_ref, (g0, g1, g2, g3), res_ref)
    store_applied(vec_ref, high_ref, low_ref, res_ref)
    write_messages(tags, ct_ref, vec_ref, out_refs)


def pack(rows, out_ref):
    rows = rows + [jnp.zeros_like(rows[0])] * (SLOTS - len(rows))
    packed = jnp.concatenate(rows, axis=0)
    for d in range(0, out_ref.shape[0], SLOTS):
        out_ref[pl.ds(d, SLOTS), :] = packed


def last_kernel(t, t0, t1, t2, t3, own_ref, c_ref, high_ref, low_ref, size_ref, r0, p0, r1, p1, r2, p2, g0, g1, g2, g3, out_ref, r3, p3):
    residual_rows((t, t0, t1, t2, t3), own_ref, c_ref, (g0, g1, g2, g3), r3)
    store_applied(p3, high_ref, low_ref, r3)
    res = (r0, r1, r2, r3)
    vec = (p0, p1, p2, p3)
    unit = size_ref[0:1, :]
    sizes = [jnp.maximum(jnp.max(jnp.abs(r[...]), axis=0, keepdims=True), 1e-30) for r in res]
    left_scale = [1.0 / v for v in sizes]
    right_scale = [1.0 / (v * unit) for v in sizes]
    rows = [jnp.zeros_like(unit)] * len(PAIRS)
    for k in range(0, r3.shape[0], LEAF):
        at = pl.ds(k, LEAF)
        left = [res[i][at, :] * left_scale[i] for i in range(BASIS)]
        right = [vec[i][at, :] * right_scale[i] for i in range(BASIS)]
        for m, (i, j) in enumerate(PAIRS):
            rows[m] = rows[m] + jnp.sum(left[i] * right[j], axis=0, keepdims=True)
    pack(rows + sizes + [unit], out_ref)


def merge(in_ref):
    senders = in_ref.shape[0] // SLOTS
    got = [in_ref[pl.ds(m, senders, stride=SLOTS), :] for m in range(len(PAIRS) + BASIS + 1)]
    size_rows, unit_row = got[len(PAIRS):-1], got[-1]
    sizes = [jnp.max(v, axis=0, keepdims=True) for v in size_rows]
    unit = jnp.max(unit_row, axis=0, keepdims=True)
    share = [v / top for v, top in zip(size_rows, sizes)]
    unit_share = unit_row / unit
    rows = []
    for m, (i, j) in enumerate(PAIRS):
        rows.append(jnp.sum(got[m] * (share[i] * share[j] * unit_share), axis=0, keepdims=True))
    return rows, sizes, unit


def merge_kernel(in_ref, out_ref):
    rows, sizes, unit = merge(in_ref)
    pack(rows + sizes + [unit], out_ref)


def recurrence(rows, sizes, unit):
    gram = {}
    for m, (i, j) in enumerate(PAIRS):
        gram[i, j] = gram[j, i] = rows[m]
    lead = sizes[1] / sizes[0]
    grow = [sizes[j + 1] / sizes[j] / lead for j in range(ITERS)]
    zero = jnp.zeros_like(unit)

    def dot(a, b):
        return sum(a[i] * b[j] * gram[i, j] for i in a for j in b)

    def axpy(a, x, y):
        out = {i: a * v for i, v in x.items()}
        for i, v in y.items():
            out[i] = out[i] + v if i in out else v
        return out

    resid_new = {0: jnp.ones_like(unit)}
    resid_old = {}
    beta_now = jnp.sqrt(dot(resid_new, resid_new))
    old_beta = zero
    phi_bar = beta_now
    cosine = -jnp.ones_like(unit)
    sine_now = eps_now = d_bar = zero
    dir_now, dir_old, total = {}, {}, {}
    for step in range(ITERS):
        lanczos = {i: v / beta_now for i, v in resid_new.items()}
        image = {i + 1: v * grow[i] for i, v in lanczos.items()}
        if step > 0:
            image = axpy(-beta_now / old_beta, resid_old, image)
        alpha_now = dot(lanczos, image)
        resid_old = resid_new
        resid_new = axpy(-alpha_now / beta_now, resid_new, image)
        old_beta = beta_now
        beta_now = jnp.sqrt(dot(resid_new, resid_new))
        old_eps = eps_now
        delta_now = cosine * d_bar + sine_now * alpha_now
        g_bar = sine_now * d_bar - cosine * alpha_now
        eps_now = sine_now * beta_now
        d_bar = -cosine * beta_now
        gamma_now = jnp.sqrt(g_bar * g_bar + beta_now * beta_now)
        cosine = g_bar / gamma_now
        sine_now = beta_now / gamma_now
        phi_now = cosine * phi_bar
        phi_bar = sine_now * phi_bar
        dir_next = axpy(-old_eps, dir_old, axpy(-delta_now, dir_now, lanczos))
        dir_next = {i: v / gamma_now for i, v in dir_next.items()}
        dir_old, dir_now = dir_now, dir_next
        total = axpy(phi_now, dir_now, total)
    coefs = [total[i] * (sizes[0] / sizes[i]) / lead for i in range(ITERS)]
    return coefs, phi_bar * sizes[0] * jnp.sqrt(unit)


def finish_kernel(in_ref, p0, p1, p2, out_ref, norm_ref):
    coefs, norm = recurrence(*merge(in_ref))
    norm_ref[...] = norm
    for k in range(0, out_ref.shape[0], LEAF):
        at = pl.ds(k, LEAF)
        out_ref[at, :] = coefs[0] * p0[at, :] + coefs[1] * p1[at, :] + coefs[2] * p2[at, :]


def neighbour_perms(count):
    even = [(i, i ^ 1) for i in range(count)]
    odd = [(i, i + 1) for i in range(1, count - 1, 2)]
    return even, odd + [(j, i) for i, j in odd]


def exchange(values):
    even_r, odd_r = neighbour_perms(lax.axis_size("tr"))
    even_c, odd_c = neighbour_perms(lax.axis_size("tc"))
    return [
        lax.ppermute(values[0], "tr", odd_r),
        lax.ppermute(values[1], "tc", odd_c),
        lax.ppermute(values[2], "tr", even_r),
        lax.ppermute(values[3], "tc", even_c),
    ]


def body(diag_block, coupling, precond, rhs, slot_time):
    n, width = rhs.shape[2:]
    own_time = slot_time
    tags = [own_time] + exchange([own_time + 1] * 4)
    sent = [jax.ShapeDtypeStruct((n, width), BF16)] * 4

    work, c_here, flipped, diag_here, res, vec, *messages = factor(
        tags, precond[0, 0], rhs[0, 0], coupling[0, 0], diag_block[0, 0]
    )
    basis = [res, vec]
    for step in range(ITERS):
        got = exchange(messages)
        if step == 0:
            high, low, size = build(work, width)
        own = pl.pallas_call(
            own_kernel,
            out_shape=pltpu.VMEM((n, width), F32),
            in_specs=[vmem()] * 2,
            out_specs=vmem(),
            compiler_params=params(8),
        )(pinned(diag_here), pinned(vec))
        if step < ITERS - 1:
            out = pl.pallas_call(
                step_kernel,
                out_shape=[pltpu.VMEM((n, width), F32)] * 2 + sent,
                in_specs=[smem()] * 5 + [vmem()] * 9,
                out_specs=[vmem()] * 6,
                compiler_params=params(12),
            )(*tags, pinned(own), pinned(c_here), pinned(flipped), pinned(high), pinned(low), *got)
            vec = out[1]
            basis += [out[0], vec]
            messages = out[2:]
    part = pl.pallas_call(
        last_kernel,
        out_shape=jax.ShapeDtypeStruct((lax.axis_size("tc") * SLOTS, width), F32),
        in_specs=[smem()] * 5 + [vmem()] * 15,
        out_specs=vmem(),
        scratch_shapes=[pltpu.VMEM((n, width), F32)] * 2,
        compiler_params=params(12),
    )(*tags, pinned(own), pinned(c_here), pinned(high), pinned(low), pinned(size), *[pinned(b) for b in basis], *got)
    part = lax.all_to_all(part, "tc", 0, 0, tiled=True)
    part = pl.pallas_call(
        merge_kernel,
        out_shape=jax.ShapeDtypeStruct((lax.axis_size("tr") * SLOTS, width), F32),
        in_specs=[vmem()],
        out_specs=vmem(),
    )(part)
    part = lax.all_to_all(part, "tr", 0, 0, tiled=True)
    solution, norm = pl.pallas_call(
        finish_kernel,
        out_shape=[jax.ShapeDtypeStruct((n, width), F32), jax.ShapeDtypeStruct((1, width), F32)],
        in_specs=[vmem()] * 4,
        out_specs=[vmem()] * 2,
        compiler_params=params(8),
    )(part, pinned(basis[1]), pinned(basis[3]), pinned(basis[5]))
    return (solution[None, None], norm[0])


def solution(mesh):
    placed = (
        P("tr", "tc", None, None),
        P("tr", "tc", None, None),
        P("tr", "tc", None, None),
        P("tr", "tc", None, None),
        P("tr", "tc"),
    )
    return jax.shard_map(
        body,
        mesh=mesh,
        in_specs=placed,
        out_specs=(P("tr", "tc", None, None), P()),
        check_vma=False,
    )
```

```python
import functools

import jax
import jax.numpy as jnp
from jax import lax
from jax.experimental import pallas as pl
from jax.experimental.pallas import tpu as pltpu
from jax.sharding import PartitionSpec as P

ITERS = 3
BASIS = ITERS + 1
PAIRS = tuple((i, j) for i in range(BASIS) for j in range(i, BASIS))
LEAF = 256
SLOTS = 16
F32 = jnp.float32
BF16 = jnp.bfloat16
MIB = 2**20


def vmem():
    return pl.BlockSpec(memory_space=pltpu.VMEM)


def smem():
    return pl.BlockSpec(memory_space=pltpu.SMEM)


def pinned(x, space=pltpu.VMEM):
    return pltpu.with_memory_space_constraint(x, space)


def params(mib):
    return pltpu.CompilerParams(vmem_limit_bytes=mib * MIB)


def mm(a, b):
    return lax.dot_general(a, b, (((1,), (0,)), ((), ())), preferred_element_type=F32)


def tn(a, b):
    return lax.dot_general(a, b, (((0,), (0,)), ((), ())), preferred_element_type=F32)


def split(x):
    high = x.astype(BF16)
    return high, (x - high.astype(F32)).astype(BF16)


def mm3(a, b):
    return mm(a[0], b[0]) + (mm(a[0], b[1]) + mm(a[1], b[0]))


def tn3(a, b):
    return tn(a[0], b[0]) + (tn(a[0], b[1]) + tn(a[1], b[0]))


def mm_full(a, b):
    return lax.dot_general(a, b, (((1,), (0,)), ((), ())), precision=lax.Precision.HIGHEST)


def tn_full(a, b):
    return lax.dot_general(a, b, (((0,), (0,)), ((), ())), precision=lax.Precision.HIGHEST)


def column_norm(x):
    return jnp.max(jnp.sum(jnp.abs(x), axis=0, keepdims=True), axis=1, keepdims=True)


def pivot_steps(block):
    n = block.shape[0]
    rows = lax.broadcasted_iota(jnp.int32, (n, n), 0)
    cols = lax.broadcasted_iota(jnp.int32, (n, n), 1)
    eye = jnp.where(rows == cols, 1.0, 0.0).astype(F32)
    diag = jnp.where(rows == cols, block, 0.0)
    across = lax.rsqrt(jnp.sum(diag, axis=0, keepdims=True))
    down = lax.rsqrt(jnp.sum(diag, axis=1, keepdims=True))
    scaled = block * down * across
    parts = split(scaled)
    square = mm(parts[0], parts[0])
    yield
    alpha = 1.8 * lax.rsqrt(column_norm(square))
    power = (eye - (2.0 * alpha) * scaled + (alpha * alpha) * square).astype(BF16)
    inv = alpha * (2.0 * eye - alpha * scaled)
    for _ in range(2):
        inv = inv + mm(inv.astype(BF16), power)
        power = mm(power, power).astype(BF16)
        yield
    inv = inv + mm(inv.astype(BF16), power)
    yield
    high = inv.astype(BF16)
    resid = eye - (mm(parts[0], high) + mm(parts[1], high))
    yield
    inv = high.astype(F32) + mm(high, resid.astype(BF16))
    yield
    inv_parts = split(inv)
    resid = eye - mm3(parts, inv_parts)
    yield
    inv = inv + mm(inv_parts[0], resid.astype(BF16))
    error = column_norm(resid)
    return inv * down * across, error


def interleave(steps, pending):
    while True:
        try:
            next(steps)
        except StopIteration as stop:
            return stop.value
        if pending:
            pending.pop(0)()


def eliminate(n, work, vec, extra, before, after):
    blocks = n // LEAF
    at = [pl.ds(k * LEAF, LEAF) for k in range(blocks)]
    worst = jnp.zeros((1, 1), F32)
    pending = []
    for k in range(blocks):
        before(k)
        pivot, error = interleave(pivot_steps(work[at[k], at[k]]), pending)
        for task in pending:
            task()
        after(k)
        worst = jnp.maximum(worst, error)
        parts = split(pivot)
        work[at[k], at[k]] = pivot
        old, row = {}, {}

        def scale_row(j, k=k, old=old, row=row, parts=parts):
            old[j] = split(work[at[k], at[j]])
            value = mm3(parts, old[j])
            row[j] = split(value)
            work[at[k], at[j]] = value

        def update(i, j, old=old, row=row):
            work[at[i], at[j]] = work[at[i], at[j]] - tn3(old[i], row[j])

        def push(i, k=k, row=row):
            vec[at[i], :] = vec[at[i], :] - tn3(row[i], split(vec[at[k], :]))

        def solve(k=k, parts=parts):
            vec[at[k], :] = mm3(parts, split(vec[at[k], :]))

        pending = []
        later = range(k + 1, blocks)
        for j in later:
            if j == k + 1:
                scale_row(j)
                update(j, j)
            else:
                pending.append(functools.partial(scale_row, j))
        for i in later:
            for j in range(i, blocks):
                if (i, j) != (k + 1, k + 1):
                    pending.append(functools.partial(update, i, j))
        for i in later:
            pending.append(functools.partial(push, i))
        pending.append(solve)
        pending += extra(k)
    for task in pending:
        task()
    for k in reversed(range(blocks - 1)):
        total = vec[at[k], :]
        for j in range(k + 1, blocks):
            total = total - mm3(split(work[at[k], at[j]]), split(vec[at[j], :]))
        vec[at[k], :] = total
    return worst


def careful_inverse(block):
    n = block.shape[0]
    rows = lax.broadcasted_iota(jnp.int32, (n, n), 0)
    cols = lax.broadcasted_iota(jnp.int32, (n, n), 1)
    eye = jnp.where(rows == cols, 1.0, 0.0).astype(F32)
    diag = jnp.where(rows == cols, block, 0.0)
    across = lax.rsqrt(jnp.sum(diag, axis=0, keepdims=True))
    down = lax.rsqrt(jnp.sum(diag, axis=1, keepdims=True))
    scaled = block * down * across

    def unfinished(carry):
        return jnp.logical_and(carry[2] > 1e-3, carry[0] < 80)

    def refine(carry):
        count, x, _ = carry
        left = eye - mm_full(scaled, x)
        return count + 1, x + mm_full(x, left), jnp.max(column_norm(left))

    start = eye * (1.8 / column_norm(scaled))
    return lax.while_loop(unfinished, refine, (jnp.int32(0), start, jnp.float32(2.0)))[1] * down * across


def eliminate_careful(n, work, vec, row):
    blocks = n // LEAF

    def at(k):
        return pl.ds(pl.multiple_of(k * LEAF, LEAF), LEAF)

    def pivot(k, _):
        work[at(k), at(k)] = careful_inverse(work[at(k), at(k)])

        def scale_row(j, _):
            row[:, at(j)] = mm_full(work[at(k), at(k)], work[at(k), at(j)])
            return 0

        def update_row(i, _):
            def update(j, _):
                work[at(i), at(j)] = work[at(i), at(j)] - tn_full(work[at(k), at(i)], row[:, at(j)])
                return 0

            lax.fori_loop(i, blocks, update, 0)
            vec[at(i), :] = vec[at(i), :] - tn_full(row[:, at(i)], vec[at(k), :])
            return 0

        def keep(j, _):
            work[at(k), at(j)] = row[:, at(j)]
            return 0

        lax.fori_loop(k + 1, blocks, scale_row, 0)
        lax.fori_loop(k + 1, blocks, update_row, 0)
        lax.fori_loop(k + 1, blocks, keep, 0)
        vec[at(k), :] = mm_full(work[at(k), at(k)], vec[at(k), :])
        return 0

    def back(m, _):
        k = blocks - 2 - m

        def subtract(j, _):
            vec[at(k), :] = vec[at(k), :] - mm_full(work[at(k), at(j)], vec[at(j), :])
            return 0

        return lax.fori_loop(k + 1, blocks, subtract, 0)

    lax.fori_loop(0, blocks, pivot, 0)
    lax.fori_loop(0, blocks - 1, back, 0)


def factor_kernel(own, t0, t1, t2, t3, p_hbm, rhs_hbm, c_hbm, d_hbm, work, c_ref, ct_ref, d_ref, rhs_ref, vec, flags, m0, m1, m2, m3, row, times, sems, time_sems):
    n = work.shape[0]
    blocks = n // LEAF
    first = pl.ds(0, LEAF)
    rest = pl.ds(LEAF, n - LEAF)
    spots = [(first, first), (first, rest)] + [(pl.ds(k * LEAF, LEAF), pl.ds(0, n)) for k in range(1, blocks)]
    panels = [pltpu.make_async_copy(p_hbm.at[spot], work.at[spot], sems.at[k]) for k, spot in enumerate(spots)]
    others = [
        pltpu.make_async_copy(src, dst, sems.at[len(spots) + i])
        for i, (src, dst) in enumerate(((rhs_hbm, rhs_ref), (c_hbm, c_ref), (d_hbm, d_ref)))
    ]
    known = [pltpu.make_async_copy(t, times.at[pl.ds(d, 1), :], time_sems.at[d]) for d, t in enumerate((own, t0, t1, t2, t3))]

    def before(k):
        if k == 0:
            panels[0].start()
            panels[0].wait()
            for copy in panels[1:] + others + known:
                copy.start()
        elif k == 1:
            others[1].wait()

    def after(k):
        if k == 0:
            for copy in panels[1:]:
                copy.wait()
            others[0].wait()
            vec[...] = rhs_ref[...]

    def flip(k):
        ct_ref[:, pl.ds(k * LEAF, LEAF)] = c_ref[pl.ds(k * LEAF, LEAF), :].T

    def extra(k):
        if k == 0:
            return []
        if k == blocks - 1:
            return []
        span = blocks // 2
        return [functools.partial(flip, j) for j in range((k - 1) * span, k * span)]

    worst = eliminate(n, work, vec, extra, before, after)

    @pl.when(jnp.logical_not(jnp.max(worst) < 5e-3))
    def _():
        for copy in panels:
            copy.start()
        for copy in panels:
            copy.wait()
        vec[...] = rhs_ref[...]
        eliminate_careful(n, work, vec, row)

    others[2].wait()
    for copy in known:
        copy.wait()
    here = times[0, 0]
    for d in range(4):
        flags[0, d] = (times[1 + d, 0] == here + 1).astype(jnp.int32)
        flags[0, 4 + d] = (times[1 + d, 0] == here - 1).astype(jnp.int32)
    write_messages(flags, ct_ref, vec, (m0, m1, m2, m3))


def factor(tags, precond, rhs, coupling, diag):
    n, width = rhs.shape
    square = pltpu.VMEM((n, n), BF16)
    column = pltpu.VMEM((n, width), F32)
    outside = pl.BlockSpec(memory_space=pltpu.HBM)
    return pl.pallas_call(
        factor_kernel,
        out_shape=[pltpu.VMEM((n, n), F32), square, square, square, column, column, pltpu.SMEM((1, 8), jnp.int32)]
        + [jax.ShapeDtypeStruct((n, width), BF16)] * 4,
        in_specs=[outside] * 9,
        out_specs=[vmem()] * 6 + [smem()] + [vmem()] * 4,
        scratch_shapes=[
            pltpu.VMEM((LEAF, n), F32),
            pltpu.SMEM((8, 1), jnp.int32),
            pltpu.SemaphoreType.DMA((n // LEAF + 4,)),
            pltpu.SemaphoreType.DMA((5,)),
        ],
        compiler_params=params(20),
    )(*[pinned(x, pltpu.HBM) for x in (*tags, precond, rhs, coupling, diag)])


def build_kernel(work, high_ref, low_ref, size_ref):
    n = work.shape[0]
    blocks = n // LEAF
    at = [pl.ds(k * LEAF, LEAF) for k in range(blocks)]
    inv = {}
    largest = jnp.zeros((1, 1), F32)
    for k in reversed(range(blocks)):
        row = {j: split(work[at[k], at[j]]) for j in range(k + 1, blocks)}
        made = {}
        for j in range(k + 1, blocks):
            made[j] = -sum(mm3(row[m], inv[m, j]) for m in range(k + 1, blocks))
            inv[k, j] = split(made[j])
            flipped = made[j].T
            inv[j, k] = split(flipped)
        made[k] = work[at[k], at[k]] - sum([mm3(row[m], inv[m, k]) for m in range(k + 1, blocks)])
        inv[k, k] = split(made[k])
        for j in range(k, blocks):
            high_ref[at[k], at[j]], low_ref[at[k], at[j]] = inv[k, j]
            if j != k:
                high_ref[at[j], at[k]], low_ref[at[j], at[k]] = inv[j, k]
            largest = jnp.maximum(largest, jnp.max(jnp.max(jnp.abs(made[j]), axis=0, keepdims=True), axis=1, keepdims=True))
    size_ref[...] = jnp.broadcast_to(largest, size_ref.shape)


def build(work, width):
    n = work.shape[0]
    return pl.pallas_call(
        build_kernel,
        out_shape=[pltpu.VMEM((n, n), BF16), pltpu.VMEM((n, n), BF16), pltpu.VMEM((8, width), F32)],
        in_specs=[vmem()],
        out_specs=[vmem()] * 3,
        compiler_params=params(16),
    )(pinned(work))


def store_applied(out_ref, high_ref, low_ref, vec_ref):
    high, low = split(vec_ref[...])
    both = jnp.concatenate([high, low], axis=1)
    width = high.shape[1]
    for k in range(0, out_ref.shape[0], LEAF):
        rows = pl.ds(k, LEAF)
        part = mm(high_ref[rows, :], both)
        out_ref[rows, :] = part[:, :width] + (part[:, width:] + mm(low_ref[rows, :], high))


def relation(flags):
    return [flags[0, d] == 1 for d in range(4)], [flags[0, 4 + d] == 1 for d in range(4)]


def write_messages(flags, ct_ref, vec_ref, out_refs):
    is_next, is_prev = relation(flags)
    high = vec_ref[...].astype(BF16)
    for k in range(0, vec_ref.shape[0], LEAF):
        rows = pl.ds(k, LEAF)
        back = mm(ct_ref[rows, :], high).astype(BF16)
        ahead = high[k:k + LEAF, :]
        for d, out in enumerate(out_refs):
            out[rows, :] = jnp.where(is_next[d], ahead, jnp.where(is_prev[d], back, jnp.zeros_like(back)))


def own_kernel(diag_ref, vec_ref, out_ref):
    both = jnp.concatenate(split(vec_ref[...]), axis=1)
    width = vec_ref.shape[1]
    for k in range(0, out_ref.shape[0], LEAF):
        rows = pl.ds(k, LEAF)
        part = mm(diag_ref[rows, :], both)
        out_ref[rows, :] = part[:, :width] + part[:, width:]


def residual_rows(flags, own_ref, c_ref, got, out_ref):
    is_next, is_prev = relation(flags)
    zero = jnp.zeros(got[0].shape, BF16)
    before = zero
    for d, ref in enumerate(got):
        before = jnp.where(is_prev[d], ref[...], before)
    for k in range(0, out_ref.shape[0], LEAF):
        rows = pl.ds(k, LEAF)
        after = zero[:LEAF]
        for d, ref in enumerate(got):
            after = jnp.where(is_next[d], ref[rows, :], after)
        out_ref[rows, :] = own_ref[rows, :] + mm(c_ref[rows, :], before) + after.astype(F32)


def step_kernel(flags, own_ref, c_ref, ct_ref, high_ref, low_ref, g0, g1, g2, g3, res_ref, vec_ref, *out_refs):
    residual_rows(flags, own_ref, c_ref, (g0, g1, g2, g3), res_ref)
    store_applied(vec_ref, high_ref, low_ref, res_ref)
    write_messages(flags, ct_ref, vec_ref, out_refs)


def pack(rows, out_ref):
    rows = rows + [jnp.zeros_like(rows[0])] * (SLOTS - len(rows))
    packed = jnp.concatenate(rows, axis=0)
    for d in range(0, out_ref.shape[0], SLOTS):
        out_ref[pl.ds(d, SLOTS), :] = packed


def last_kernel(flags, own_ref, c_ref, high_ref, low_ref, size_ref, r0, p0, r1, p1, r2, p2, g0, g1, g2, g3, out_ref, r3, p3):
    residual_rows(flags, own_ref, c_ref, (g0, g1, g2, g3), r3)
    store_applied(p3, high_ref, low_ref, r3)
    res = (r0, r1, r2, r3)
    vec = (p0, p1, p2, p3)
    unit = size_ref[0:1, :]
    sizes = [jnp.maximum(jnp.max(jnp.abs(r[...]), axis=0, keepdims=True), 1e-30) for r in res]
    left_scale = [1.0 / v for v in sizes]
    right_scale = [1.0 / (v * unit) for v in sizes]
    rows = [jnp.zeros_like(unit)] * len(PAIRS)
    for k in range(0, r3.shape[0], LEAF):
        at = pl.ds(k, LEAF)
        left = [res[i][at, :] * left_scale[i] for i in range(BASIS)]
        right = [vec[i][at, :] * right_scale[i] for i in range(BASIS)]
        for m, (i, j) in enumerate(PAIRS):
            rows[m] = rows[m] + jnp.sum(left[i] * right[j], axis=0, keepdims=True)
    pack(rows + sizes + [unit], out_ref)


def merge(in_ref):
    senders = in_ref.shape[0] // SLOTS
    got = [in_ref[pl.ds(m, senders, stride=SLOTS), :] for m in range(len(PAIRS) + BASIS + 1)]
    size_rows, unit_row = got[len(PAIRS):-1], got[-1]
    sizes = [jnp.max(v, axis=0, keepdims=True) for v in size_rows]
    unit = jnp.max(unit_row, axis=0, keepdims=True)
    share = [v / top for v, top in zip(size_rows, sizes)]
    unit_share = unit_row / unit
    rows = []
    for m, (i, j) in enumerate(PAIRS):
        rows.append(jnp.sum(got[m] * (share[i] * share[j] * unit_share), axis=0, keepdims=True))
    return rows, sizes, unit


def merge_kernel(in_ref, out_ref):
    rows, sizes, unit = merge(in_ref)
    pack(rows + sizes + [unit], out_ref)


def recurrence(rows, sizes, unit):
    gram = {}
    for m, (i, j) in enumerate(PAIRS):
        gram[i, j] = gram[j, i] = rows[m]
    lead = sizes[1] / sizes[0]
    grow = [sizes[j + 1] / sizes[j] / lead for j in range(ITERS)]
    zero = jnp.zeros_like(unit)

    def dot(a, b):
        return sum(a[i] * b[j] * gram[i, j] for i in a for j in b)

    def axpy(a, x, y):
        out = {i: a * v for i, v in x.items()}
        for i, v in y.items():
            out[i] = out[i] + v if i in out else v
        return out

    resid_new = {0: jnp.ones_like(unit)}
    resid_old = {}
    beta_now = jnp.sqrt(dot(resid_new, resid_new))
    old_beta = zero
    phi_bar = beta_now
    cosine = -jnp.ones_like(unit)
    sine_now = eps_now = d_bar = zero
    dir_now, dir_old, total = {}, {}, {}
    for step in range(ITERS):
        lanczos = {i: v / beta_now for i, v in resid_new.items()}
        image = {i + 1: v * grow[i] for i, v in lanczos.items()}
        if step > 0:
            image = axpy(-beta_now / old_beta, resid_old, image)
        alpha_now = dot(lanczos, image)
        resid_old = resid_new
        resid_new = axpy(-alpha_now / beta_now, resid_new, image)
        old_beta = beta_now
        beta_now = jnp.sqrt(dot(resid_new, resid_new))
        old_eps = eps_now
        delta_now = cosine * d_bar + sine_now * alpha_now
        g_bar = sine_now * d_bar - cosine * alpha_now
        eps_now = sine_now * beta_now
        d_bar = -cosine * beta_now
        gamma_now = jnp.sqrt(g_bar * g_bar + beta_now * beta_now)
        cosine = g_bar / gamma_now
        sine_now = beta_now / gamma_now
        phi_now = cosine * phi_bar
        phi_bar = sine_now * phi_bar
        dir_next = axpy(-old_eps, dir_old, axpy(-delta_now, dir_now, lanczos))
        dir_next = {i: v / gamma_now for i, v in dir_next.items()}
        dir_old, dir_now = dir_now, dir_next
        total = axpy(phi_now, dir_now, total)
    coefs = [total[i] * (sizes[0] / sizes[i]) / lead for i in range(ITERS)]
    return coefs, phi_bar * sizes[0] * jnp.sqrt(unit)


def finish_kernel(in_ref, p0, p1, p2, out_ref, norm_ref):
    coefs, norm = recurrence(*merge(in_ref))
    norm_ref[...] = norm
    for k in range(0, out_ref.shape[0], LEAF):
        at = pl.ds(k, LEAF)
        out_ref[at, :] = coefs[0] * p0[at, :] + coefs[1] * p1[at, :] + coefs[2] * p2[at, :]


def neighbour_perms(count):
    even = [(i, i ^ 1) for i in range(count)]
    odd = [(i, i + 1) for i in range(1, count - 1, 2)]
    return even, odd + [(j, i) for i, j in odd]


def exchange(values):
    even_r, odd_r = neighbour_perms(lax.axis_size("tr"))
    even_c, odd_c = neighbour_perms(lax.axis_size("tc"))
    return [
        lax.ppermute(values[0], "tr", odd_r),
        lax.ppermute(values[1], "tc", odd_c),
        lax.ppermute(values[2], "tr", even_r),
        lax.ppermute(values[3], "tc", even_c),
    ]


def body(diag_block, coupling, precond, rhs, slot_time):
    n, width = rhs.shape[2:]
    own_tag = slot_time + 1
    tags = [own_tag] + exchange([own_tag] * 4)
    sent = [jax.ShapeDtypeStruct((n, width), BF16)] * 4

    work, c_here, flipped, diag_here, res, vec, flags, *messages = factor(
        tags, precond[0, 0], rhs[0, 0], coupling[0, 0], diag_block[0, 0]
    )
    basis = [res, vec]
    for step in range(ITERS):
        got = exchange(messages)
        if step == 0:
            high, low, size = build(work, width)
        own = pl.pallas_call(
            own_kernel,
            out_shape=pltpu.VMEM((n, width), F32),
            in_specs=[vmem()] * 2,
            out_specs=vmem(),
            compiler_params=params(8),
        )(pinned(diag_here), pinned(vec))
        if step < ITERS - 1:
            out = pl.pallas_call(
                step_kernel,
                out_shape=[pltpu.VMEM((n, width), F32)] * 2 + sent,
                in_specs=[smem()] + [vmem()] * 9,
                out_specs=[vmem()] * 6,
                compiler_params=params(12),
            )(pinned(flags, pltpu.SMEM), pinned(own), pinned(c_here), pinned(flipped), pinned(high), pinned(low), *got)
            vec = out[1]
            basis += [out[0], vec]
            messages = out[2:]
    part = pl.pallas_call(
        last_kernel,
        out_shape=jax.ShapeDtypeStruct((lax.axis_size("tc") * SLOTS, width), F32),
        in_specs=[smem()] + [vmem()] * 15,
        out_specs=vmem(),
        scratch_shapes=[pltpu.VMEM((n, width), F32)] * 2,
        compiler_params=params(12),
    )(pinned(flags, pltpu.SMEM), pinned(own), pinned(c_here), pinned(high), pinned(low), pinned(size), *[pinned(b) for b in basis], *got)
    part = lax.all_to_all(part, "tc", 0, 0, tiled=True)
    part = pl.pallas_call(
        merge_kernel,
        out_shape=jax.ShapeDtypeStruct((lax.axis_size("tr") * SLOTS, width), F32),
        in_specs=[vmem()],
        out_specs=vmem(),
    )(part)
    part = lax.all_to_all(part, "tr", 0, 0, tiled=True)
    solution, norm = pl.pallas_call(
        finish_kernel,
        out_shape=[jax.ShapeDtypeStruct((n, width), F32), jax.ShapeDtypeStruct((1, width), F32)],
        in_specs=[vmem()] * 4,
        out_specs=[vmem()] * 2,
        compiler_params=params(8),
    )(part, pinned(basis[1]), pinned(basis[3]), pinned(basis[5]))
    return (solution[None, None], norm[0])


def solution(mesh):
    placed = (
        P("tr", "tc", None, None),
        P("tr", "tc", None, None),
        P("tr", "tc", None, None),
        P("tr", "tc", None, None),
        P("tr", "tc"),
    )
    return jax.shard_map(
        body,
        mesh=mesh,
        in_specs=placed,
        out_specs=(P("tr", "tc", None, None), P()),
        check_vma=False,
    )
```

```python
import functools

import jax
import jax.numpy as jnp
from jax import lax
from jax.experimental import pallas as pl
from jax.experimental.pallas import tpu as pltpu
from jax.sharding import PartitionSpec as P

ITERS = 3
BASIS = ITERS + 1
PAIRS = tuple((i, j) for i in range(BASIS) for j in range(i, BASIS))
LEAF = 256
ROWS = 256
SLOTS = 16
F32 = jnp.float32
BF16 = jnp.bfloat16
MIB = 2**20


def vmem():
    return pl.BlockSpec(memory_space=pltpu.VMEM)


def smem():
    return pl.BlockSpec(memory_space=pltpu.SMEM)


def outside():
    return pl.BlockSpec(memory_space=pltpu.HBM)


def pinned(x, space=pltpu.VMEM):
    return pltpu.with_memory_space_constraint(x, space)


def params(mib):
    return pltpu.CompilerParams(vmem_limit_bytes=mib * MIB)


def mm(a, b):
    return lax.dot_general(a, b, (((1,), (0,)), ((), ())), preferred_element_type=F32)


def tn(a, b):
    return lax.dot_general(a, b, (((0,), (0,)), ((), ())), preferred_element_type=F32)


def split(x):
    high = x.astype(BF16)
    return high, (x - high.astype(F32)).astype(BF16)


def mm3(a, b):
    return mm(a[0], b[0]) + (mm(a[0], b[1]) + mm(a[1], b[0]))


def tn3(a, b):
    return tn(a[0], b[0]) + (tn(a[0], b[1]) + tn(a[1], b[0]))


def mm_full(a, b):
    return lax.dot_general(a, b, (((1,), (0,)), ((), ())), precision=lax.Precision.HIGHEST)


def tn_full(a, b):
    return lax.dot_general(a, b, (((0,), (0,)), ((), ())), precision=lax.Precision.HIGHEST)


def column_norm(x):
    return jnp.max(jnp.sum(jnp.abs(x), axis=0, keepdims=True), axis=1, keepdims=True)


def pivot_steps(block):
    n = block.shape[0]
    rows = lax.broadcasted_iota(jnp.int32, (n, n), 0)
    cols = lax.broadcasted_iota(jnp.int32, (n, n), 1)
    eye = jnp.where(rows == cols, 1.0, 0.0).astype(F32)
    diag = jnp.where(rows == cols, block, 0.0)
    across = lax.rsqrt(jnp.sum(diag, axis=0, keepdims=True))
    down = lax.rsqrt(jnp.sum(diag, axis=1, keepdims=True))
    scaled = block * down * across
    parts = split(scaled)
    square = mm(parts[0], parts[0])
    yield
    alpha = 1.8 * lax.rsqrt(column_norm(square))
    power = (eye - (2.0 * alpha) * scaled + (alpha * alpha) * square).astype(BF16)
    inv = alpha * (2.0 * eye - alpha * scaled)
    for _ in range(2):
        inv = inv + mm(inv.astype(BF16), power)
        power = mm(power, power).astype(BF16)
        yield
    inv = inv + mm(inv.astype(BF16), power)
    yield
    high = inv.astype(BF16)
    resid = eye - (mm(parts[0], high) + mm(parts[1], high))
    yield
    resid_high = resid.astype(BF16)
    second = mm(resid_high, resid_high)
    yield
    more = split(resid + second)
    inv = high.astype(F32) + (mm(high, more[0]) + mm(high, more[1]))
    error = column_norm(second)
    return inv * down * across, error


def interleave(steps, pending):
    while True:
        try:
            next(steps)
        except StopIteration as stop:
            return stop.value
        if pending:
            pending.pop(0)()


def eliminate(n, work, vec, extra, before, after):
    blocks = n // LEAF
    at = [pl.ds(k * LEAF, LEAF) for k in range(blocks)]
    worst = jnp.zeros((1, 1), F32)
    pending = []
    for k in range(blocks):
        before(k)
        pivot, error = interleave(pivot_steps(work[at[k], at[k]]), pending)
        for task in pending:
            task()
        after(k)
        worst = jnp.maximum(worst, error)
        parts = split(pivot)
        work[at[k], at[k]] = pivot
        old, row = {}, {}

        def scale_row(j, k=k, old=old, row=row, parts=parts):
            old[j] = split(work[at[k], at[j]])
            value = mm3(parts, old[j])
            row[j] = split(value)
            work[at[k], at[j]] = value

        def update(i, j, old=old, row=row):
            work[at[i], at[j]] = work[at[i], at[j]] - tn3(old[i], row[j])

        def push(i, k=k, row=row):
            vec[at[i], :] = vec[at[i], :] - tn3(row[i], split(vec[at[k], :]))

        def solve(k=k, parts=parts):
            vec[at[k], :] = mm3(parts, split(vec[at[k], :]))

        pending = []
        later = range(k + 1, blocks)
        for j in later:
            if j == k + 1:
                scale_row(j)
                update(j, j)
            else:
                pending.append(functools.partial(scale_row, j))
        for i in later:
            for j in range(i, blocks):
                if (i, j) != (k + 1, k + 1):
                    pending.append(functools.partial(update, i, j))
        for i in later:
            pending.append(functools.partial(push, i))
        pending.append(solve)
        pending += extra(k)
    for task in pending:
        task()
    for k in reversed(range(blocks - 1)):
        total = vec[at[k], :]
        for j in range(k + 1, blocks):
            total = total - mm3(split(work[at[k], at[j]]), split(vec[at[j], :]))
        vec[at[k], :] = total
    return worst


def careful_inverse(block):
    n = block.shape[0]
    rows = lax.broadcasted_iota(jnp.int32, (n, n), 0)
    cols = lax.broadcasted_iota(jnp.int32, (n, n), 1)
    eye = jnp.where(rows == cols, 1.0, 0.0).astype(F32)
    diag = jnp.where(rows == cols, block, 0.0)
    across = lax.rsqrt(jnp.sum(diag, axis=0, keepdims=True))
    down = lax.rsqrt(jnp.sum(diag, axis=1, keepdims=True))
    scaled = block * down * across

    def unfinished(carry):
        return jnp.logical_and(carry[2] > 1e-3, carry[0] < 80)

    def refine(carry):
        count, x, _ = carry
        left = eye - mm_full(scaled, x)
        return count + 1, x + mm_full(x, left), jnp.max(column_norm(left))

    start = eye * (1.8 / column_norm(scaled))
    return lax.while_loop(unfinished, refine, (jnp.int32(0), start, jnp.float32(2.0)))[1] * down * across


def eliminate_careful(n, work, vec, row):
    blocks = n // LEAF

    def at(k):
        return pl.ds(pl.multiple_of(k * LEAF, LEAF), LEAF)

    def pivot(k, _):
        work[at(k), at(k)] = careful_inverse(work[at(k), at(k)])

        def scale_row(j, _):
            row[:, at(j)] = mm_full(work[at(k), at(k)], work[at(k), at(j)])
            return 0

        def update_row(i, _):
            def update(j, _):
                work[at(i), at(j)] = work[at(i), at(j)] - tn_full(work[at(k), at(i)], row[:, at(j)])
                return 0

            lax.fori_loop(i, blocks, update, 0)
            vec[at(i), :] = vec[at(i), :] - tn_full(row[:, at(i)], vec[at(k), :])
            return 0

        def keep(j, _):
            work[at(k), at(j)] = row[:, at(j)]
            return 0

        lax.fori_loop(k + 1, blocks, scale_row, 0)
        lax.fori_loop(k + 1, blocks, update_row, 0)
        lax.fori_loop(k + 1, blocks, keep, 0)
        vec[at(k), :] = mm_full(work[at(k), at(k)], vec[at(k), :])
        return 0

    def back(m, _):
        k = blocks - 2 - m

        def subtract(j, _):
            vec[at(k), :] = vec[at(k), :] - mm_full(work[at(k), at(j)], vec[at(j), :])
            return 0

        return lax.fori_loop(k + 1, blocks, subtract, 0)

    lax.fori_loop(0, blocks, pivot, 0)
    lax.fori_loop(0, blocks - 1, back, 0)


def factor_kernel(p_hbm, rhs_hbm, c_hbm, d_hbm, work, c_ref, ct_ref, d_ref, rhs_ref, vec, row, sems):
    n = work.shape[0]
    blocks = n // LEAF
    first = pl.ds(0, LEAF)
    rest = pl.ds(LEAF, n - LEAF)
    spots = [(first, first), (first, rest)] + [(pl.ds(k * LEAF, LEAF), pl.ds(0, n)) for k in range(1, blocks)]
    panels = [pltpu.make_async_copy(p_hbm.at[spot], work.at[spot], sems.at[k]) for k, spot in enumerate(spots)]
    others = [
        pltpu.make_async_copy(src, dst, sems.at[len(spots) + i])
        for i, (src, dst) in enumerate(((rhs_hbm, rhs_ref), (c_hbm, c_ref), (d_hbm, d_ref)))
    ]
    def before(k):
        if k == 0:
            panels[0].start()
            panels[0].wait()
            for copy in panels[1:] + others:
                copy.start()
        elif k == 1:
            others[1].wait()

    def after(k):
        if k == 0:
            for copy in panels[1:]:
                copy.wait()
            others[0].wait()
            vec[...] = rhs_ref[...]

    def flip(k):
        ct_ref[:, pl.ds(k * LEAF, LEAF)] = c_ref[pl.ds(k * LEAF, LEAF), :].T

    def extra(k):
        if k == 0:
            return []
        if k == blocks - 1:
            return []
        span = blocks // 2
        return [functools.partial(flip, j) for j in range((k - 1) * span, k * span)]

    worst = eliminate(n, work, vec, extra, before, after)

    @pl.when(jnp.logical_not(jnp.max(worst) < 4e-3))
    def _():
        for copy in panels:
            copy.start()
        for copy in panels:
            copy.wait()
        vec[...] = rhs_ref[...]
        eliminate_careful(n, work, vec, row)

    others[2].wait()


def factor(precond, rhs, coupling, diag):
    n, width = rhs.shape
    square = pltpu.VMEM((n, n), BF16)
    column = pltpu.VMEM((n, width), F32)
    return pl.pallas_call(
        factor_kernel,
        out_shape=[pltpu.VMEM((n, n), F32), square, square, square, column, column],
        in_specs=[outside()] * 4,
        out_specs=[vmem()] * 6,
        scratch_shapes=[pltpu.VMEM((LEAF, n), F32), pltpu.SemaphoreType.DMA((n // LEAF + 4,))],
        compiler_params=params(20),
    )(*[pinned(x, pltpu.HBM) for x in (precond, rhs, coupling, diag)])


def message_kernel(last, own, t1, t2, t3, ct_ref, vec_ref, flags, m0, m1, m2, m3, back, times, sems):
    known = [pltpu.make_async_copy(t, times.at[pl.ds(d, 1), :], sems.at[d]) for d, t in enumerate((own, t1, t2, t3))]
    for copy in known:
        copy.start()
    high = vec_ref[...].astype(BF16)
    for k in range(0, back.shape[0], ROWS):
        rows = pl.ds(k, ROWS)
        back[rows, :] = mm(ct_ref[rows, :], high).astype(BF16)
    for copy in known:
        copy.wait()
    here = times[0, 0]
    next_left = here < last
    prev_left = here > 1
    for d in range(1, 4):
        is_next = times[d, 0] == here + 1
        is_prev = jnp.logical_and(times[d, 0] == here - 1, here > 1)
        flags[0, d] = is_next.astype(jnp.int32)
        flags[0, 4 + d] = is_prev.astype(jnp.int32)
        next_left = jnp.logical_and(next_left, jnp.logical_not(is_next))
        prev_left = jnp.logical_and(prev_left, jnp.logical_not(is_prev))
    flags[0, 0] = next_left.astype(jnp.int32)
    flags[0, 4] = prev_left.astype(jnp.int32)
    for k in range(0, back.shape[0], ROWS):
        rows = pl.ds(k, ROWS)
        choose_messages(flags, rows, high[k:k + ROWS, :], back[rows, :], (m0, m1, m2, m3))


def first_messages(last, tags, flipped, vec):
    n, width = vec.shape
    return pl.pallas_call(
        functools.partial(message_kernel, last),
        out_shape=[pltpu.SMEM((1, 8), jnp.int32)] + [jax.ShapeDtypeStruct((n, width), BF16)] * 4,
        in_specs=[outside()] * 4 + [vmem()] * 2,
        out_specs=[smem()] + [vmem()] * 4,
        scratch_shapes=[pltpu.VMEM((n, width), BF16), pltpu.SMEM((8, 1), jnp.int32), pltpu.SemaphoreType.DMA((4,))],
        compiler_params=params(8),
    )(*[pinned(t, pltpu.HBM) for t in tags], pinned(flipped), pinned(vec))


def build_kernel(work, high_ref, low_ref, size_ref):
    n = work.shape[0]
    blocks = n // LEAF
    at = [pl.ds(k * LEAF, LEAF) for k in range(blocks)]
    inv = {}
    largest = jnp.zeros((1, 1), F32)
    for k in reversed(range(blocks)):
        row = {j: split(work[at[k], at[j]]) for j in range(k + 1, blocks)}
        made = {}
        for j in range(k + 1, blocks):
            made[j] = -sum(mm3(row[m], inv[m, j]) for m in range(k + 1, blocks))
            inv[k, j] = split(made[j])
            flipped = made[j].T
            inv[j, k] = split(flipped)
        made[k] = work[at[k], at[k]] - sum([mm3(row[m], inv[m, k]) for m in range(k + 1, blocks)])
        inv[k, k] = split(made[k])
        for j in range(k, blocks):
            high_ref[at[k], at[j]], low_ref[at[k], at[j]] = inv[k, j]
            if j != k:
                high_ref[at[j], at[k]], low_ref[at[j], at[k]] = inv[j, k]
            largest = jnp.maximum(largest, jnp.max(jnp.max(jnp.abs(made[j]), axis=0, keepdims=True), axis=1, keepdims=True))
    size_ref[...] = jnp.broadcast_to(largest, size_ref.shape)


def build(work, width):
    n = work.shape[0]
    return pl.pallas_call(
        build_kernel,
        out_shape=[pltpu.VMEM((n, n), BF16), pltpu.VMEM((n, n), BF16), pltpu.VMEM((8, width), F32)],
        in_specs=[vmem()],
        out_specs=[vmem()] * 3,
        compiler_params=params(16),
    )(pinned(work))


def store_applied(out_ref, high_ref, low_ref, vec_ref):
    high, low = split(vec_ref[...])
    both = jnp.concatenate([high, low], axis=1)
    width = high.shape[1]
    for k in range(0, out_ref.shape[0], ROWS):
        rows = pl.ds(k, ROWS)
        part = mm(high_ref[rows, :], both)
        out_ref[rows, :] = part[:, :width] + (part[:, width:] + mm(low_ref[rows, :], high))


def relation(flags):
    return [flags[0, d] == 1 for d in range(4)], [flags[0, 4 + d] == 1 for d in range(4)]


def choose_messages(flags, rows, ahead, back, out_refs):
    is_next, is_prev = relation(flags)
    for d, out in enumerate(out_refs):
        out[rows, :] = jnp.where(is_next[d], ahead, jnp.where(is_prev[d], back, jnp.zeros_like(back)))


def write_messages(flags, ct_ref, vec_ref, out_refs):
    high = vec_ref[...].astype(BF16)
    for k in range(0, vec_ref.shape[0], ROWS):
        rows = pl.ds(k, ROWS)
        back = mm(ct_ref[rows, :], high).astype(BF16)
        choose_messages(flags, rows, high[k:k + ROWS, :], back, out_refs)


def own_kernel(diag_ref, vec_ref, out_ref):
    both = jnp.concatenate(split(vec_ref[...]), axis=1)
    width = vec_ref.shape[1]
    for k in range(0, out_ref.shape[0], ROWS):
        rows = pl.ds(k, ROWS)
        part = mm(diag_ref[rows, :], both)
        out_ref[rows, :] = part[:, :width] + part[:, width:]


def residual_rows(flags, own_ref, c_ref, got, out_ref):
    is_next, is_prev = relation(flags)
    zero = jnp.zeros(got[0].shape, BF16)
    before = zero
    for d, ref in enumerate(got):
        before = jnp.where(is_prev[d], ref[...], before)
    for k in range(0, out_ref.shape[0], ROWS):
        rows = pl.ds(k, ROWS)
        after = zero[:ROWS]
        for d, ref in enumerate(got):
            after = jnp.where(is_next[d], ref[rows, :], after)
        out_ref[rows, :] = own_ref[rows, :] + mm(c_ref[rows, :], before) + after.astype(F32)


def step_kernel(flags, own_ref, c_ref, ct_ref, high_ref, low_ref, g0, g1, g2, g3, res_ref, vec_ref, *out_refs):
    residual_rows(flags, own_ref, c_ref, (g0, g1, g2, g3), res_ref)
    store_applied(vec_ref, high_ref, low_ref, res_ref)
    write_messages(flags, ct_ref, vec_ref, out_refs)


def pack(rows, out_ref):
    rows = rows + [jnp.zeros_like(rows[0])] * (SLOTS - len(rows))
    packed = jnp.concatenate(rows, axis=0)
    for d in range(0, out_ref.shape[0], SLOTS):
        out_ref[pl.ds(d, SLOTS), :] = packed


def last_kernel(flags, own_ref, c_ref, high_ref, low_ref, size_ref, r0, p0, r1, p1, r2, p2, g0, g1, g2, g3, out_ref, r3, p3):
    residual_rows(flags, own_ref, c_ref, (g0, g1, g2, g3), r3)
    store_applied(p3, high_ref, low_ref, r3)
    res = (r0, r1, r2, r3)
    vec = (p0, p1, p2, p3)
    unit = size_ref[0:1, :]
    sizes = [jnp.maximum(jnp.max(jnp.abs(r[...]), axis=0, keepdims=True), 1e-30) for r in res]
    left_scale = [1.0 / v for v in sizes]
    right_scale = [1.0 / (v * unit) for v in sizes]
    rows = [jnp.zeros_like(unit)] * len(PAIRS)
    for k in range(0, r3.shape[0], LEAF):
        at = pl.ds(k, LEAF)
        left = [res[i][at, :] * left_scale[i] for i in range(BASIS)]
        right = [vec[i][at, :] * right_scale[i] for i in range(BASIS)]
        for m, (i, j) in enumerate(PAIRS):
            rows[m] = rows[m] + jnp.sum(left[i] * right[j], axis=0, keepdims=True)
    pack(rows + sizes + [unit], out_ref)


def merge(in_ref):
    senders = in_ref.shape[0] // SLOTS
    got = [in_ref[pl.ds(m, senders, stride=SLOTS), :] for m in range(len(PAIRS) + BASIS + 1)]
    size_rows, unit_row = got[len(PAIRS):-1], got[-1]
    sizes = [jnp.max(v, axis=0, keepdims=True) for v in size_rows]
    unit = jnp.max(unit_row, axis=0, keepdims=True)
    share = [v / top for v, top in zip(size_rows, sizes)]
    unit_share = unit_row / unit
    rows = []
    for m, (i, j) in enumerate(PAIRS):
        rows.append(jnp.sum(got[m] * (share[i] * share[j] * unit_share), axis=0, keepdims=True))
    return rows, sizes, unit


def merge_kernel(in_ref, out_ref):
    rows, sizes, unit = merge(in_ref)
    pack(rows + sizes + [unit], out_ref)


def recurrence(rows, sizes, unit):
    gram = {}
    for m, (i, j) in enumerate(PAIRS):
        gram[i, j] = gram[j, i] = rows[m]
    lead = sizes[1] / sizes[0]
    grow = [sizes[j + 1] / sizes[j] / lead for j in range(ITERS)]
    zero = jnp.zeros_like(unit)

    def dot(a, b):
        return sum(a[i] * b[j] * gram[i, j] for i in a for j in b)

    def axpy(a, x, y):
        out = {i: a * v for i, v in x.items()}
        for i, v in y.items():
            out[i] = out[i] + v if i in out else v
        return out

    resid_new = {0: jnp.ones_like(unit)}
    resid_old = {}
    beta_now = jnp.sqrt(dot(resid_new, resid_new))
    old_beta = zero
    phi_bar = beta_now
    cosine = -jnp.ones_like(unit)
    sine_now = eps_now = d_bar = zero
    dir_now, dir_old, total = {}, {}, {}
    for step in range(ITERS):
        lanczos = {i: v / beta_now for i, v in resid_new.items()}
        image = {i + 1: v * grow[i] for i, v in lanczos.items()}
        if step > 0:
            image = axpy(-beta_now / old_beta, resid_old, image)
        alpha_now = dot(lanczos, image)
        resid_old = resid_new
        resid_new = axpy(-alpha_now / beta_now, resid_new, image)
        old_beta = beta_now
        beta_now = jnp.sqrt(dot(resid_new, resid_new))
        old_eps = eps_now
        delta_now = cosine * d_bar + sine_now * alpha_now
        g_bar = sine_now * d_bar - cosine * alpha_now
        eps_now = sine_now * beta_now
        d_bar = -cosine * beta_now
        gamma_now = jnp.sqrt(g_bar * g_bar + beta_now * beta_now)
        cosine = g_bar / gamma_now
        sine_now = beta_now / gamma_now
        phi_now = cosine * phi_bar
        phi_bar = sine_now * phi_bar
        dir_next = axpy(-old_eps, dir_old, axpy(-delta_now, dir_now, lanczos))
        dir_next = {i: v / gamma_now for i, v in dir_next.items()}
        dir_old, dir_now = dir_now, dir_next
        total = axpy(phi_now, dir_now, total)
    coefs = [total[i] * (sizes[0] / sizes[i]) / lead for i in range(ITERS)]
    return coefs, phi_bar * sizes[0] * jnp.sqrt(unit)


def finish_kernel(in_ref, p0, p1, p2, out_ref, norm_ref):
    coefs, norm = recurrence(*merge(in_ref))
    norm_ref[...] = norm
    for k in range(0, out_ref.shape[0], LEAF):
        at = pl.ds(k, LEAF)
        out_ref[at, :] = coefs[0] * p0[at, :] + coefs[1] * p1[at, :] + coefs[2] * p2[at, :]


def neighbour_perms(count):
    even = [(i, i ^ 1) for i in range(count)]
    odd = [(i, i + 1) for i in range(1, count - 1, 2)]
    return even, odd + [(j, i) for i, j in odd]


def exchange(values):
    even_r, odd_r = neighbour_perms(lax.axis_size("tr"))
    even_c, odd_c = neighbour_perms(lax.axis_size("tc"))
    routes = (("tr", odd_r), ("tc", odd_c), ("tr", even_r), ("tc", even_c))
    return [None if v is None else lax.ppermute(v, *route) for v, route in zip(values, routes)]


def body(diag_block, coupling, precond, rhs, slot_time):
    n, width = rhs.shape[2:]
    own_tag = slot_time + 1
    tags = [own_tag] + exchange([None] + [own_tag] * 3)[1:]
    last = lax.axis_size("tr") * lax.axis_size("tc")
    sent = [jax.ShapeDtypeStruct((n, width), BF16)] * 4

    work, c_here, flipped, diag_here, res, vec = factor(precond[0, 0], rhs[0, 0], coupling[0, 0], diag_block[0, 0])
    flags, *messages = first_messages(last, tags, flipped, vec)
    basis = [res, vec]
    for step in range(ITERS):
        got = exchange(messages)
        if step == 0:
            high, low, size = build(work, width)
        own = pl.pallas_call(
            own_kernel,
            out_shape=pltpu.VMEM((n, width), F32),
            in_specs=[vmem()] * 2,
            out_specs=vmem(),
            compiler_params=params(8),
        )(pinned(diag_here), pinned(vec))
        if step < ITERS - 1:
            out = pl.pallas_call(
                step_kernel,
                out_shape=[pltpu.VMEM((n, width), F32)] * 2 + sent,
                in_specs=[smem()] + [vmem()] * 9,
                out_specs=[vmem()] * 6,
                compiler_params=params(12),
            )(pinned(flags, pltpu.SMEM), pinned(own), pinned(c_here), pinned(flipped), pinned(high), pinned(low), *got)
            vec = out[1]
            basis += [out[0], vec]
            messages = out[2:]
    part = pl.pallas_call(
        last_kernel,
        out_shape=pltpu.VMEM((lax.axis_size("tc") * SLOTS, width), F32),
        in_specs=[smem()] + [vmem()] * 15,
        out_specs=vmem(),
        scratch_shapes=[pltpu.VMEM((n, width), F32)] * 2,
        compiler_params=params(12),
    )(pinned(flags, pltpu.SMEM), pinned(own), pinned(c_here), pinned(high), pinned(low), pinned(size), *[pinned(b) for b in basis], *got)
    part = lax.all_to_all(part, "tc", 0, 0, tiled=True)
    part = pl.pallas_call(
        merge_kernel,
        out_shape=pltpu.VMEM((lax.axis_size("tr") * SLOTS, width), F32),
        in_specs=[vmem()],
        out_specs=vmem(),
    )(pinned(part))
    part = lax.all_to_all(part, "tr", 0, 0, tiled=True)
    solution, norm = pl.pallas_call(
        finish_kernel,
        out_shape=[jax.ShapeDtypeStruct((n, width), F32), jax.ShapeDtypeStruct((1, width), F32)],
        in_specs=[vmem()] * 4,
        out_specs=[vmem()] * 2,
        compiler_params=params(8),
    )(pinned(part), pinned(basis[1]), pinned(basis[3]), pinned(basis[5]))
    return (solution[None, None], norm[0])


def solution(mesh):
    placed = (
        P("tr", "tc", None, None),
        P("tr", "tc", None, None),
        P("tr", "tc", None, None),
        P("tr", "tc", None, None),
        P("tr", "tc"),
    )
    return jax.shard_map(
        body,
        mesh=mesh,
        in_specs=placed,
        out_specs=(P("tr", "tc", None, None), P()),
        check_vma=False,
    )
```

```python
import functools

import jax
import jax.numpy as jnp
from jax import lax
from jax.experimental import pallas as pl
from jax.experimental.pallas import tpu as pltpu
from jax.sharding import PartitionSpec as P

ITERS = 3
BASIS = ITERS + 1
PAIRS = tuple((i, j) for i in range(BASIS) for j in range(i, BASIS))
LEAF = 256
ROWS = 256
SLOTS = 16
F32 = jnp.float32
BF16 = jnp.bfloat16
MIB = 2**20


def vmem():
    return pl.BlockSpec(memory_space=pltpu.VMEM)


def smem():
    return pl.BlockSpec(memory_space=pltpu.SMEM)


def outside():
    return pl.BlockSpec(memory_space=pltpu.HBM)


def pinned(x, space=pltpu.VMEM):
    return pltpu.with_memory_space_constraint(x, space)


def params(mib):
    return pltpu.CompilerParams(vmem_limit_bytes=mib * MIB)


def mm(a, b):
    return lax.dot_general(a, b, (((1,), (0,)), ((), ())), preferred_element_type=F32)


def tn(a, b):
    return lax.dot_general(a, b, (((0,), (0,)), ((), ())), preferred_element_type=F32)


def split(x):
    high = x.astype(BF16)
    return high, (x - high.astype(F32)).astype(BF16)


def mm3(a, b):
    return mm(a[0], b[0]) + (mm(a[0], b[1]) + mm(a[1], b[0]))


def tn3(a, b):
    return tn(a[0], b[0]) + (tn(a[0], b[1]) + tn(a[1], b[0]))


def mm_full(a, b):
    return lax.dot_general(a, b, (((1,), (0,)), ((), ())), precision=lax.Precision.HIGHEST)


def tn_full(a, b):
    return lax.dot_general(a, b, (((0,), (0,)), ((), ())), precision=lax.Precision.HIGHEST)


def column_norm(x):
    return jnp.max(jnp.sum(jnp.abs(x), axis=0, keepdims=True), axis=1, keepdims=True)


def pivot_steps(block):
    n = block.shape[0]
    rows = lax.broadcasted_iota(jnp.int32, (n, n), 0)
    cols = lax.broadcasted_iota(jnp.int32, (n, n), 1)
    eye = jnp.where(rows == cols, 1.0, 0.0).astype(F32)
    diag = jnp.where(rows == cols, block, 0.0)
    across = lax.rsqrt(jnp.sum(diag, axis=0, keepdims=True))
    down = lax.rsqrt(jnp.sum(diag, axis=1, keepdims=True))
    scaled = block * down * across
    parts = split(scaled)
    square = mm(parts[0], parts[0])
    yield
    alpha = 1.8 * lax.rsqrt(column_norm(square))
    power = (eye - (2.0 * alpha) * scaled + (alpha * alpha) * square).astype(BF16)
    inv = alpha * (2.0 * eye - alpha * scaled)
    for _ in range(2):
        inv = inv + mm(inv.astype(BF16), power)
        power = mm(power, power).astype(BF16)
        yield
    inv = inv + mm(inv.astype(BF16), power)
    yield
    high = inv.astype(BF16)
    resid = eye - (mm(parts[0], high) + mm(parts[1], high))
    yield
    resid_high = resid.astype(BF16)
    second = mm(resid_high, resid_high)
    yield
    more = split(resid + second)
    inv = high.astype(F32) + (mm(high, more[0]) + mm(high, more[1]))
    error = column_norm(second)
    return inv * down * across, error


def interleave(steps, pending):
    while True:
        try:
            next(steps)
        except StopIteration as stop:
            return stop.value
        if pending:
            pending.pop(0)()


def eliminate(n, work, vec, extra, before, after):
    blocks = n // LEAF
    at = [pl.ds(k * LEAF, LEAF) for k in range(blocks)]
    worst = jnp.zeros((1, 1), F32)
    pending = []
    for k in range(blocks):
        before(k)
        pivot, error = interleave(pivot_steps(work[at[k], at[k]]), pending)
        for task in pending:
            task()
        after(k)
        worst = jnp.maximum(worst, error)
        parts = split(pivot)
        work[at[k], at[k]] = pivot
        old, row = {}, {}

        def scale_row(j, k=k, old=old, row=row, parts=parts):
            old[j] = split(work[at[k], at[j]])
            value = mm3(parts, old[j])
            row[j] = split(value)
            work[at[k], at[j]] = value

        def update(i, j, old=old, row=row):
            work[at[i], at[j]] = work[at[i], at[j]] - tn3(old[i], row[j])

        def push(i, k=k, row=row):
            vec[at[i], :] = vec[at[i], :] - tn3(row[i], split(vec[at[k], :]))

        def solve(k=k, parts=parts):
            vec[at[k], :] = mm3(parts, split(vec[at[k], :]))

        pending = []
        later = range(k + 1, blocks)
        for j in later:
            if j == k + 1:
                scale_row(j)
                update(j, j)
            else:
                pending.append(functools.partial(scale_row, j))
        for i in later:
            for j in range(i, blocks):
                if (i, j) != (k + 1, k + 1):
                    pending.append(functools.partial(update, i, j))
        for i in later:
            pending.append(functools.partial(push, i))
        pending.append(solve)
        pending += extra(k)
    for task in pending:
        task()
    for k in reversed(range(blocks - 1)):
        total = vec[at[k], :]
        for j in range(k + 1, blocks):
            total = total - mm3(split(work[at[k], at[j]]), split(vec[at[j], :]))
        vec[at[k], :] = total
    return worst


def careful_inverse(block):
    n = block.shape[0]
    rows = lax.broadcasted_iota(jnp.int32, (n, n), 0)
    cols = lax.broadcasted_iota(jnp.int32, (n, n), 1)
    eye = jnp.where(rows == cols, 1.0, 0.0).astype(F32)
    diag = jnp.where(rows == cols, block, 0.0)
    across = lax.rsqrt(jnp.sum(diag, axis=0, keepdims=True))
    down = lax.rsqrt(jnp.sum(diag, axis=1, keepdims=True))
    scaled = block * down * across

    def unfinished(carry):
        return jnp.logical_and(carry[2] > 1e-3, carry[0] < 80)

    def refine(carry):
        count, x, _ = carry
        left = eye - mm_full(scaled, x)
        return count + 1, x + mm_full(x, left), jnp.max(column_norm(left))

    start = eye * (1.8 / column_norm(scaled))
    return lax.while_loop(unfinished, refine, (jnp.int32(0), start, jnp.float32(2.0)))[1] * down * across


def eliminate_careful(n, work, vec, row):
    blocks = n // LEAF

    def at(k):
        return pl.ds(pl.multiple_of(k * LEAF, LEAF), LEAF)

    def pivot(k, _):
        work[at(k), at(k)] = careful_inverse(work[at(k), at(k)])

        def scale_row(j, _):
            row[:, at(j)] = mm_full(work[at(k), at(k)], work[at(k), at(j)])
            return 0

        def update_row(i, _):
            def update(j, _):
                work[at(i), at(j)] = work[at(i), at(j)] - tn_full(work[at(k), at(i)], row[:, at(j)])
                return 0

            lax.fori_loop(i, blocks, update, 0)
            vec[at(i), :] = vec[at(i), :] - tn_full(row[:, at(i)], vec[at(k), :])
            return 0

        def keep(j, _):
            work[at(k), at(j)] = row[:, at(j)]
            return 0

        lax.fori_loop(k + 1, blocks, scale_row, 0)
        lax.fori_loop(k + 1, blocks, update_row, 0)
        lax.fori_loop(k + 1, blocks, keep, 0)
        vec[at(k), :] = mm_full(work[at(k), at(k)], vec[at(k), :])
        return 0

    def back(m, _):
        k = blocks - 2 - m

        def subtract(j, _):
            vec[at(k), :] = vec[at(k), :] - mm_full(work[at(k), at(j)], vec[at(j), :])
            return 0

        return lax.fori_loop(k + 1, blocks, subtract, 0)

    lax.fori_loop(0, blocks, pivot, 0)
    lax.fori_loop(0, blocks - 1, back, 0)


def factor_kernel(time, p_hbm, rhs_hbm, c_hbm, d_hbm, work, c_ref, ct_ref, d_ref, rhs_ref, vec, tag, row, sems):
    n = work.shape[0]
    blocks = n // LEAF
    first = pl.ds(0, LEAF)
    rest = pl.ds(LEAF, n - LEAF)
    spots = [(first, first), (first, rest)] + [(pl.ds(k * LEAF, LEAF), pl.ds(0, n)) for k in range(1, blocks)]
    panels = [pltpu.make_async_copy(p_hbm.at[spot], work.at[spot], sems.at[k]) for k, spot in enumerate(spots)]
    others = [
        pltpu.make_async_copy(src, dst, sems.at[len(spots) + i])
        for i, (src, dst) in enumerate(((rhs_hbm, rhs_ref), (c_hbm, c_ref), (d_hbm, d_ref)))
    ]
    def before(k):
        if k == 0:
            panels[0].start()
            panels[0].wait()
            for copy in panels[1:] + others:
                copy.start()
        elif k == 1:
            others[1].wait()

    def after(k):
        if k == 0:
            for copy in panels[1:]:
                copy.wait()
            others[0].wait()
            vec[...] = rhs_ref[...]

    def flip(k):
        ct_ref[:, pl.ds(k * LEAF, LEAF)] = c_ref[pl.ds(k * LEAF, LEAF), :].T

    def extra(k):
        if k == 0:
            return []
        if k == blocks - 1:
            return []
        span = blocks // 2
        return [functools.partial(flip, j) for j in range((k - 1) * span, k * span)]

    worst = eliminate(n, work, vec, extra, before, after)

    @pl.when(jnp.logical_not(jnp.max(worst) < 4e-3))
    def _():
        for copy in panels:
            copy.start()
        for copy in panels:
            copy.wait()
        vec[...] = rhs_ref[...]
        eliminate_careful(n, work, vec, row)

    others[2].wait()
    tag[...] = jnp.full(tag.shape, time[0, 0] + 1, jnp.int32)


def factor(precond, rhs, coupling, diag, time):
    n, width = rhs.shape
    square = pltpu.VMEM((n, n), BF16)
    column = pltpu.VMEM((n, width), F32)
    return pl.pallas_call(
        factor_kernel,
        out_shape=[pltpu.VMEM((n, n), F32), square, square, square, column, column, jax.ShapeDtypeStruct(time.shape, jnp.int32)],
        in_specs=[smem()] + [outside()] * 4,
        out_specs=[vmem()] * 7,
        scratch_shapes=[pltpu.VMEM((LEAF, n), F32), pltpu.SemaphoreType.DMA((n // LEAF + 4,))],
        compiler_params=params(20),
    )(time, *[pinned(x, pltpu.HBM) for x in (precond, rhs, coupling, diag)])


def back_kernel(ct_ref, vec_ref, ahead, back):
    high = vec_ref[...].astype(BF16)
    ahead[...] = high
    for k in range(0, back.shape[0], ROWS):
        rows = pl.ds(k, ROWS)
        back[rows, :] = mm(ct_ref[rows, :], high).astype(BF16)


def message_kernel(last, own, t1, t2, t3, ahead, back, flags, m0, m1, m2, m3):
    here, *times = [jnp.max(t[...]) for t in (own, t1, t2, t3)]
    next_left = here < last
    prev_left = here > 1
    for d, time in enumerate(times, 1):
        is_next = time == here + 1
        is_prev = jnp.logical_and(time == here - 1, here > 1)
        flags[0, d] = is_next.astype(jnp.int32)
        flags[0, 4 + d] = is_prev.astype(jnp.int32)
        next_left = jnp.logical_and(next_left, jnp.logical_not(is_next))
        prev_left = jnp.logical_and(prev_left, jnp.logical_not(is_prev))
    flags[0, 0] = next_left.astype(jnp.int32)
    flags[0, 4] = prev_left.astype(jnp.int32)
    for k in range(0, back.shape[0], ROWS):
        rows = pl.ds(k, ROWS)
        choose_messages(flags, rows, ahead[rows, :], back[rows, :], (m0, m1, m2, m3))


def first_messages(last, tags, flipped, vec):
    n, width = vec.shape
    parts = pl.pallas_call(
        back_kernel,
        out_shape=[pltpu.VMEM((n, width), BF16)] * 2,
        in_specs=[vmem()] * 2,
        out_specs=[vmem()] * 2,
        compiler_params=params(8),
    )(pinned(flipped), pinned(vec))
    return pl.pallas_call(
        functools.partial(message_kernel, last),
        out_shape=[pltpu.SMEM((1, 8), jnp.int32)] + [jax.ShapeDtypeStruct((n, width), BF16)] * 4,
        in_specs=[vmem()] * 6,
        out_specs=[smem()] + [vmem()] * 4,
        compiler_params=params(8),
    )(*[pinned(t) for t in tags], *[pinned(p) for p in parts])


def build_kernel(work, high_ref, low_ref, size_ref):
    n = work.shape[0]
    blocks = n // LEAF
    at = [pl.ds(k * LEAF, LEAF) for k in range(blocks)]
    inv = {}
    largest = jnp.zeros((1, 1), F32)
    for k in reversed(range(blocks)):
        row = {j: split(work[at[k], at[j]]) for j in range(k + 1, blocks)}
        made = {}
        for j in range(k + 1, blocks):
            made[j] = -sum(mm3(row[m], inv[m, j]) for m in range(k + 1, blocks))
            inv[k, j] = split(made[j])
            flipped = made[j].T
            inv[j, k] = split(flipped)
        made[k] = work[at[k], at[k]] - sum([mm3(row[m], inv[m, k]) for m in range(k + 1, blocks)])
        inv[k, k] = split(made[k])
        for j in range(k, blocks):
            high_ref[at[k], at[j]], low_ref[at[k], at[j]] = inv[k, j]
            if j != k:
                high_ref[at[j], at[k]], low_ref[at[j], at[k]] = inv[j, k]
            largest = jnp.maximum(largest, jnp.max(jnp.max(jnp.abs(made[j]), axis=0, keepdims=True), axis=1, keepdims=True))
    size_ref[...] = jnp.broadcast_to(largest, size_ref.shape)


def build(work, width):
    n = work.shape[0]
    return pl.pallas_call(
        build_kernel,
        out_shape=[pltpu.VMEM((n, n), BF16), pltpu.VMEM((n, n), BF16), pltpu.VMEM((8, width), F32)],
        in_specs=[vmem()],
        out_specs=[vmem()] * 3,
        compiler_params=params(16),
    )(pinned(work))


def store_applied(out_ref, high_ref, low_ref, vec_ref):
    high, low = split(vec_ref[...])
    both = jnp.concatenate([high, low], axis=1)
    width = high.shape[1]
    for k in range(0, out_ref.shape[0], ROWS):
        rows = pl.ds(k, ROWS)
        part = mm(high_ref[rows, :], both)
        out_ref[rows, :] = part[:, :width] + (part[:, width:] + mm(low_ref[rows, :], high))


def relation(flags):
    return [flags[0, d] == 1 for d in range(4)], [flags[0, 4 + d] == 1 for d in range(4)]


def choose_messages(flags, rows, ahead, back, out_refs):
    is_next, is_prev = relation(flags)
    for d, out in enumerate(out_refs):
        out[rows, :] = jnp.where(is_next[d], ahead, jnp.where(is_prev[d], back, jnp.zeros_like(back)))


def write_messages(flags, ct_ref, vec_ref, out_refs):
    high = vec_ref[...].astype(BF16)
    for k in range(0, vec_ref.shape[0], ROWS):
        rows = pl.ds(k, ROWS)
        back = mm(ct_ref[rows, :], high).astype(BF16)
        choose_messages(flags, rows, high[k:k + ROWS, :], back, out_refs)


def own_kernel(diag_ref, vec_ref, out_ref):
    both = jnp.concatenate(split(vec_ref[...]), axis=1)
    width = vec_ref.shape[1]
    for k in range(0, out_ref.shape[0], ROWS):
        rows = pl.ds(k, ROWS)
        part = mm(diag_ref[rows, :], both)
        out_ref[rows, :] = part[:, :width] + part[:, width:]


def residual_rows(flags, own_ref, c_ref, got, out_ref):
    is_next, is_prev = relation(flags)
    zero = jnp.zeros(got[0].shape, BF16)
    before = zero
    for d, ref in enumerate(got):
        before = jnp.where(is_prev[d], ref[...], before)
    for k in range(0, out_ref.shape[0], ROWS):
        rows = pl.ds(k, ROWS)
        after = zero[:ROWS]
        for d, ref in enumerate(got):
            after = jnp.where(is_next[d], ref[rows, :], after)
        out_ref[rows, :] = own_ref[rows, :] + mm(c_ref[rows, :], before) + after.astype(F32)


def step_kernel(flags, own_ref, c_ref, ct_ref, high_ref, low_ref, g0, g1, g2, g3, res_ref, vec_ref, *out_refs):
    residual_rows(flags, own_ref, c_ref, (g0, g1, g2, g3), res_ref)
    store_applied(vec_ref, high_ref, low_ref, res_ref)
    write_messages(flags, ct_ref, vec_ref, out_refs)


def pack(rows, out_ref):
    rows = rows + [jnp.zeros_like(rows[0])] * (SLOTS - len(rows))
    packed = jnp.concatenate(rows, axis=0)
    for d in range(0, out_ref.shape[0], SLOTS):
        out_ref[pl.ds(d, SLOTS), :] = packed


def last_kernel(flags, own_ref, c_ref, high_ref, low_ref, size_ref, r0, p0, r1, p1, r2, p2, g0, g1, g2, g3, out_ref, r3, p3):
    residual_rows(flags, own_ref, c_ref, (g0, g1, g2, g3), r3)
    store_applied(p3, high_ref, low_ref, r3)
    res = (r0, r1, r2, r3)
    vec = (p0, p1, p2, p3)
    unit = size_ref[0:1, :]
    sizes = [jnp.maximum(jnp.max(jnp.abs(r[...]), axis=0, keepdims=True), 1e-30) for r in res]
    left_scale = [1.0 / v for v in sizes]
    right_scale = [1.0 / (v * unit) for v in sizes]
    rows = [jnp.zeros_like(unit)] * len(PAIRS)
    for k in range(0, r3.shape[0], LEAF):
        at = pl.ds(k, LEAF)
        left = [res[i][at, :] * left_scale[i] for i in range(BASIS)]
        right = [vec[i][at, :] * right_scale[i] for i in range(BASIS)]
        for m, (i, j) in enumerate(PAIRS):
            rows[m] = rows[m] + jnp.sum(left[i] * right[j], axis=0, keepdims=True)
    pack(rows + sizes + [unit], out_ref)


def merge(in_ref):
    senders = in_ref.shape[0] // SLOTS
    got = [in_ref[pl.ds(m, senders, stride=SLOTS), :] for m in range(len(PAIRS) + BASIS + 1)]
    size_rows, unit_row = got[len(PAIRS):-1], got[-1]
    sizes = [jnp.max(v, axis=0, keepdims=True) for v in size_rows]
    unit = jnp.max(unit_row, axis=0, keepdims=True)
    share = [v / top for v, top in zip(size_rows, sizes)]
    unit_share = unit_row / unit
    rows = []
    for m, (i, j) in enumerate(PAIRS):
        rows.append(jnp.sum(got[m] * (share[i] * share[j] * unit_share), axis=0, keepdims=True))
    return rows, sizes, unit


def merge_kernel(in_ref, out_ref):
    rows, sizes, unit = merge(in_ref)
    pack(rows + sizes + [unit], out_ref)


def recurrence(rows, sizes, unit):
    gram = {}
    for m, (i, j) in enumerate(PAIRS):
        gram[i, j] = gram[j, i] = rows[m]
    lead = sizes[1] / sizes[0]
    grow = [sizes[j + 1] / sizes[j] / lead for j in range(ITERS)]
    zero = jnp.zeros_like(unit)

    def dot(a, b):
        return sum(a[i] * b[j] * gram[i, j] for i in a for j in b)

    def axpy(a, x, y):
        out = {i: a * v for i, v in x.items()}
        for i, v in y.items():
            out[i] = out[i] + v if i in out else v
        return out

    resid_new = {0: jnp.ones_like(unit)}
    resid_old = {}
    beta_now = jnp.sqrt(dot(resid_new, resid_new))
    old_beta = zero
    phi_bar = beta_now
    cosine = -jnp.ones_like(unit)
    sine_now = eps_now = d_bar = zero
    dir_now, dir_old, total = {}, {}, {}
    for step in range(ITERS):
        lanczos = {i: v / beta_now for i, v in resid_new.items()}
        image = {i + 1: v * grow[i] for i, v in lanczos.items()}
        if step > 0:
            image = axpy(-beta_now / old_beta, resid_old, image)
        alpha_now = dot(lanczos, image)
        resid_old = resid_new
        resid_new = axpy(-alpha_now / beta_now, resid_new, image)
        old_beta = beta_now
        beta_now = jnp.sqrt(dot(resid_new, resid_new))
        old_eps = eps_now
        delta_now = cosine * d_bar + sine_now * alpha_now
        g_bar = sine_now * d_bar - cosine * alpha_now
        eps_now = sine_now * beta_now
        d_bar = -cosine * beta_now
        gamma_now = jnp.sqrt(g_bar * g_bar + beta_now * beta_now)
        cosine = g_bar / gamma_now
        sine_now = beta_now / gamma_now
        phi_now = cosine * phi_bar
        phi_bar = sine_now * phi_bar
        dir_next = axpy(-old_eps, dir_old, axpy(-delta_now, dir_now, lanczos))
        dir_next = {i: v / gamma_now for i, v in dir_next.items()}
        dir_old, dir_now = dir_now, dir_next
        total = axpy(phi_now, dir_now, total)
    coefs = [total[i] * (sizes[0] / sizes[i]) / lead for i in range(ITERS)]
    return coefs, phi_bar * sizes[0] * jnp.sqrt(unit)


def finish_kernel(in_ref, p0, p1, p2, out_ref, norm_ref):
    coefs, norm = recurrence(*merge(in_ref))
    norm_ref[...] = norm
    for k in range(0, out_ref.shape[0], LEAF):
        at = pl.ds(k, LEAF)
        out_ref[at, :] = coefs[0] * p0[at, :] + coefs[1] * p1[at, :] + coefs[2] * p2[at, :]


def neighbour_perms(count):
    even = [(i, i ^ 1) for i in range(count)]
    odd = [(i, i + 1) for i in range(1, count - 1, 2)]
    return even, odd + [(j, i) for i, j in odd]


def exchange(values):
    even_r, odd_r = neighbour_perms(lax.axis_size("tr"))
    even_c, odd_c = neighbour_perms(lax.axis_size("tc"))
    routes = (("tr", odd_r), ("tc", odd_c), ("tr", even_r), ("tc", even_c))
    return [None if v is None else lax.ppermute(v, *route) for v, route in zip(values, routes)]


def reduce_groups():
    rows, cols = lax.axis_size("tr"), lax.axis_size("tc")
    deep = rows // 2

    def rank(h, z, q, c):
        return (h * deep + z) * cols + q * 2 + c

    lines = [[rank(h, z, q, c) for z in range(deep) for c in range(2)] for h in range(2) for q in range(cols // 2)]
    planes = [[rank(h, z, q, c) for h in range(2) for q in range(cols // 2)] for z in range(deep) for c in range(2)]
    return lines, planes


def body(diag_block, coupling, precond, rhs, slot_time):
    n, width = rhs.shape[2:]
    last = lax.axis_size("tr") * lax.axis_size("tc")
    sent = [jax.ShapeDtypeStruct((n, width), BF16)] * 4

    work, c_here, flipped, diag_here, res, vec, own_tag = factor(
        precond[0, 0], rhs[0, 0], coupling[0, 0], diag_block[0, 0], slot_time
    )
    tags = [own_tag] + exchange([None] + [own_tag] * 3)[1:]
    flags, *messages = first_messages(last, tags, flipped, vec)
    basis = [res, vec]
    for step in range(ITERS):
        got = exchange(messages)
        if step == 0:
            high, low, size = build(work, width)
        own = pl.pallas_call(
            own_kernel,
            out_shape=pltpu.VMEM((n, width), F32),
            in_specs=[vmem()] * 2,
            out_specs=vmem(),
            compiler_params=params(8),
        )(pinned(diag_here), pinned(vec))
        if step < ITERS - 1:
            out = pl.pallas_call(
                step_kernel,
                out_shape=[pltpu.VMEM((n, width), F32)] * 2 + sent,
                in_specs=[smem()] + [vmem()] * 9,
                out_specs=[vmem()] * 6,
                compiler_params=params(12),
            )(pinned(flags, pltpu.SMEM), pinned(own), pinned(c_here), pinned(flipped), pinned(high), pinned(low), *got)
            vec = out[1]
            basis += [out[0], vec]
            messages = out[2:]
    lines, planes = reduce_groups()
    part = pl.pallas_call(
        last_kernel,
        out_shape=pltpu.VMEM((len(lines[0]) * SLOTS, width), F32),
        in_specs=[smem()] + [vmem()] * 15,
        out_specs=vmem(),
        scratch_shapes=[pltpu.VMEM((n, width), F32)] * 2,
        compiler_params=params(12),
    )(pinned(flags, pltpu.SMEM), pinned(own), pinned(c_here), pinned(high), pinned(low), pinned(size), *[pinned(b) for b in basis], *got)
    part = lax.all_to_all(part, ("tr", "tc"), 0, 0, tiled=True, axis_index_groups=lines)
    part = pl.pallas_call(
        merge_kernel,
        out_shape=pltpu.VMEM((len(planes[0]) * SLOTS, width), F32),
        in_specs=[vmem()],
        out_specs=vmem(),
    )(pinned(part))
    part = lax.all_to_all(part, ("tr", "tc"), 0, 0, tiled=True, axis_index_groups=planes)
    solution, norm = pl.pallas_call(
        finish_kernel,
        out_shape=[jax.ShapeDtypeStruct((n, width), F32), jax.ShapeDtypeStruct((1, width), F32)],
        in_specs=[vmem()] * 4,
        out_specs=[vmem()] * 2,
        compiler_params=params(8),
    )(pinned(part), pinned(basis[1]), pinned(basis[3]), pinned(basis[5]))
    return (solution[None, None], norm[0])


def solution(mesh):
    placed = (
        P("tr", "tc", None, None),
        P("tr", "tc", None, None),
        P("tr", "tc", None, None),
        P("tr", "tc", None, None),
        P("tr", "tc"),
    )
    return jax.shard_map(
        body,
        mesh=mesh,
        in_specs=placed,
        out_specs=(P("tr", "tc", None, None), P()),
        check_vma=False,
    )
```

```python
import functools

import jax
import jax.numpy as jnp
from jax import lax
from jax.experimental import pallas as pl
from jax.experimental.pallas import tpu as pltpu
from jax.sharding import PartitionSpec as P

ITERS = 3
BASIS = ITERS + 1
PAIRS = tuple((i, j) for i in range(BASIS) for j in range(i, BASIS))
LEAF = 256
ROWS = 256
SLOTS = 16
F32 = jnp.float32
BF16 = jnp.bfloat16
MIB = 2**20


def vmem():
    return pl.BlockSpec(memory_space=pltpu.VMEM)


def smem():
    return pl.BlockSpec(memory_space=pltpu.SMEM)


def outside():
    return pl.BlockSpec(memory_space=pltpu.HBM)


def pinned(x, space=pltpu.VMEM):
    return pltpu.with_memory_space_constraint(x, space)


def params(mib):
    return pltpu.CompilerParams(vmem_limit_bytes=mib * MIB)


def mm(a, b):
    return lax.dot_general(a, b, (((1,), (0,)), ((), ())), preferred_element_type=F32)


def tn(a, b):
    return lax.dot_general(a, b, (((0,), (0,)), ((), ())), preferred_element_type=F32)


def split(x):
    high = x.astype(BF16)
    return high, (x - high.astype(F32)).astype(BF16)


def mm3(a, b):
    return mm(a[0], b[0]) + (mm(a[0], b[1]) + mm(a[1], b[0]))


def tn3(a, b):
    return tn(a[0], b[0]) + (tn(a[0], b[1]) + tn(a[1], b[0]))


def mm_full(a, b):
    return lax.dot_general(a, b, (((1,), (0,)), ((), ())), precision=lax.Precision.HIGHEST)


def tn_full(a, b):
    return lax.dot_general(a, b, (((0,), (0,)), ((), ())), precision=lax.Precision.HIGHEST)


def column_norm(x):
    return jnp.max(jnp.sum(jnp.abs(x), axis=0, keepdims=True), axis=1, keepdims=True)


def pivot_steps(block):
    n = block.shape[0]
    rows = lax.broadcasted_iota(jnp.int32, (n, n), 0)
    cols = lax.broadcasted_iota(jnp.int32, (n, n), 1)
    eye = jnp.where(rows == cols, 1.0, 0.0).astype(F32)
    diag = jnp.where(rows == cols, block, 0.0)
    across = lax.rsqrt(jnp.sum(diag, axis=0, keepdims=True))
    down = lax.rsqrt(jnp.sum(diag, axis=1, keepdims=True))
    scaled = block * down * across
    parts = split(scaled)
    square = mm(parts[0], parts[0])
    yield
    alpha = 1.8 * lax.rsqrt(column_norm(square))
    power = (eye - (2.0 * alpha) * scaled + (alpha * alpha) * square).astype(BF16)
    inv = alpha * (2.0 * eye - alpha * scaled)
    for _ in range(2):
        inv = inv + mm(inv.astype(BF16), power)
        power = mm(power, power).astype(BF16)
        yield
    inv = inv + mm(inv.astype(BF16), power)
    yield
    high = inv.astype(BF16)
    resid = eye - (mm(parts[0], high) + mm(parts[1], high))
    yield
    resid_high = resid.astype(BF16)
    second = mm(resid_high, resid_high)
    yield
    more = split(resid + second)
    inv = high.astype(F32) + (mm(high, more[0]) + mm(high, more[1]))
    error = column_norm(second)
    return inv * down * across, error


def interleave(steps, pending):
    while True:
        try:
            next(steps)
        except StopIteration as stop:
            return stop.value
        if pending:
            pending.pop(0)()


def combine_rows(blocks, at, work, vec, ahead):
    tail = blocks - 1

    def begin():
        ahead[tail - 1] = split(work[at[tail - 1], at[tail]])

    def combine(k):
        factor_row = work[at[k], at[tail]]
        for j in range(k + 1, tail):
            scaled = split(work[at[k], at[j]])
            factor_row = factor_row - mm3(scaled, ahead[j])
            vec[at[k], :] = vec[at[k], :] - mm3(scaled, split(vec[at[j], :]))
        ahead[k] = split(factor_row)

    return [begin] + [functools.partial(combine, k) for k in reversed(range(tail - 1))]


def eliminate(n, work, vec, extra, before, after):
    blocks = n // LEAF
    at = [pl.ds(k * LEAF, LEAF) for k in range(blocks)]
    worst = jnp.zeros((1, 1), F32)
    ahead = {}
    pending = []
    for k in range(blocks):
        before(k)
        pivot, error = interleave(pivot_steps(work[at[k], at[k]]), pending)
        for task in pending:
            task()
        after(k)
        worst = jnp.maximum(worst, error)
        parts = split(pivot)
        work[at[k], at[k]] = pivot
        old, row = {}, {}

        def scale_row(j, k=k, old=old, row=row, parts=parts):
            old[j] = split(work[at[k], at[j]])
            value = mm3(parts, old[j])
            row[j] = split(value)
            work[at[k], at[j]] = value

        def update(i, j, old=old, row=row):
            work[at[i], at[j]] = work[at[i], at[j]] - tn3(old[i], row[j])

        def push(i, k=k, row=row):
            vec[at[i], :] = vec[at[i], :] - tn3(row[i], split(vec[at[k], :]))

        def solve(k=k, parts=parts):
            vec[at[k], :] = mm3(parts, split(vec[at[k], :]))

        pending = []
        later = range(k + 1, blocks)
        for j in later:
            if j == k + 1:
                scale_row(j)
                update(j, j)
            else:
                pending.append(functools.partial(scale_row, j))
        for i in later:
            for j in range(i, blocks):
                if (i, j) != (k + 1, k + 1):
                    pending.append(functools.partial(update, i, j))
        for i in later:
            pending.append(functools.partial(push, i))
        pending.append(solve)
        pending += extra(k)
        if k == blocks - 2:
            pending += combine_rows(blocks, at, work, vec, ahead)
    for task in pending:
        task()
    final = split(vec[at[-1], :])
    for k in range(blocks - 1):
        vec[at[k], :] = vec[at[k], :] - mm3(ahead[k], final)
    return worst


def careful_inverse(block):
    n = block.shape[0]
    rows = lax.broadcasted_iota(jnp.int32, (n, n), 0)
    cols = lax.broadcasted_iota(jnp.int32, (n, n), 1)
    eye = jnp.where(rows == cols, 1.0, 0.0).astype(F32)
    diag = jnp.where(rows == cols, block, 0.0)
    across = lax.rsqrt(jnp.sum(diag, axis=0, keepdims=True))
    down = lax.rsqrt(jnp.sum(diag, axis=1, keepdims=True))
    scaled = block * down * across

    def unfinished(carry):
        return jnp.logical_and(carry[2] > 1e-3, carry[0] < 80)

    def refine(carry):
        count, x, _ = carry
        left = eye - mm_full(scaled, x)
        return count + 1, x + mm_full(x, left), jnp.max(column_norm(left))

    start = eye * (1.8 / column_norm(scaled))
    return lax.while_loop(unfinished, refine, (jnp.int32(0), start, jnp.float32(2.0)))[1] * down * across


def eliminate_careful(n, work, vec, row):
    blocks = n // LEAF

    def at(k):
        return pl.ds(pl.multiple_of(k * LEAF, LEAF), LEAF)

    def pivot(k, _):
        work[at(k), at(k)] = careful_inverse(work[at(k), at(k)])

        def scale_row(j, _):
            row[:, at(j)] = mm_full(work[at(k), at(k)], work[at(k), at(j)])
            return 0

        def update_row(i, _):
            def update(j, _):
                work[at(i), at(j)] = work[at(i), at(j)] - tn_full(work[at(k), at(i)], row[:, at(j)])
                return 0

            lax.fori_loop(i, blocks, update, 0)
            vec[at(i), :] = vec[at(i), :] - tn_full(row[:, at(i)], vec[at(k), :])
            return 0

        def keep(j, _):
            work[at(k), at(j)] = row[:, at(j)]
            return 0

        lax.fori_loop(k + 1, blocks, scale_row, 0)
        lax.fori_loop(k + 1, blocks, update_row, 0)
        lax.fori_loop(k + 1, blocks, keep, 0)
        vec[at(k), :] = mm_full(work[at(k), at(k)], vec[at(k), :])
        return 0

    def back(m, _):
        k = blocks - 2 - m

        def subtract(j, _):
            vec[at(k), :] = vec[at(k), :] - mm_full(work[at(k), at(j)], vec[at(j), :])
            return 0

        return lax.fori_loop(k + 1, blocks, subtract, 0)

    lax.fori_loop(0, blocks, pivot, 0)
    lax.fori_loop(0, blocks - 1, back, 0)


def factor_kernel(time, p_hbm, rhs_hbm, c_hbm, d_hbm, work, c_ref, ct_ref, d_ref, rhs_ref, vec, tag, row, sems):
    n = work.shape[0]
    blocks = n // LEAF
    first = pl.ds(0, LEAF)
    rest = pl.ds(LEAF, n - LEAF)
    spots = [(first, first), (first, rest)] + [(pl.ds(k * LEAF, LEAF), pl.ds(0, n)) for k in range(1, blocks)]
    panels = [pltpu.make_async_copy(p_hbm.at[spot], work.at[spot], sems.at[k]) for k, spot in enumerate(spots)]
    others = [
        pltpu.make_async_copy(src, dst, sems.at[len(spots) + i])
        for i, (src, dst) in enumerate(((rhs_hbm, rhs_ref), (c_hbm, c_ref), (d_hbm, d_ref)))
    ]
    def before(k):
        if k == 0:
            panels[0].start()
            panels[0].wait()
            for copy in panels[1:] + others:
                copy.start()
        elif k == 1:
            others[1].wait()

    def after(k):
        if k == 0:
            for copy in panels[1:]:
                copy.wait()
            others[0].wait()
            vec[...] = rhs_ref[...]

    def flip(k):
        ct_ref[:, pl.ds(k * LEAF, LEAF)] = c_ref[pl.ds(k * LEAF, LEAF), :].T

    def extra(k):
        if k == 0:
            return []
        if k == blocks - 1:
            return []
        span = blocks // 2
        return [functools.partial(flip, j) for j in range((k - 1) * span, k * span)]

    worst = eliminate(n, work, vec, extra, before, after)

    @pl.when(jnp.logical_not(jnp.max(worst) < 4e-3))
    def _():
        for copy in panels:
            copy.start()
        for copy in panels:
            copy.wait()
        vec[...] = rhs_ref[...]
        eliminate_careful(n, work, vec, row)

    others[2].wait()
    tag[...] = jnp.full(tag.shape, time[0, 0] + 1, jnp.int32)


def factor(precond, rhs, coupling, diag, time):
    n, width = rhs.shape
    square = pltpu.VMEM((n, n), BF16)
    column = pltpu.VMEM((n, width), F32)
    return pl.pallas_call(
        factor_kernel,
        out_shape=[pltpu.VMEM((n, n), F32), square, square, square, column, column, pltpu.VMEM((8, 128), jnp.int32)],
        in_specs=[smem()] + [outside()] * 4,
        out_specs=[vmem()] * 7,
        scratch_shapes=[pltpu.VMEM((LEAF, n), F32), pltpu.SemaphoreType.DMA((n // LEAF + 4,))],
        compiler_params=params(20),
    )(time, *[pinned(x, pltpu.HBM) for x in (precond, rhs, coupling, diag)])


def back_kernel(ct_ref, vec_ref, ahead, back):
    high = vec_ref[...].astype(BF16)
    ahead[...] = high
    for k in range(0, back.shape[0], ROWS):
        rows = pl.ds(k, ROWS)
        back[rows, :] = mm(ct_ref[rows, :], high).astype(BF16)


def message_kernel(last, own, t1, t2, t3, ahead, back, flags, m0, m1, m2, m3):
    here, *times = [jnp.max(t[...]) for t in (own, t1, t2, t3)]
    next_left = here < last
    prev_left = here > 1
    for d, time in enumerate(times, 1):
        is_next = time == here + 1
        is_prev = jnp.logical_and(time == here - 1, here > 1)
        flags[0, d] = is_next.astype(jnp.int32)
        flags[0, 4 + d] = is_prev.astype(jnp.int32)
        next_left = jnp.logical_and(next_left, jnp.logical_not(is_next))
        prev_left = jnp.logical_and(prev_left, jnp.logical_not(is_prev))
    flags[0, 0] = next_left.astype(jnp.int32)
    flags[0, 4] = prev_left.astype(jnp.int32)
    for k in range(0, back.shape[0], ROWS):
        rows = pl.ds(k, ROWS)
        choose_messages(flags, rows, ahead[rows, :], back[rows, :], (m0, m1, m2, m3))


def first_messages(last, tags, flipped, vec):
    n, width = vec.shape
    parts = pl.pallas_call(
        back_kernel,
        out_shape=[pltpu.VMEM((n, width), BF16)] * 2,
        in_specs=[vmem()] * 2,
        out_specs=[vmem()] * 2,
        compiler_params=params(8),
    )(pinned(flipped), pinned(vec))
    return pl.pallas_call(
        functools.partial(message_kernel, last),
        out_shape=[pltpu.SMEM((1, 8), jnp.int32)] + [jax.ShapeDtypeStruct((n, width), BF16)] * 4,
        in_specs=[vmem()] * 6,
        out_specs=[smem()] + [vmem()] * 4,
        compiler_params=params(8),
    )(*[pinned(t) for t in tags], *[pinned(p) for p in parts])


def build_kernel(work, high_ref, low_ref, size_ref):
    n = work.shape[0]
    blocks = n // LEAF
    at = [pl.ds(k * LEAF, LEAF) for k in range(blocks)]
    inv = {}
    largest = jnp.zeros((1, 1), F32)
    for k in reversed(range(blocks)):
        row = {j: split(work[at[k], at[j]]) for j in range(k + 1, blocks)}
        made = {}
        for j in range(k + 1, blocks):
            made[j] = -sum(mm3(row[m], inv[m, j]) for m in range(k + 1, blocks))
            inv[k, j] = split(made[j])
            flipped = made[j].T
            inv[j, k] = split(flipped)
        made[k] = work[at[k], at[k]] - sum([mm3(row[m], inv[m, k]) for m in range(k + 1, blocks)])
        inv[k, k] = split(made[k])
        for j in range(k, blocks):
            high_ref[at[k], at[j]], low_ref[at[k], at[j]] = inv[k, j]
            if j != k:
                high_ref[at[j], at[k]], low_ref[at[j], at[k]] = inv[j, k]
            largest = jnp.maximum(largest, jnp.max(jnp.max(jnp.abs(made[j]), axis=0, keepdims=True), axis=1, keepdims=True))
    size_ref[...] = jnp.broadcast_to(largest, size_ref.shape)


def build(work, width):
    n = work.shape[0]
    return pl.pallas_call(
        build_kernel,
        out_shape=[pltpu.VMEM((n, n), BF16), pltpu.VMEM((n, n), BF16), pltpu.VMEM((8, width), F32)],
        in_specs=[vmem()],
        out_specs=[vmem()] * 3,
        compiler_params=params(16),
    )(pinned(work))


def store_applied(out_ref, high_ref, low_ref, vec_ref):
    high, low = split(vec_ref[...])
    both = jnp.concatenate([high, low], axis=1)
    width = high.shape[1]
    for k in range(0, out_ref.shape[0], ROWS):
        rows = pl.ds(k, ROWS)
        part = mm(high_ref[rows, :], both)
        out_ref[rows, :] = part[:, :width] + (part[:, width:] + mm(low_ref[rows, :], high))


def relation(flags):
    return [flags[0, d] == 1 for d in range(4)], [flags[0, 4 + d] == 1 for d in range(4)]


def choose_messages(flags, rows, ahead, back, out_refs):
    is_next, is_prev = relation(flags)
    for d, out in enumerate(out_refs):
        out[rows, :] = jnp.where(is_next[d], ahead, jnp.where(is_prev[d], back, jnp.zeros_like(back)))


def write_messages(flags, ct_ref, vec_ref, out_refs):
    high = vec_ref[...].astype(BF16)
    for k in range(0, vec_ref.shape[0], ROWS):
        rows = pl.ds(k, ROWS)
        back = mm(ct_ref[rows, :], high).astype(BF16)
        choose_messages(flags, rows, high[k:k + ROWS, :], back, out_refs)


def own_kernel(diag_ref, vec_ref, out_ref):
    both = jnp.concatenate(split(vec_ref[...]), axis=1)
    width = vec_ref.shape[1]
    for k in range(0, out_ref.shape[0], ROWS):
        rows = pl.ds(k, ROWS)
        part = mm(diag_ref[rows, :], both)
        out_ref[rows, :] = part[:, :width] + part[:, width:]


def residual_rows(flags, own_ref, c_ref, got, out_ref):
    is_next, is_prev = relation(flags)
    zero = jnp.zeros(got[0].shape, BF16)
    before = zero
    for d, ref in enumerate(got):
        before = jnp.where(is_prev[d], ref[...], before)
    for k in range(0, out_ref.shape[0], ROWS):
        rows = pl.ds(k, ROWS)
        after = zero[:ROWS]
        for d, ref in enumerate(got):
            after = jnp.where(is_next[d], ref[rows, :], after)
        out_ref[rows, :] = own_ref[rows, :] + mm(c_ref[rows, :], before) + after.astype(F32)


def step_kernel(flags, own_ref, c_ref, ct_ref, high_ref, low_ref, g0, g1, g2, g3, res_ref, vec_ref, *out_refs):
    residual_rows(flags, own_ref, c_ref, (g0, g1, g2, g3), res_ref)
    store_applied(vec_ref, high_ref, low_ref, res_ref)
    write_messages(flags, ct_ref, vec_ref, out_refs)


def pack(rows, out_ref):
    rows = rows + [jnp.zeros_like(rows[0])] * (SLOTS - len(rows))
    packed = jnp.concatenate(rows, axis=0)
    for d in range(0, out_ref.shape[0], SLOTS):
        out_ref[pl.ds(d, SLOTS), :] = packed


def last_kernel(flags, own_ref, c_ref, high_ref, low_ref, size_ref, r0, p0, r1, p1, r2, p2, g0, g1, g2, g3, out_ref, r3, p3):
    residual_rows(flags, own_ref, c_ref, (g0, g1, g2, g3), r3)
    store_applied(p3, high_ref, low_ref, r3)
    res = (r0, r1, r2, r3)
    vec = (p0, p1, p2, p3)
    unit = size_ref[0:1, :]
    sizes = [jnp.maximum(jnp.max(jnp.abs(r[...]), axis=0, keepdims=True), 1e-30) for r in res]
    left_scale = [1.0 / v for v in sizes]
    right_scale = [1.0 / (v * unit) for v in sizes]
    rows = [jnp.zeros_like(unit)] * len(PAIRS)
    for k in range(0, r3.shape[0], LEAF):
        at = pl.ds(k, LEAF)
        left = [res[i][at, :] * left_scale[i] for i in range(BASIS)]
        right = [vec[i][at, :] * right_scale[i] for i in range(BASIS)]
        for m, (i, j) in enumerate(PAIRS):
            rows[m] = rows[m] + jnp.sum(left[i] * right[j], axis=0, keepdims=True)
    pack(rows + sizes + [unit], out_ref)


def merge(in_ref):
    senders = in_ref.shape[0] // SLOTS
    got = [in_ref[pl.ds(m, senders, stride=SLOTS), :] for m in range(len(PAIRS) + BASIS + 1)]
    size_rows, unit_row = got[len(PAIRS):-1], got[-1]
    sizes = [jnp.max(v, axis=0, keepdims=True) for v in size_rows]
    unit = jnp.max(unit_row, axis=0, keepdims=True)
    share = [v / top for v, top in zip(size_rows, sizes)]
    unit_share = unit_row / unit
    rows = []
    for m, (i, j) in enumerate(PAIRS):
        rows.append(jnp.sum(got[m] * (share[i] * share[j] * unit_share), axis=0, keepdims=True))
    return rows, sizes, unit


def merge_kernel(in_ref, out_ref):
    rows, sizes, unit = merge(in_ref)
    pack(rows + sizes + [unit], out_ref)


def recurrence(rows, sizes, unit):
    gram = {}
    for m, (i, j) in enumerate(PAIRS):
        gram[i, j] = gram[j, i] = rows[m]
    lead = sizes[1] / sizes[0]
    grow = [sizes[j + 1] / sizes[j] / lead for j in range(ITERS)]
    zero = jnp.zeros_like(unit)

    def dot(a, b):
        return sum(a[i] * b[j] * gram[i, j] for i in a for j in b)

    def axpy(a, x, y):
        out = {i: a * v for i, v in x.items()}
        for i, v in y.items():
            out[i] = out[i] + v if i in out else v
        return out

    resid_new = {0: jnp.ones_like(unit)}
    resid_old = {}
    beta_now = jnp.sqrt(dot(resid_new, resid_new))
    old_beta = zero
    phi_bar = beta_now
    cosine = -jnp.ones_like(unit)
    sine_now = eps_now = d_bar = zero
    dir_now, dir_old, total = {}, {}, {}
    for step in range(ITERS):
        lanczos = {i: v / beta_now for i, v in resid_new.items()}
        image = {i + 1: v * grow[i] for i, v in lanczos.items()}
        if step > 0:
            image = axpy(-beta_now / old_beta, resid_old, image)
        alpha_now = dot(lanczos, image)
        resid_old = resid_new
        resid_new = axpy(-alpha_now / beta_now, resid_new, image)
        old_beta = beta_now
        beta_now = jnp.sqrt(dot(resid_new, resid_new))
        old_eps = eps_now
        delta_now = cosine * d_bar + sine_now * alpha_now
        g_bar = sine_now * d_bar - cosine * alpha_now
        eps_now = sine_now * beta_now
        d_bar = -cosine * beta_now
        gamma_now = jnp.sqrt(g_bar * g_bar + beta_now * beta_now)
        cosine = g_bar / gamma_now
        sine_now = beta_now / gamma_now
        phi_now = cosine * phi_bar
        phi_bar = sine_now * phi_bar
        dir_next = axpy(-old_eps, dir_old, axpy(-delta_now, dir_now, lanczos))
        dir_next = {i: v / gamma_now for i, v in dir_next.items()}
        dir_old, dir_now = dir_now, dir_next
        total = axpy(phi_now, dir_now, total)
    coefs = [total[i] * (sizes[0] / sizes[i]) / lead for i in range(ITERS)]
    return coefs, phi_bar * sizes[0] * jnp.sqrt(unit)


def finish_kernel(in_ref, p0, p1, p2, out_ref, norm_ref):
    coefs, norm = recurrence(*merge(in_ref))
    norm_ref[...] = norm
    for k in range(0, out_ref.shape[0], LEAF):
        at = pl.ds(k, LEAF)
        out_ref[at, :] = coefs[0] * p0[at, :] + coefs[1] * p1[at, :] + coefs[2] * p2[at, :]


def neighbour_perms(count):
    even = [(i, i ^ 1) for i in range(count)]
    odd = [(i, i + 1) for i in range(1, count - 1, 2)]
    return even, odd + [(j, i) for i, j in odd]


def exchange(values):
    even_r, odd_r = neighbour_perms(lax.axis_size("tr"))
    even_c, odd_c = neighbour_perms(lax.axis_size("tc"))
    routes = (("tr", odd_r), ("tc", odd_c), ("tr", even_r), ("tc", even_c))
    return [None if v is None else lax.ppermute(v, *route) for v, route in zip(values, routes)]


def reduce_groups():
    rows, cols = lax.axis_size("tr"), lax.axis_size("tc")
    deep = rows // 2

    def rank(h, z, q, c):
        return (h * deep + z) * cols + q * 2 + c

    lines = [[rank(h, z, q, c) for z in range(deep) for c in range(2)] for h in range(2) for q in range(cols // 2)]
    planes = [[rank(h, z, q, c) for h in range(2) for q in range(cols // 2)] for z in range(deep) for c in range(2)]
    return lines, planes


def body(diag_block, coupling, precond, rhs, slot_time):
    n, width = rhs.shape[2:]
    last = lax.axis_size("tr") * lax.axis_size("tc")
    sent = [jax.ShapeDtypeStruct((n, width), BF16)] * 4

    work, c_here, flipped, diag_here, res, vec, own_tag = factor(
        precond[0, 0], rhs[0, 0], coupling[0, 0], diag_block[0, 0], slot_time
    )
    tags = [own_tag] + exchange([None] + [own_tag] * 3)[1:]
    flags, *messages = first_messages(last, tags, flipped, vec)
    basis = [res, vec]
    for step in range(ITERS):
        got = exchange(messages)
        if step == 0:
            high, low, size = build(work, width)
        own = pl.pallas_call(
            own_kernel,
            out_shape=pltpu.VMEM((n, width), F32),
            in_specs=[vmem()] * 2,
            out_specs=vmem(),
            compiler_params=params(8),
        )(pinned(diag_here), pinned(vec))
        if step < ITERS - 1:
            out = pl.pallas_call(
                step_kernel,
                out_shape=[pltpu.VMEM((n, width), F32)] * 2 + sent,
                in_specs=[smem()] + [vmem()] * 9,
                out_specs=[vmem()] * 6,
                compiler_params=params(12),
            )(pinned(flags, pltpu.SMEM), pinned(own), pinned(c_here), pinned(flipped), pinned(high), pinned(low), *got)
            vec = out[1]
            basis += [out[0], vec]
            messages = out[2:]
    lines, planes = reduce_groups()
    part = pl.pallas_call(
        last_kernel,
        out_shape=pltpu.VMEM((len(lines[0]) * SLOTS, width), F32),
        in_specs=[smem()] + [vmem()] * 15,
        out_specs=vmem(),
        scratch_shapes=[pltpu.VMEM((n, width), F32)] * 2,
        compiler_params=params(12),
    )(pinned(flags, pltpu.SMEM), pinned(own), pinned(c_here), pinned(high), pinned(low), pinned(size), *[pinned(b) for b in basis], *got)
    part = lax.all_to_all(part, ("tr", "tc"), 0, 0, tiled=True, axis_index_groups=lines)
    part = pl.pallas_call(
        merge_kernel,
        out_shape=pltpu.VMEM((len(planes[0]) * SLOTS, width), F32),
        in_specs=[vmem()],
        out_specs=vmem(),
    )(pinned(part))
    part = lax.all_to_all(part, ("tr", "tc"), 0, 0, tiled=True, axis_index_groups=planes)
    solution, norm = pl.pallas_call(
        finish_kernel,
        out_shape=[jax.ShapeDtypeStruct((n, width), F32), jax.ShapeDtypeStruct((1, width), F32)],
        in_specs=[vmem()] * 4,
        out_specs=[vmem()] * 2,
        compiler_params=params(8),
    )(pinned(part), pinned(basis[1]), pinned(basis[3]), pinned(basis[5]))
    return (solution[None, None], norm[0])


def solution(mesh):
    placed = (
        P("tr", "tc", None, None),
        P("tr", "tc", None, None),
        P("tr", "tc", None, None),
        P("tr", "tc", None, None),
        P("tr", "tc"),
    )
    return jax.shard_map(
        body,
        mesh=mesh,
        in_specs=placed,
        out_specs=(P("tr", "tc", None, None), P()),
        check_vma=False,
    )
```

```python
import functools

import jax
import jax.numpy as jnp
from jax import lax
from jax.experimental import pallas as pl
from jax.experimental.pallas import tpu as pltpu
from jax.sharding import PartitionSpec as P

ITERS = 3
BASIS = ITERS + 1
PAIRS = tuple((i, j) for i in range(BASIS) for j in range(i, BASIS))
LEAF = 256
ROWS = 256
SLOTS = 16
F32 = jnp.float32
BF16 = jnp.bfloat16
MIB = 2**20


def vmem():
    return pl.BlockSpec(memory_space=pltpu.VMEM)


def smem():
    return pl.BlockSpec(memory_space=pltpu.SMEM)


def outside():
    return pl.BlockSpec(memory_space=pltpu.HBM)


def pinned(x, space=pltpu.VMEM):
    return pltpu.with_memory_space_constraint(x, space)


def params(mib):
    return pltpu.CompilerParams(vmem_limit_bytes=mib * MIB)


def mm(a, b):
    return lax.dot_general(a, b, (((1,), (0,)), ((), ())), preferred_element_type=F32)


def tn(a, b):
    return lax.dot_general(a, b, (((0,), (0,)), ((), ())), preferred_element_type=F32)


def split(x):
    high = x.astype(BF16)
    return high, (x - high.astype(F32)).astype(BF16)


def mm3(a, b):
    return mm(a[0], b[0]) + (mm(a[0], b[1]) + mm(a[1], b[0]))


def tn3(a, b):
    return tn(a[0], b[0]) + (tn(a[0], b[1]) + tn(a[1], b[0]))


def mm_full(a, b):
    return lax.dot_general(a, b, (((1,), (0,)), ((), ())), precision=lax.Precision.HIGHEST)


def tn_full(a, b):
    return lax.dot_general(a, b, (((0,), (0,)), ((), ())), precision=lax.Precision.HIGHEST)


def column_norm(x):
    return jnp.max(jnp.sum(jnp.abs(x), axis=0, keepdims=True), axis=1, keepdims=True)


def pivot_steps(block):
    n = block.shape[0]
    rows = lax.broadcasted_iota(jnp.int32, (n, n), 0)
    cols = lax.broadcasted_iota(jnp.int32, (n, n), 1)
    eye = jnp.where(rows == cols, 1.0, 0.0).astype(F32)
    diag = jnp.where(rows == cols, block, 0.0)
    across = lax.rsqrt(jnp.sum(diag, axis=0, keepdims=True))
    down = lax.rsqrt(jnp.sum(diag, axis=1, keepdims=True))
    scaled = block * down * across
    parts = split(scaled)
    square = mm(parts[0], parts[0])
    yield
    alpha = 1.8 * lax.rsqrt(column_norm(square))
    power = (eye - (2.0 * alpha) * scaled + (alpha * alpha) * square).astype(BF16)
    inv = alpha * (2.0 * eye - alpha * scaled)
    for _ in range(2):
        inv = inv + mm(inv.astype(BF16), power)
        power = mm(power, power).astype(BF16)
        yield
    inv = inv + mm(inv.astype(BF16), power)
    yield
    high = inv.astype(BF16)
    resid = eye - (mm(parts[0], high) + mm(parts[1], high))
    yield
    resid_high = resid.astype(BF16)
    second = mm(resid_high, resid_high)
    yield
    more = split(resid + second)
    inv = high.astype(F32) + (mm(high, more[0]) + mm(high, more[1]))
    error = column_norm(second)
    return inv * down * across, error


def interleave(steps, pending):
    while True:
        try:
            next(steps)
        except StopIteration as stop:
            return stop.value
        if pending:
            pending.pop(0)()


def combine_rows(blocks, at, work, vec, ahead):
    tail = blocks - 1

    def begin():
        ahead[tail - 1] = split(work[at[tail - 1], at[tail]])

    def combine(k):
        factor_row = work[at[k], at[tail]]
        for j in range(k + 1, tail):
            scaled = split(work[at[k], at[j]])
            factor_row = factor_row - mm3(scaled, ahead[j])
            vec[at[k], :] = vec[at[k], :] - mm3(scaled, split(vec[at[j], :]))
        ahead[k] = split(factor_row)

    return [begin] + [functools.partial(combine, k) for k in reversed(range(tail - 1))]


def eliminate(n, work, vec, extra, before, after):
    blocks = n // LEAF
    at = [pl.ds(k * LEAF, LEAF) for k in range(blocks)]
    worst = jnp.zeros((1, 1), F32)
    ahead = {}
    pending = []
    for k in range(blocks):
        before(k)
        pivot, error = interleave(pivot_steps(work[at[k], at[k]]), pending)
        for task in pending:
            task()
        after(k)
        worst = jnp.maximum(worst, error)
        parts = split(pivot)
        work[at[k], at[k]] = pivot
        old, row = {}, {}

        def scale_row(j, k=k, old=old, row=row, parts=parts):
            old[j] = split(work[at[k], at[j]])
            value = mm3(parts, old[j])
            row[j] = split(value)
            work[at[k], at[j]] = value

        def update(i, j, old=old, row=row):
            work[at[i], at[j]] = work[at[i], at[j]] - tn3(old[i], row[j])

        def push(i, k=k, row=row):
            vec[at[i], :] = vec[at[i], :] - tn3(row[i], split(vec[at[k], :]))

        def solve(k=k, parts=parts):
            vec[at[k], :] = mm3(parts, split(vec[at[k], :]))

        pending = []
        later = range(k + 1, blocks)
        for j in later:
            if j == k + 1:
                scale_row(j)
                update(j, j)
            else:
                pending.append(functools.partial(scale_row, j))
        for i in later:
            for j in range(i, blocks):
                if (i, j) != (k + 1, k + 1):
                    pending.append(functools.partial(update, i, j))
        for i in later:
            pending.append(functools.partial(push, i))
        pending.append(solve)
        pending += extra(k)
        if k == blocks - 2:
            pending += combine_rows(blocks, at, work, vec, ahead)
    for task in pending:
        task()
    final = split(vec[at[-1], :])
    for k in range(blocks - 1):
        vec[at[k], :] = vec[at[k], :] - mm3(ahead[k], final)
    return worst


def careful_inverse(block):
    n = block.shape[0]
    rows = lax.broadcasted_iota(jnp.int32, (n, n), 0)
    cols = lax.broadcasted_iota(jnp.int32, (n, n), 1)
    eye = jnp.where(rows == cols, 1.0, 0.0).astype(F32)
    diag = jnp.where(rows == cols, block, 0.0)
    across = lax.rsqrt(jnp.sum(diag, axis=0, keepdims=True))
    down = lax.rsqrt(jnp.sum(diag, axis=1, keepdims=True))
    scaled = block * down * across

    def unfinished(carry):
        return jnp.logical_and(carry[2] > 1e-3, carry[0] < 80)

    def refine(carry):
        count, x, _ = carry
        left = eye - mm_full(scaled, x)
        return count + 1, x + mm_full(x, left), jnp.max(column_norm(left))

    start = eye * (1.8 / column_norm(scaled))
    return lax.while_loop(unfinished, refine, (jnp.int32(0), start, jnp.float32(2.0)))[1] * down * across


def eliminate_careful(n, work, vec, row):
    blocks = n // LEAF

    def at(k):
        return pl.ds(pl.multiple_of(k * LEAF, LEAF), LEAF)

    def pivot(k, _):
        work[at(k), at(k)] = careful_inverse(work[at(k), at(k)])

        def scale_row(j, _):
            row[:, at(j)] = mm_full(work[at(k), at(k)], work[at(k), at(j)])
            return 0

        def update_row(i, _):
            def update(j, _):
                work[at(i), at(j)] = work[at(i), at(j)] - tn_full(work[at(k), at(i)], row[:, at(j)])
                return 0

            lax.fori_loop(i, blocks, update, 0)
            vec[at(i), :] = vec[at(i), :] - tn_full(row[:, at(i)], vec[at(k), :])
            return 0

        def keep(j, _):
            work[at(k), at(j)] = row[:, at(j)]
            return 0

        lax.fori_loop(k + 1, blocks, scale_row, 0)
        lax.fori_loop(k + 1, blocks, update_row, 0)
        lax.fori_loop(k + 1, blocks, keep, 0)
        vec[at(k), :] = mm_full(work[at(k), at(k)], vec[at(k), :])
        return 0

    def back(m, _):
        k = blocks - 2 - m

        def subtract(j, _):
            vec[at(k), :] = vec[at(k), :] - mm_full(work[at(k), at(j)], vec[at(j), :])
            return 0

        return lax.fori_loop(k + 1, blocks, subtract, 0)

    lax.fori_loop(0, blocks, pivot, 0)
    lax.fori_loop(0, blocks - 1, back, 0)


def factor_kernel(time, p_hbm, rhs_hbm, c_hbm, d_hbm, work, c_ref, ct_ref, d_ref, rhs_ref, vec, tag, row, sems):
    n = work.shape[0]
    blocks = n // LEAF
    first = pl.ds(0, LEAF)
    rest = pl.ds(LEAF, n - LEAF)
    spots = [(first, first), (first, rest)] + [(pl.ds(k * LEAF, LEAF), pl.ds(0, n)) for k in range(1, blocks)]
    panels = [pltpu.make_async_copy(p_hbm.at[spot], work.at[spot], sems.at[k]) for k, spot in enumerate(spots)]
    others = [
        pltpu.make_async_copy(src, dst, sems.at[len(spots) + i])
        for i, (src, dst) in enumerate(((rhs_hbm, rhs_ref), (c_hbm, c_ref), (d_hbm, d_ref)))
    ]
    def before(k):
        if k == 0:
            panels[0].start()
            panels[0].wait()
            for copy in panels[1:] + others:
                copy.start()
        elif k == 1:
            others[1].wait()

    def after(k):
        if k == 0:
            for copy in panels[1:]:
                copy.wait()
            others[0].wait()
            vec[...] = rhs_ref[...]

    def flip(k):
        ct_ref[:, pl.ds(k * LEAF, LEAF)] = c_ref[pl.ds(k * LEAF, LEAF), :].T

    def extra(k):
        if k == 0:
            return []
        if k == blocks - 1:
            return []
        span = blocks // 2
        return [functools.partial(flip, j) for j in range((k - 1) * span, k * span)]

    worst = eliminate(n, work, vec, extra, before, after)

    @pl.when(jnp.logical_not(jnp.max(worst) < 4e-3))
    def _():
        for copy in panels:
            copy.start()
        for copy in panels:
            copy.wait()
        vec[...] = rhs_ref[...]
        eliminate_careful(n, work, vec, row)

    others[2].wait()
    tag[...] = jnp.full(tag.shape, time[0, 0] + 1, jnp.int32)


def factor(precond, rhs, coupling, diag, time):
    n, width = rhs.shape
    square = pltpu.VMEM((n, n), BF16)
    column = pltpu.VMEM((n, width), F32)
    return pl.pallas_call(
        factor_kernel,
        out_shape=[pltpu.VMEM((n, n), F32), square, square, square, column, column, pltpu.VMEM((8, 128), jnp.int32)],
        in_specs=[smem()] + [outside()] * 4,
        out_specs=[vmem()] * 7,
        scratch_shapes=[pltpu.VMEM((LEAF, n), F32), pltpu.SemaphoreType.DMA((n // LEAF + 4,))],
        compiler_params=params(20),
    )(time, *[pinned(x, pltpu.HBM) for x in (precond, rhs, coupling, diag)])


def back_kernel(ct_ref, vec_ref, ahead, back):
    high = vec_ref[...].astype(BF16)
    ahead[...] = high
    for k in range(0, back.shape[0], ROWS):
        rows = pl.ds(k, ROWS)
        back[rows, :] = mm(ct_ref[rows, :], high).astype(BF16)


def message_kernel(last, t3, t2, t1, own, ahead, back, flags, m0, m1, m2, m3):
    here, *times = [jnp.max(t[...]) for t in (own, t1, t2, t3)]
    next_left = here < last
    prev_left = here > 1
    for d, time in enumerate(times, 1):
        is_next = time == here + 1
        is_prev = jnp.logical_and(time == here - 1, here > 1)
        flags[0, d] = is_next.astype(jnp.int32)
        flags[0, 4 + d] = is_prev.astype(jnp.int32)
        next_left = jnp.logical_and(next_left, jnp.logical_not(is_next))
        prev_left = jnp.logical_and(prev_left, jnp.logical_not(is_prev))
    flags[0, 0] = next_left.astype(jnp.int32)
    flags[0, 4] = prev_left.astype(jnp.int32)
    for k in range(0, back.shape[0], ROWS):
        rows = pl.ds(k, ROWS)
        choose_messages(flags, rows, ahead[rows, :], back[rows, :], (m0, m1, m2, m3))


def first_messages(last, tags, flipped, vec):
    n, width = vec.shape
    parts = pl.pallas_call(
        back_kernel,
        out_shape=[pltpu.VMEM((n, width), BF16)] * 2,
        in_specs=[vmem()] * 2,
        out_specs=[vmem()] * 2,
        compiler_params=params(8),
    )(pinned(flipped), pinned(vec))
    return pl.pallas_call(
        functools.partial(message_kernel, last),
        out_shape=[pltpu.SMEM((1, 8), jnp.int32)] + [jax.ShapeDtypeStruct((n, width), BF16)] * 4,
        in_specs=[vmem()] * 6,
        out_specs=[smem()] + [vmem()] * 4,
        compiler_params=params(8),
    )(*[pinned(t) for t in reversed(tags)], *[pinned(p) for p in parts])


def build_kernel(work, high_ref, low_ref, size_ref):
    n = work.shape[0]
    blocks = n // LEAF
    at = [pl.ds(k * LEAF, LEAF) for k in range(blocks)]
    inv = {}
    largest = jnp.zeros((1, 1), F32)
    for k in reversed(range(blocks)):
        row = {j: split(work[at[k], at[j]]) for j in range(k + 1, blocks)}
        made = {}
        for j in range(k + 1, blocks):
            made[j] = -sum(mm3(row[m], inv[m, j]) for m in range(k + 1, blocks))
            inv[k, j] = split(made[j])
            flipped = made[j].T
            inv[j, k] = split(flipped)
        made[k] = work[at[k], at[k]] - sum([mm3(row[m], inv[m, k]) for m in range(k + 1, blocks)])
        inv[k, k] = split(made[k])
        for j in range(k, blocks):
            high_ref[at[k], at[j]], low_ref[at[k], at[j]] = inv[k, j]
            if j != k:
                high_ref[at[j], at[k]], low_ref[at[j], at[k]] = inv[j, k]
            largest = jnp.maximum(largest, jnp.max(jnp.max(jnp.abs(made[j]), axis=0, keepdims=True), axis=1, keepdims=True))
    size_ref[...] = jnp.broadcast_to(largest, size_ref.shape)


def build(work, width):
    n = work.shape[0]
    return pl.pallas_call(
        build_kernel,
        out_shape=[pltpu.VMEM((n, n), BF16), pltpu.VMEM((n, n), BF16), pltpu.VMEM((8, width), F32)],
        in_specs=[vmem()],
        out_specs=[vmem()] * 3,
        compiler_params=params(16),
    )(pinned(work))


def store_applied(out_ref, high_ref, low_ref, vec_ref):
    high, low = split(vec_ref[...])
    both = jnp.concatenate([high, low], axis=1)
    width = high.shape[1]
    for k in range(0, out_ref.shape[0], ROWS):
        rows = pl.ds(k, ROWS)
        part = mm(high_ref[rows, :], both)
        out_ref[rows, :] = part[:, :width] + (part[:, width:] + mm(low_ref[rows, :], high))


def relation(flags):
    return [flags[0, d] == 1 for d in range(4)], [flags[0, 4 + d] == 1 for d in range(4)]


def choose_messages(flags, rows, ahead, back, out_refs):
    is_next, is_prev = relation(flags)
    for d, out in enumerate(out_refs):
        out[rows, :] = jnp.where(is_next[d], ahead, jnp.where(is_prev[d], back, jnp.zeros_like(back)))


def write_messages(flags, ct_ref, vec_ref, out_refs):
    high = vec_ref[...].astype(BF16)
    for k in range(0, vec_ref.shape[0], ROWS):
        rows = pl.ds(k, ROWS)
        back = mm(ct_ref[rows, :], high).astype(BF16)
        choose_messages(flags, rows, high[k:k + ROWS, :], back, out_refs)


def own_kernel(diag_ref, vec_ref, out_ref):
    both = jnp.concatenate(split(vec_ref[...]), axis=1)
    width = vec_ref.shape[1]
    for k in range(0, out_ref.shape[0], ROWS):
        rows = pl.ds(k, ROWS)
        part = mm(diag_ref[rows, :], both)
        out_ref[rows, :] = part[:, :width] + part[:, width:]


def residual_rows(flags, own_ref, c_ref, got, out_ref):
    is_next, is_prev = relation(flags)
    zero = jnp.zeros(got[0].shape, BF16)
    before = zero
    for d, ref in enumerate(got):
        before = jnp.where(is_prev[d], ref[...], before)
    for k in range(0, out_ref.shape[0], ROWS):
        rows = pl.ds(k, ROWS)
        after = zero[:ROWS]
        for d, ref in enumerate(got):
            after = jnp.where(is_next[d], ref[rows, :], after)
        out_ref[rows, :] = own_ref[rows, :] + mm(c_ref[rows, :], before) + after.astype(F32)


def step_kernel(flags, own_ref, c_ref, ct_ref, high_ref, low_ref, g0, g1, g2, g3, res_ref, vec_ref, *out_refs):
    residual_rows(flags, own_ref, c_ref, (g0, g1, g2, g3), res_ref)
    store_applied(vec_ref, high_ref, low_ref, res_ref)
    write_messages(flags, ct_ref, vec_ref, out_refs)


def pack(rows, out_ref):
    rows = rows + [jnp.zeros_like(rows[0])] * (SLOTS - len(rows))
    packed = jnp.concatenate(rows, axis=0)
    for d in range(0, out_ref.shape[0], SLOTS):
        out_ref[pl.ds(d, SLOTS), :] = packed


def magnitude(ref):
    return jnp.maximum(jnp.max(jnp.abs(ref[...]), axis=0, keepdims=True), 1e-30)


def add_gram(rows, pairs, res, vec, sizes, unit):
    used_left = sorted({i for i, _ in pairs})
    used_right = sorted({j for _, j in pairs})
    left_scale = {i: 1.0 / sizes[i] for i in used_left}
    right_scale = {j: 1.0 / (sizes[j] * unit) for j in used_right}
    for pair in pairs:
        rows[pair] = jnp.zeros_like(unit)
    for k in range(0, res[0].shape[0], ROWS):
        at = pl.ds(k, ROWS)
        left = {i: res[i][at, :] * left_scale[i] for i in used_left}
        right = {j: vec[j][at, :] * right_scale[j] for j in used_right}
        for i, j in pairs:
            rows[i, j] = rows[i, j] + jnp.sum(left[i] * right[j], axis=0, keepdims=True)


def early_kernel(diag_ref, size_ref, r0, p0, r1, p1, r2, p2, out_ref, rows_ref):
    own_kernel(diag_ref, p2, out_ref)
    res, vec = (r0, r1, r2), (p0, p1, p2)
    sizes = [magnitude(r) for r in res]
    rows = {}
    add_gram(rows, [pair for pair in PAIRS if pair[1] < ITERS], res, vec, sizes, size_ref[0:1, :])
    listed = [rows[pair] for pair in PAIRS if pair[1] < ITERS] + sizes
    listed = listed + [jnp.zeros_like(sizes[0])] * (SLOTS - len(listed))
    rows_ref[...] = jnp.concatenate(listed, axis=0)


def last_kernel(flags, own_ref, c_ref, high_ref, low_ref, size_ref, rows_ref, r0, r1, r2, g0, g1, g2, g3, out_ref, r3, p3):
    residual_rows(flags, own_ref, c_ref, (g0, g1, g2, g3), r3)
    store_applied(p3, high_ref, low_ref, r3)
    unit = size_ref[0:1, :]
    early = [pair for pair in PAIRS if pair[1] < ITERS]
    rows = {pair: rows_ref[m:m + 1, :] for m, pair in enumerate(early)}
    sizes = [rows_ref[len(early) + i:len(early) + i + 1, :] for i in range(ITERS)] + [magnitude(r3)]
    late = [pair for pair in PAIRS if pair[1] == ITERS]
    add_gram(rows, late, (r0, r1, r2, r3), {ITERS: p3}, sizes, unit)
    pack([rows[pair] for pair in PAIRS] + sizes + [unit], out_ref)


def merge(in_ref):
    senders = in_ref.shape[0] // SLOTS
    got = [in_ref[pl.ds(m, senders, stride=SLOTS), :] for m in range(len(PAIRS) + BASIS + 1)]
    size_rows, unit_row = got[len(PAIRS):-1], got[-1]
    sizes = [jnp.max(v, axis=0, keepdims=True) for v in size_rows]
    unit = jnp.max(unit_row, axis=0, keepdims=True)
    share = [v / top for v, top in zip(size_rows, sizes)]
    unit_share = unit_row / unit
    rows = []
    for m, (i, j) in enumerate(PAIRS):
        rows.append(jnp.sum(got[m] * (share[i] * share[j] * unit_share), axis=0, keepdims=True))
    return rows, sizes, unit


def merge_kernel(in_ref, out_ref):
    rows, sizes, unit = merge(in_ref)
    pack(rows + sizes + [unit], out_ref)


def recurrence(rows, sizes, unit):
    gram = {}
    for m, (i, j) in enumerate(PAIRS):
        gram[i, j] = gram[j, i] = rows[m]
    lead = sizes[1] / sizes[0]
    grow = [sizes[j + 1] / sizes[j] / lead for j in range(ITERS)]
    zero = jnp.zeros_like(unit)

    def dot(a, b):
        return sum(a[i] * b[j] * gram[i, j] for i in a for j in b)

    def axpy(a, x, y):
        out = {i: a * v for i, v in x.items()}
        for i, v in y.items():
            out[i] = out[i] + v if i in out else v
        return out

    resid_new = {0: jnp.ones_like(unit)}
    resid_old = {}
    beta_now = jnp.sqrt(dot(resid_new, resid_new))
    old_beta = zero
    phi_bar = beta_now
    cosine = -jnp.ones_like(unit)
    sine_now = eps_now = d_bar = zero
    dir_now, dir_old, total = {}, {}, {}
    for step in range(ITERS):
        lanczos = {i: v / beta_now for i, v in resid_new.items()}
        image = {i + 1: v * grow[i] for i, v in lanczos.items()}
        if step > 0:
            image = axpy(-beta_now / old_beta, resid_old, image)
        alpha_now = dot(lanczos, image)
        resid_old = resid_new
        resid_new = axpy(-alpha_now / beta_now, resid_new, image)
        old_beta = beta_now
        beta_now = jnp.sqrt(dot(resid_new, resid_new))
        old_eps = eps_now
        delta_now = cosine * d_bar + sine_now * alpha_now
        g_bar = sine_now * d_bar - cosine * alpha_now
        eps_now = sine_now * beta_now
        d_bar = -cosine * beta_now
        gamma_now = jnp.sqrt(g_bar * g_bar + beta_now * beta_now)
        cosine = g_bar / gamma_now
        sine_now = beta_now / gamma_now
        phi_now = cosine * phi_bar
        phi_bar = sine_now * phi_bar
        dir_next = axpy(-old_eps, dir_old, axpy(-delta_now, dir_now, lanczos))
        dir_next = {i: v / gamma_now for i, v in dir_next.items()}
        dir_old, dir_now = dir_now, dir_next
        total = axpy(phi_now, dir_now, total)
    coefs = [total[i] * (sizes[0] / sizes[i]) / lead for i in range(ITERS)]
    return coefs, phi_bar * sizes[0] * jnp.sqrt(unit)


def finish_kernel(in_ref, p0, p1, p2, out_ref, norm_ref):
    coefs, norm = recurrence(*merge(in_ref))
    norm_ref[...] = norm
    for k in range(0, out_ref.shape[0], LEAF):
        at = pl.ds(k, LEAF)
        out_ref[at, :] = coefs[0] * p0[at, :] + coefs[1] * p1[at, :] + coefs[2] * p2[at, :]


def neighbour_perms(count):
    even = [(i, i ^ 1) for i in range(count)]
    odd = [(i, i + 1) for i in range(1, count - 1, 2)]
    return even, odd + [(j, i) for i, j in odd]


def exchange(values):
    even_r, odd_r = neighbour_perms(lax.axis_size("tr"))
    even_c, odd_c = neighbour_perms(lax.axis_size("tc"))
    routes = (("tr", odd_r), ("tc", odd_c), ("tr", even_r), ("tc", even_c))
    return [lax.ppermute(v, *route) for v, route in zip(values, routes)]


def exchange_tags(tag):
    even_r, _ = neighbour_perms(lax.axis_size("tr"))
    even_c, odd_c = neighbour_perms(lax.axis_size("tc"))
    near = lax.ppermute(tag, "tc", even_c)
    below = lax.ppermute(tag, "tr", even_r)
    return [lax.ppermute(tag, "tc", odd_c), below, near]


def reduce_groups():
    rows, cols = lax.axis_size("tr"), lax.axis_size("tc")
    deep = rows // 2

    def rank(h, z, q, c):
        return (h * deep + z) * cols + q * 2 + c

    lines = [[rank(h, z, q, c) for z in range(deep) for c in range(2)] for h in range(2) for q in range(cols // 2)]
    planes = [[rank(h, z, q, c) for h in range(2) for q in range(cols // 2)] for z in range(deep) for c in range(2)]
    return lines, planes


def body(diag_block, coupling, precond, rhs, slot_time):
    n, width = rhs.shape[2:]
    last = lax.axis_size("tr") * lax.axis_size("tc")
    sent = [jax.ShapeDtypeStruct((n, width), BF16)] * 4

    work, c_here, flipped, diag_here, res, vec, own_tag = factor(
        precond[0, 0], rhs[0, 0], coupling[0, 0], diag_block[0, 0], slot_time
    )
    tags = [own_tag] + exchange_tags(own_tag)
    flags, *messages = first_messages(last, tags, flipped, vec)
    basis = [res, vec]
    for step in range(ITERS):
        got = exchange(messages)
        if step == 0:
            high, low, size = build(work, width)
        if step < ITERS - 1:
            own = pl.pallas_call(
                own_kernel,
                out_shape=pltpu.VMEM((n, width), F32),
                in_specs=[vmem()] * 2,
                out_specs=vmem(),
                compiler_params=params(8),
            )(pinned(diag_here), pinned(vec))
        else:
            own, early = pl.pallas_call(
                early_kernel,
                out_shape=[pltpu.VMEM((n, width), F32), pltpu.VMEM((SLOTS, width), F32)],
                in_specs=[vmem()] * 8,
                out_specs=[vmem()] * 2,
                compiler_params=params(8),
            )(pinned(diag_here), pinned(size), *[pinned(b) for b in basis])
        if step < ITERS - 1:
            out = pl.pallas_call(
                step_kernel,
                out_shape=[pltpu.VMEM((n, width), F32)] * 2 + sent,
                in_specs=[smem()] + [vmem()] * 9,
                out_specs=[vmem()] * 6,
                compiler_params=params(12),
            )(pinned(flags, pltpu.SMEM), pinned(own), pinned(c_here), pinned(flipped), pinned(high), pinned(low), *got)
            vec = out[1]
            basis += [out[0], vec]
            messages = out[2:]
    lines, planes = reduce_groups()
    part = pl.pallas_call(
        last_kernel,
        out_shape=pltpu.VMEM((len(lines[0]) * SLOTS, width), F32),
        in_specs=[smem()] + [vmem()] * 13,
        out_specs=vmem(),
        scratch_shapes=[pltpu.VMEM((n, width), F32)] * 2,
        compiler_params=params(12),
    )(pinned(flags, pltpu.SMEM), pinned(own), pinned(c_here), pinned(high), pinned(low), pinned(size), pinned(early), *[pinned(b) for b in basis[::2]], *got)
    part = lax.all_to_all(part, ("tr", "tc"), 0, 0, tiled=True, axis_index_groups=lines)
    part = pl.pallas_call(
        merge_kernel,
        out_shape=pltpu.VMEM((len(planes[0]) * SLOTS, width), F32),
        in_specs=[vmem()],
        out_specs=vmem(),
    )(pinned(part))
    part = lax.all_to_all(part, ("tr", "tc"), 0, 0, tiled=True, axis_index_groups=planes)
    solution, norm = pl.pallas_call(
        finish_kernel,
        out_shape=[jax.ShapeDtypeStruct((n, width), F32), jax.ShapeDtypeStruct((1, width), F32)],
        in_specs=[vmem()] * 4,
        out_specs=[vmem()] * 2,
        compiler_params=params(8),
    )(pinned(part), pinned(basis[1]), pinned(basis[3]), pinned(basis[5]))
    return (solution[None, None], norm[0])


def solution(mesh):
    placed = (
        P("tr", "tc", None, None),
        P("tr", "tc", None, None),
        P("tr", "tc", None, None),
        P("tr", "tc", None, None),
        P("tr", "tc"),
    )
    return jax.shard_map(
        body,
        mesh=mesh,
        in_specs=placed,
        out_specs=(P("tr", "tc", None, None), P()),
        check_vma=False,
    )
```

```python
import functools

import jax
import jax.numpy as jnp
from jax import lax
from jax.experimental import pallas as pl
from jax.experimental.pallas import tpu as pltpu
from jax.sharding import PartitionSpec as P

ITERS = 3
BASIS = ITERS + 1
PAIRS = tuple((i, j) for i in range(BASIS) for j in range(i, BASIS))
LEAF = 256
ROWS = 256
SLOTS = 16
F32 = jnp.float32
BF16 = jnp.bfloat16
MIB = 2**20


def vmem():
    return pl.BlockSpec(memory_space=pltpu.VMEM)


def smem():
    return pl.BlockSpec(memory_space=pltpu.SMEM)


def outside():
    return pl.BlockSpec(memory_space=pltpu.HBM)


def pinned(x, space=pltpu.VMEM):
    return pltpu.with_memory_space_constraint(x, space)


def params(mib):
    return pltpu.CompilerParams(vmem_limit_bytes=mib * MIB)


def mm(a, b):
    return lax.dot_general(a, b, (((1,), (0,)), ((), ())), preferred_element_type=F32)


def tn(a, b):
    return lax.dot_general(a, b, (((0,), (0,)), ((), ())), preferred_element_type=F32)


def split(x):
    high = x.astype(BF16)
    return high, (x - high.astype(F32)).astype(BF16)


def mm3(a, b):
    return mm(a[0], b[0]) + (mm(a[0], b[1]) + mm(a[1], b[0]))


def tn3(a, b):
    return tn(a[0], b[0]) + (tn(a[0], b[1]) + tn(a[1], b[0]))


def mm_full(a, b):
    return lax.dot_general(a, b, (((1,), (0,)), ((), ())), precision=lax.Precision.HIGHEST)


def tn_full(a, b):
    return lax.dot_general(a, b, (((0,), (0,)), ((), ())), precision=lax.Precision.HIGHEST)


def column_norm(x):
    return jnp.max(jnp.sum(jnp.abs(x), axis=0, keepdims=True), axis=1, keepdims=True)


def pivot_steps(block):
    n = block.shape[0]
    rows = lax.broadcasted_iota(jnp.int32, (n, n), 0)
    cols = lax.broadcasted_iota(jnp.int32, (n, n), 1)
    eye = jnp.where(rows == cols, 1.0, 0.0).astype(F32)
    diag = jnp.where(rows == cols, block, 0.0)
    across = lax.rsqrt(jnp.sum(diag, axis=0, keepdims=True))
    down = lax.rsqrt(jnp.sum(diag, axis=1, keepdims=True))
    scaled = block * down * across
    parts = split(scaled)
    square = mm(parts[0], parts[0])
    yield
    alpha = 1.8 * lax.rsqrt(column_norm(square))
    power = (eye - (2.0 * alpha) * scaled + (alpha * alpha) * square).astype(BF16)
    inv = alpha * (2.0 * eye - alpha * scaled)
    for _ in range(2):
        inv = inv + mm(inv.astype(BF16), power)
        power = mm(power, power).astype(BF16)
        yield
    inv = inv + mm(inv.astype(BF16), power)
    yield
    high = inv.astype(BF16)
    resid = eye - (mm(parts[0], high) + mm(parts[1], high))
    yield
    resid_high = resid.astype(BF16)
    second = mm(resid_high, resid_high)
    yield
    more = split(resid + second)
    inv = high.astype(F32) + (mm(high, more[0]) + mm(high, more[1]))
    error = column_norm(second)
    return inv * down * across, error


def interleave(steps, pending):
    while True:
        try:
            next(steps)
        except StopIteration as stop:
            return stop.value
        if pending:
            pending.pop(0)()


def combine_rows(blocks, at, work, vec, ahead):
    tail = blocks - 1

    def begin():
        ahead[tail - 1] = split(work[at[tail - 1], at[tail]])

    def combine(k):
        factor_row = work[at[k], at[tail]]
        for j in range(k + 1, tail):
            scaled = split(work[at[k], at[j]])
            factor_row = factor_row - mm3(scaled, ahead[j])
            vec[at[k], :] = vec[at[k], :] - mm3(scaled, split(vec[at[j], :]))
        ahead[k] = split(factor_row)

    return [begin] + [functools.partial(combine, k) for k in reversed(range(tail - 1))]


def eliminate(n, work, vec, extra, before, after):
    blocks = n // LEAF
    at = [pl.ds(k * LEAF, LEAF) for k in range(blocks)]
    worst = jnp.zeros((1, 1), F32)
    ahead = {}
    pending = []
    for k in range(blocks):
        before(k)
        pivot, error = interleave(pivot_steps(work[at[k], at[k]]), pending)
        for task in pending:
            task()
        after(k)
        worst = jnp.maximum(worst, error)
        parts = split(pivot)
        work[at[k], at[k]] = pivot
        old, row = {}, {}

        def scale_row(j, k=k, old=old, row=row, parts=parts):
            old[j] = split(work[at[k], at[j]])
            value = mm3(parts, old[j])
            row[j] = split(value)
            work[at[k], at[j]] = value

        def update(i, j, old=old, row=row):
            work[at[i], at[j]] = work[at[i], at[j]] - tn3(old[i], row[j])

        def push(i, k=k, row=row):
            vec[at[i], :] = vec[at[i], :] - tn3(row[i], split(vec[at[k], :]))

        def solve(k=k, parts=parts):
            vec[at[k], :] = mm3(parts, split(vec[at[k], :]))

        pending = []
        later = range(k + 1, blocks)
        for j in later:
            if j == k + 1:
                scale_row(j)
                update(j, j)
            else:
                pending.append(functools.partial(scale_row, j))
        for i in later:
            for j in range(i, blocks):
                if (i, j) != (k + 1, k + 1):
                    pending.append(functools.partial(update, i, j))
        for i in later:
            pending.append(functools.partial(push, i))
        pending.append(solve)
        pending += extra(k)
        if k == blocks - 2:
            pending += combine_rows(blocks, at, work, vec, ahead)
    for task in pending:
        task()
    final = split(vec[at[-1], :])
    for k in range(blocks - 1):
        vec[at[k], :] = vec[at[k], :] - mm3(ahead[k], final)
    return worst


def careful_inverse(block):
    n = block.shape[0]
    rows = lax.broadcasted_iota(jnp.int32, (n, n), 0)
    cols = lax.broadcasted_iota(jnp.int32, (n, n), 1)
    eye = jnp.where(rows == cols, 1.0, 0.0).astype(F32)
    diag = jnp.where(rows == cols, block, 0.0)
    across = lax.rsqrt(jnp.sum(diag, axis=0, keepdims=True))
    down = lax.rsqrt(jnp.sum(diag, axis=1, keepdims=True))
    scaled = block * down * across

    def unfinished(carry):
        return jnp.logical_and(carry[2] > 1e-3, carry[0] < 80)

    def refine(carry):
        count, x, _ = carry
        left = eye - mm_full(scaled, x)
        return count + 1, x + mm_full(x, left), jnp.max(column_norm(left))

    start = eye * (1.8 / column_norm(scaled))
    return lax.while_loop(unfinished, refine, (jnp.int32(0), start, jnp.float32(2.0)))[1] * down * across


def eliminate_careful(n, work, vec, row):
    blocks = n // LEAF

    def at(k):
        return pl.ds(pl.multiple_of(k * LEAF, LEAF), LEAF)

    def pivot(k, _):
        work[at(k), at(k)] = careful_inverse(work[at(k), at(k)])

        def scale_row(j, _):
            row[:, at(j)] = mm_full(work[at(k), at(k)], work[at(k), at(j)])
            return 0

        def update_row(i, _):
            def update(j, _):
                work[at(i), at(j)] = work[at(i), at(j)] - tn_full(work[at(k), at(i)], row[:, at(j)])
                return 0

            lax.fori_loop(i, blocks, update, 0)
            vec[at(i), :] = vec[at(i), :] - tn_full(row[:, at(i)], vec[at(k), :])
            return 0

        def keep(j, _):
            work[at(k), at(j)] = row[:, at(j)]
            return 0

        lax.fori_loop(k + 1, blocks, scale_row, 0)
        lax.fori_loop(k + 1, blocks, update_row, 0)
        lax.fori_loop(k + 1, blocks, keep, 0)
        vec[at(k), :] = mm_full(work[at(k), at(k)], vec[at(k), :])
        return 0

    def back(m, _):
        k = blocks - 2 - m

        def subtract(j, _):
            vec[at(k), :] = vec[at(k), :] - mm_full(work[at(k), at(j)], vec[at(j), :])
            return 0

        return lax.fori_loop(k + 1, blocks, subtract, 0)

    lax.fori_loop(0, blocks, pivot, 0)
    lax.fori_loop(0, blocks - 1, back, 0)


def factor_kernel(time, p_hbm, rhs_hbm, c_hbm, d_hbm, work, c_ref, ct_ref, d_ref, rhs_ref, vec, tag, row, sems):
    n = work.shape[0]
    blocks = n // LEAF
    first = pl.ds(0, LEAF)
    rest = pl.ds(LEAF, n - LEAF)
    spots = [(first, first), (first, rest)] + [(pl.ds(k * LEAF, LEAF), pl.ds(0, n)) for k in range(1, blocks)]
    panels = [pltpu.make_async_copy(p_hbm.at[spot], work.at[spot], sems.at[k]) for k, spot in enumerate(spots)]
    others = [
        pltpu.make_async_copy(src, dst, sems.at[len(spots) + i])
        for i, (src, dst) in enumerate(((rhs_hbm, rhs_ref), (c_hbm, c_ref), (d_hbm, d_ref)))
    ]
    def before(k):
        if k == 0:
            panels[0].start()
            panels[0].wait()
            for copy in panels[1:] + others:
                copy.start()
        elif k == 1:
            others[1].wait()

    def after(k):
        if k == 0:
            for copy in panels[1:]:
                copy.wait()
            others[0].wait()
            vec[...] = rhs_ref[...]

    def flip(k):
        ct_ref[:, pl.ds(k * LEAF, LEAF)] = c_ref[pl.ds(k * LEAF, LEAF), :].T

    def extra(k):
        if k == 0:
            return []
        if k == blocks - 1:
            return []
        span = blocks // 2
        return [functools.partial(flip, j) for j in range((k - 1) * span, k * span)]

    worst = eliminate(n, work, vec, extra, before, after)

    @pl.when(jnp.logical_not(jnp.max(worst) < 4e-3))
    def _():
        for copy in panels:
            copy.start()
        for copy in panels:
            copy.wait()
        vec[...] = rhs_ref[...]
        eliminate_careful(n, work, vec, row)

    others[2].wait()
    tag[...] = jnp.full(tag.shape, time[0, 0] + 1, jnp.int32)


def factor(precond, rhs, coupling, diag, time):
    n, width = rhs.shape
    square = pltpu.VMEM((n, n), BF16)
    column = pltpu.VMEM((n, width), F32)
    return pl.pallas_call(
        factor_kernel,
        out_shape=[pltpu.VMEM((n, n), F32), square, square, square, column, column, pltpu.VMEM((8, 128), jnp.int32)],
        in_specs=[smem()] + [outside()] * 4,
        out_specs=[vmem()] * 7,
        scratch_shapes=[pltpu.VMEM((LEAF, n), F32), pltpu.SemaphoreType.DMA((n // LEAF + 4,))],
        compiler_params=params(20),
    )(time, *[pinned(x, pltpu.HBM) for x in (precond, rhs, coupling, diag)])


def back_kernel(ct_ref, vec_ref, ahead, back):
    high = vec_ref[...].astype(BF16)
    ahead[...] = high
    for k in range(0, back.shape[0], ROWS):
        rows = pl.ds(k, ROWS)
        back[rows, :] = mm(ct_ref[rows, :], high).astype(BF16)


def message_kernel(last, t3, t1, t2, own, ahead, back, flags, m0, m1, m2, m3):
    here, *times = [jnp.max(t[...]) for t in (own, t1, t2, t3)]
    next_left = here < last
    prev_left = here > 1
    for d, time in enumerate(times, 1):
        is_next = time == here + 1
        is_prev = jnp.logical_and(time == here - 1, here > 1)
        flags[0, d] = is_next.astype(jnp.int32)
        flags[0, 4 + d] = is_prev.astype(jnp.int32)
        next_left = jnp.logical_and(next_left, jnp.logical_not(is_next))
        prev_left = jnp.logical_and(prev_left, jnp.logical_not(is_prev))
    flags[0, 0] = next_left.astype(jnp.int32)
    flags[0, 4] = prev_left.astype(jnp.int32)
    for k in range(0, back.shape[0], ROWS):
        rows = pl.ds(k, ROWS)
        choose_messages(flags, rows, ahead[rows, :], back[rows, :], (m0, m1, m2, m3))


def first_messages(last, tags, flipped, vec):
    n, width = vec.shape
    parts = pl.pallas_call(
        back_kernel,
        out_shape=[pltpu.VMEM((n, width), BF16)] * 2,
        in_specs=[vmem()] * 2,
        out_specs=[vmem()] * 2,
        compiler_params=params(8),
    )(pinned(flipped), pinned(vec))
    return pl.pallas_call(
        functools.partial(message_kernel, last),
        out_shape=[pltpu.SMEM((1, 8), jnp.int32)] + [jax.ShapeDtypeStruct((n, width), BF16)] * 4,
        in_specs=[vmem()] * 6,
        out_specs=[smem()] + [vmem()] * 4,
        compiler_params=params(8),
    )(*[pinned(tags[i]) for i in (3, 1, 2, 0)], *[pinned(p) for p in parts])


def build_kernel(work, high_ref, low_ref, size_ref):
    n = work.shape[0]
    blocks = n // LEAF
    at = [pl.ds(k * LEAF, LEAF) for k in range(blocks)]
    inv = {}
    largest = jnp.zeros((1, 1), F32)
    for k in reversed(range(blocks)):
        row = {j: split(work[at[k], at[j]]) for j in range(k + 1, blocks)}
        made = {}
        for j in range(k + 1, blocks):
            made[j] = -sum(mm3(row[m], inv[m, j]) for m in range(k + 1, blocks))
            inv[k, j] = split(made[j])
            flipped = made[j].T
            inv[j, k] = split(flipped)
        made[k] = work[at[k], at[k]] - sum([mm3(row[m], inv[m, k]) for m in range(k + 1, blocks)])
        inv[k, k] = split(made[k])
        for j in range(k, blocks):
            high_ref[at[k], at[j]], low_ref[at[k], at[j]] = inv[k, j]
            if j != k:
                high_ref[at[j], at[k]], low_ref[at[j], at[k]] = inv[j, k]
            largest = jnp.maximum(largest, jnp.max(jnp.max(jnp.abs(made[j]), axis=0, keepdims=True), axis=1, keepdims=True))
    size_ref[...] = jnp.broadcast_to(largest, size_ref.shape)


def build(work, width):
    n = work.shape[0]
    return pl.pallas_call(
        build_kernel,
        out_shape=[pltpu.VMEM((n, n), BF16), pltpu.VMEM((n, n), BF16), pltpu.VMEM((8, width), F32)],
        in_specs=[vmem()],
        out_specs=[vmem()] * 3,
        compiler_params=params(16),
    )(pinned(work))


def store_applied(out_ref, high_ref, low_ref, vec_ref):
    high, low = split(vec_ref[...])
    both = jnp.concatenate([high, low], axis=1)
    width = high.shape[1]
    for k in range(0, out_ref.shape[0], ROWS):
        rows = pl.ds(k, ROWS)
        part = mm(high_ref[rows, :], both)
        out_ref[rows, :] = part[:, :width] + (part[:, width:] + mm(low_ref[rows, :], high))


def relation(flags):
    return [flags[0, d] == 1 for d in range(4)], [flags[0, 4 + d] == 1 for d in range(4)]


def choose_messages(flags, rows, ahead, back, out_refs):
    is_next, is_prev = relation(flags)
    for d, out in enumerate(out_refs):
        out[rows, :] = jnp.where(is_next[d], ahead, jnp.where(is_prev[d], back, jnp.zeros_like(back)))


def write_messages(flags, ct_ref, vec_ref, out_refs):
    high = vec_ref[...].astype(BF16)
    for k in range(0, vec_ref.shape[0], ROWS):
        rows = pl.ds(k, ROWS)
        back = mm(ct_ref[rows, :], high).astype(BF16)
        choose_messages(flags, rows, high[k:k + ROWS, :], back, out_refs)


def own_kernel(diag_ref, vec_ref, out_ref):
    both = jnp.concatenate(split(vec_ref[...]), axis=1)
    width = vec_ref.shape[1]
    for k in range(0, out_ref.shape[0], ROWS):
        rows = pl.ds(k, ROWS)
        part = mm(diag_ref[rows, :], both)
        out_ref[rows, :] = part[:, :width] + part[:, width:]


def residual_rows(flags, own_ref, c_ref, got, out_ref):
    is_next, is_prev = relation(flags)
    zero = jnp.zeros(got[0].shape, BF16)
    before = zero
    for d, ref in enumerate(got):
        before = jnp.where(is_prev[d], ref[...], before)
    for k in range(0, out_ref.shape[0], ROWS):
        rows = pl.ds(k, ROWS)
        after = zero[:ROWS]
        for d, ref in enumerate(got):
            after = jnp.where(is_next[d], ref[rows, :], after)
        out_ref[rows, :] = own_ref[rows, :] + mm(c_ref[rows, :], before) + after.astype(F32)


def step_kernel(flags, own_ref, c_ref, ct_ref, high_ref, low_ref, g0, g1, g2, g3, res_ref, vec_ref, *out_refs):
    residual_rows(flags, own_ref, c_ref, (g0, g1, g2, g3), res_ref)
    store_applied(vec_ref, high_ref, low_ref, res_ref)
    write_messages(flags, ct_ref, vec_ref, out_refs)


def pack(rows, out_ref):
    rows = rows + [jnp.zeros_like(rows[0])] * (SLOTS - len(rows))
    packed = jnp.concatenate(rows, axis=0)
    for d in range(0, out_ref.shape[0], SLOTS):
        out_ref[pl.ds(d, SLOTS), :] = packed


def magnitude(ref):
    return jnp.maximum(jnp.max(jnp.abs(ref[...]), axis=0, keepdims=True), 1e-30)


def add_gram(rows, pairs, res, vec, sizes, unit):
    used_left = sorted({i for i, _ in pairs})
    used_right = sorted({j for _, j in pairs})
    left_scale = {i: 1.0 / sizes[i] for i in used_left}
    right_scale = {j: 1.0 / (sizes[j] * unit) for j in used_right}
    for pair in pairs:
        rows[pair] = jnp.zeros_like(unit)
    for k in range(0, res[0].shape[0], ROWS):
        at = pl.ds(k, ROWS)
        left = {i: res[i][at, :] * left_scale[i] for i in used_left}
        right = {j: vec[j][at, :] * right_scale[j] for j in used_right}
        for i, j in pairs:
            rows[i, j] = rows[i, j] + jnp.sum(left[i] * right[j], axis=0, keepdims=True)


def early_kernel(diag_ref, size_ref, r0, p0, r1, p1, r2, p2, out_ref, rows_ref):
    own_kernel(diag_ref, p2, out_ref)
    res, vec = (r0, r1, r2), (p0, p1, p2)
    sizes = [magnitude(r) for r in res]
    rows = {}
    add_gram(rows, [pair for pair in PAIRS if pair[1] < ITERS], res, vec, sizes, size_ref[0:1, :])
    listed = [rows[pair] for pair in PAIRS if pair[1] < ITERS] + sizes
    listed = listed + [jnp.zeros_like(sizes[0])] * (SLOTS - len(listed))
    rows_ref[...] = jnp.concatenate(listed, axis=0)


def last_kernel(flags, own_ref, c_ref, high_ref, low_ref, size_ref, rows_ref, r0, r1, r2, g0, g1, g2, g3, out_ref, r3, p3):
    residual_rows(flags, own_ref, c_ref, (g0, g1, g2, g3), r3)
    store_applied(p3, high_ref, low_ref, r3)
    unit = size_ref[0:1, :]
    early = [pair for pair in PAIRS if pair[1] < ITERS]
    rows = {pair: rows_ref[m:m + 1, :] for m, pair in enumerate(early)}
    sizes = [rows_ref[len(early) + i:len(early) + i + 1, :] for i in range(ITERS)] + [magnitude(r3)]
    late = [pair for pair in PAIRS if pair[1] == ITERS]
    add_gram(rows, late, (r0, r1, r2, r3), {ITERS: p3}, sizes, unit)
    pack([rows[pair] for pair in PAIRS] + sizes + [unit], out_ref)


def merge(in_ref):
    senders = in_ref.shape[0] // SLOTS
    got = [in_ref[pl.ds(m, senders, stride=SLOTS), :] for m in range(len(PAIRS) + BASIS + 1)]
    size_rows, unit_row = got[len(PAIRS):-1], got[-1]
    sizes = [jnp.max(v, axis=0, keepdims=True) for v in size_rows]
    unit = jnp.max(unit_row, axis=0, keepdims=True)
    share = [v / top for v, top in zip(size_rows, sizes)]
    unit_share = unit_row / unit
    rows = []
    for m, (i, j) in enumerate(PAIRS):
        rows.append(jnp.sum(got[m] * (share[i] * share[j] * unit_share), axis=0, keepdims=True))
    return rows, sizes, unit


def merge_kernel(in_ref, out_ref):
    rows, sizes, unit = merge(in_ref)
    pack(rows + sizes + [unit], out_ref)


def recurrence(rows, sizes, unit):
    gram = {}
    for m, (i, j) in enumerate(PAIRS):
        gram[i, j] = gram[j, i] = rows[m]
    lead = sizes[1] / sizes[0]
    grow = [sizes[j + 1] / sizes[j] / lead for j in range(ITERS)]
    zero = jnp.zeros_like(unit)

    def dot(a, b):
        return sum(a[i] * b[j] * gram[i, j] for i in a for j in b)

    def axpy(a, x, y):
        out = {i: a * v for i, v in x.items()}
        for i, v in y.items():
            out[i] = out[i] + v if i in out else v
        return out

    resid_new = {0: jnp.ones_like(unit)}
    resid_old = {}
    beta_now = jnp.sqrt(dot(resid_new, resid_new))
    old_beta = zero
    phi_bar = beta_now
    cosine = -jnp.ones_like(unit)
    sine_now = eps_now = d_bar = zero
    dir_now, dir_old, total = {}, {}, {}
    for step in range(ITERS):
        lanczos = {i: v / beta_now for i, v in resid_new.items()}
        image = {i + 1: v * grow[i] for i, v in lanczos.items()}
        if step > 0:
            image = axpy(-beta_now / old_beta, resid_old, image)
        alpha_now = dot(lanczos, image)
        resid_old = resid_new
        resid_new = axpy(-alpha_now / beta_now, resid_new, image)
        old_beta = beta_now
        beta_now = jnp.sqrt(dot(resid_new, resid_new))
        old_eps = eps_now
        delta_now = cosine * d_bar + sine_now * alpha_now
        g_bar = sine_now * d_bar - cosine * alpha_now
        eps_now = sine_now * beta_now
        d_bar = -cosine * beta_now
        gamma_now = jnp.sqrt(g_bar * g_bar + beta_now * beta_now)
        cosine = g_bar / gamma_now
        sine_now = beta_now / gamma_now
        phi_now = cosine * phi_bar
        phi_bar = sine_now * phi_bar
        dir_next = axpy(-old_eps, dir_old, axpy(-delta_now, dir_now, lanczos))
        dir_next = {i: v / gamma_now for i, v in dir_next.items()}
        dir_old, dir_now = dir_now, dir_next
        total = axpy(phi_now, dir_now, total)
    coefs = [total[i] * (sizes[0] / sizes[i]) / lead for i in range(ITERS)]
    return coefs, phi_bar * sizes[0] * jnp.sqrt(unit)


def finish_kernel(in_ref, p0, p1, p2, out_ref, norm_ref):
    coefs, norm = recurrence(*merge(in_ref))
    norm_ref[...] = norm
    for k in range(0, out_ref.shape[0], LEAF):
        at = pl.ds(k, LEAF)
        out_ref[at, :] = coefs[0] * p0[at, :] + coefs[1] * p1[at, :] + coefs[2] * p2[at, :]


def neighbour_perms(count):
    even = [(i, i ^ 1) for i in range(count)]
    odd = [(i, i + 1) for i in range(1, count - 1, 2)]
    return even, odd + [(j, i) for i, j in odd]


def exchange(values):
    even_r, odd_r = neighbour_perms(lax.axis_size("tr"))
    even_c, odd_c = neighbour_perms(lax.axis_size("tc"))
    routes = (("tr", odd_r), ("tr", even_r), ("tc", odd_c), ("tc", even_c))
    return [lax.ppermute(v, *route) for v, route in zip(values, routes)]


def exchange_tags(tag):
    even_r, _ = neighbour_perms(lax.axis_size("tr"))
    even_c, odd_c = neighbour_perms(lax.axis_size("tc"))
    near = lax.ppermute(tag, "tc", even_c)
    below = lax.ppermute(tag, "tr", even_r)
    return [below, lax.ppermute(tag, "tc", odd_c), near]


def body(diag_block, coupling, precond, rhs, slot_time):
    n, width = rhs.shape[2:]
    last = lax.axis_size("tr") * lax.axis_size("tc")
    sent = [jax.ShapeDtypeStruct((n, width), BF16)] * 4

    work, c_here, flipped, diag_here, res, vec, own_tag = factor(
        precond[0, 0], rhs[0, 0], coupling[0, 0], diag_block[0, 0], slot_time
    )
    tags = [own_tag] + exchange_tags(own_tag)
    flags, *messages = first_messages(last, tags, flipped, vec)
    basis = [res, vec]
    for step in range(ITERS):
        got = exchange(messages)
        if step == 0:
            high, low, size = build(work, width)
        if step < ITERS - 1:
            own = pl.pallas_call(
                own_kernel,
                out_shape=pltpu.VMEM((n, width), F32),
                in_specs=[vmem()] * 2,
                out_specs=vmem(),
                compiler_params=params(8),
            )(pinned(diag_here), pinned(vec))
        else:
            own, early = pl.pallas_call(
                early_kernel,
                out_shape=[pltpu.VMEM((n, width), F32), pltpu.VMEM((SLOTS, width), F32)],
                in_specs=[vmem()] * 8,
                out_specs=[vmem()] * 2,
                compiler_params=params(8),
            )(pinned(diag_here), pinned(size), *[pinned(b) for b in basis])
        if step < ITERS - 1:
            out = pl.pallas_call(
                step_kernel,
                out_shape=[pltpu.VMEM((n, width), F32)] * 2 + sent,
                in_specs=[smem()] + [vmem()] * 9,
                out_specs=[vmem()] * 6,
                compiler_params=params(12),
            )(pinned(flags, pltpu.SMEM), pinned(own), pinned(c_here), pinned(flipped), pinned(high), pinned(low), *got)
            vec = out[1]
            basis += [out[0], vec]
            messages = out[2:]
    part = pl.pallas_call(
        last_kernel,
        out_shape=pltpu.VMEM((lax.axis_size("tc") * SLOTS, width), F32),
        in_specs=[smem()] + [vmem()] * 13,
        out_specs=vmem(),
        scratch_shapes=[pltpu.VMEM((n, width), F32)] * 2,
        compiler_params=params(12),
    )(pinned(flags, pltpu.SMEM), pinned(own), pinned(c_here), pinned(high), pinned(low), pinned(size), pinned(early), *[pinned(b) for b in basis[::2]], *got)
    part = lax.all_to_all(part, "tc", 0, 0, tiled=True)
    part = pl.pallas_call(
        merge_kernel,
        out_shape=pltpu.VMEM((lax.axis_size("tr") * SLOTS, width), F32),
        in_specs=[vmem()],
        out_specs=vmem(),
    )(pinned(part))
    part = lax.all_to_all(part, "tr", 0, 0, tiled=True)
    solution, norm = pl.pallas_call(
        finish_kernel,
        out_shape=[jax.ShapeDtypeStruct((n, width), F32), jax.ShapeDtypeStruct((1, width), F32)],
        in_specs=[vmem()] * 4,
        out_specs=[vmem()] * 2,
        compiler_params=params(8),
    )(pinned(part), pinned(basis[1]), pinned(basis[3]), pinned(basis[5]))
    return (solution[None, None], norm[0])


def solution(mesh):
    placed = (
        P("tr", "tc", None, None),
        P("tr", "tc", None, None),
        P("tr", "tc", None, None),
        P("tr", "tc", None, None),
        P("tr", "tc"),
    )
    return jax.shard_map(
        body,
        mesh=mesh,
        in_specs=placed,
        out_specs=(P("tr", "tc", None, None), P()),
        check_vma=False,
    )
```
